256 devices in a mesh: blk: 4 (over x_hi, core), tower: 64 (over x_lo, z, y).
Axes of the slice: x: 4 (x_hi: 2, x_lo: 2; x = x_hi * 2 + x_lo), y: 4, z: 8, core: 2. Of those that a mesh axis runs over, the one named last changes fastest.
Arguments:
- clip_tokens: bfloat16 [16384, 16, 3200], P(('blk', 'tower')), may hold values from -6 to 6
- clip_video: int32 [16384], P(('blk', 'tower')), may hold values from 0 to 511, as said below
- pool_vectors: bfloat16 [25, 3200], replicated, may hold values from -0.29882812 to 0.29882812
- out_proj: bfloat16 [3200, 768], replicated, may hold values from -0.109375 to 0.109375
- text_embed: bfloat16 [2048, 768], P(('blk', 'tower')), may hold values from -0.59765625 to 0.59765625
- pair_text: int32 [2048], P(('blk', 'tower')), may hold values from 0 to 2047, each once
Outputs:
- video_embed: bfloat16 [2048, 768], P(('blk', 'tower'))
- video_grad: float32 [2048, 768], P(('blk', 'tower'))
- text_grad: float32 [2048, 768], P(('blk', 'tower'))
- loss: float32 [], replicated
The draws below stay inside these ranges and needn't reach their ends.
Inputs may be any that keep to these rules, and one draw needn't show every extreme that they name: `clip_video`: owner of video v of a row is device v // 8 of that row's 64 devices (in the order of tower); every video has 1 to 16 clips; the clips of one device name videos of any one owner at most 2 times; in every row one owner is named exactly 2 times by every device of the row, all its videos having 16 clips.
All inputs are finite; a program needn't handle non-finite values.
Results may differ from the reference program's by a relative error of at most 0.004.
Values may be sent and summed in bfloat16 or wider, within the bound.
No kernel may reach another device: no remote copies, remote signals or barrier semaphores. Data moves between devices by JAX's collectives and lax.ppermute only.
A program may use at most 128 MiB of HBM per device.

```python
import jax
import jax.numpy as jnp
from jax import lax

H = 25
HD = 128
D = 3200
E = 768
TOK_CLIP = 16
MAX_CLIPS = 16
VID_DEV = 8
CLIP_DEV = 64
ROW_CLIPS = 4096
ROW_VIDEOS = 512
VIDEOS = 2048
CLIPS = 16384
N_BLK = 4
N_TOWER = 64


def draw_clip_video(key, part):
    key = jax.random.fold_in(key, 11)

    def one_row(row_key):
        key_busy, key_cells, key_order = jax.random.split(row_key, 3)
        busy_owner = jax.random.randint(key_busy, (), 0, N_TOWER)
        others = (N_TOWER - 1) * VID_DEV
        extra = ROW_CLIPS - MAX_CLIPS * VID_DEV - others
        cells = jax.random.permutation(key_cells, others * (MAX_CLIPS - 1))
        chosen = cells[:extra] // (MAX_CLIPS - 1)
        rest_counts = 1 + jnp.zeros((others,), jnp.int32).at[chosen].add(1)
        rest_counts = rest_counts.reshape(N_TOWER - 1, VID_DEV)
        owners = jnp.arange(N_TOWER, dtype=jnp.int32)
        rest_index = jnp.clip(owners - (owners > busy_owner).astype(jnp.int32), 0, N_TOWER - 2)
        counts = jnp.where((owners == busy_owner)[:, None], MAX_CLIPS, rest_counts[rest_index])
        bounds = jnp.cumsum(counts.reshape(-1))
        clip_index = jnp.arange(ROW_CLIPS, dtype=jnp.int32)
        video_of = jnp.searchsorted(bounds, clip_index, side='right').astype(jnp.int32)
        source = clip_index % N_TOWER
        position = clip_index // N_TOWER
        orders = jax.vmap(lambda order_key: jax.random.permutation(order_key, CLIP_DEV))(jax.random.split(key_order, N_TOWER))
        new_position = orders[source, position]
        return jnp.zeros((ROW_CLIPS,), jnp.int32).at[source * CLIP_DEV + new_position].set(video_of)
    rows = jax.vmap(one_row)(jax.random.split(key, N_BLK))
    return rows.reshape(-1).astype(jnp.int32)


def block_scale(key, extent, cuts, least, top_value):
    def one(dim, blocks):
        draws = jax.random.uniform(jax.random.fold_in(jax.random.fold_in(key, 6), dim), (blocks,), jnp.float32, least / len(cuts), top_value / len(cuts))
        return jnp.repeat(jnp.exp(draws), extent[dim] // blocks).reshape((-1,) + (1,) * (len(extent) - dim - 1))

    gain = one(*cuts[0])
    for cut in cuts[1:]:
        gain = gain * one(*cut)
    return gain


def bell_draw(own_key, extent, spread, bound, cuts=(), held_as=jnp.bfloat16):
    drawn = spread * jax.random.normal(own_key, extent, jnp.float32)
    if cuts:
        drawn = drawn * block_scale(own_key, extent, cuts, -0.22, 0.18)
    return jnp.clip(drawn, -bound, bound).astype(held_as)


def setup_inputs(seed: int = 0) -> dict:
    key_list = jax.random.split(jax.random.key(seed), 7)
    clip_tokens = bell_draw(key_list[0], (CLIPS, TOK_CLIP, D), 1.0, 6.0, ((0, 256),))
    clip_video = draw_clip_video(jax.random.fold_in(key_list[6], 71), 0)
    pool_vectors = bell_draw(key_list[2], (H, D), 0.05, 0.29882812)
    out_proj = bell_draw(key_list[3], (D, E), D ** -0.5, 0.109375)
    text_embed = bell_draw(key_list[4], (VIDEOS, E), 0.1, 0.59765625, ((0, 256),))
    pair_text = jax.random.permutation(key_list[5], VIDEOS).astype(jnp.int32)
    return {"clip_tokens": clip_tokens, "clip_video": clip_video, "pool_vectors": pool_vectors, "out_proj": out_proj, "text_embed": text_embed, "pair_text": pair_text}


SOFT_CAP = 20.0
LOGIT_SCALE = 40.0
EPSILON = 1e-06

def clip_partials(clip_block, pool_vectors):
    clip_count = clip_block.shape[0]
    flat_tokens = clip_block.reshape(clip_count * TOK_CLIP, D)
    scores = jnp.dot(pool_vectors, flat_tokens.T, preferred_element_type=jnp.float32)
    weights = jnp.exp(SOFT_CAP * jnp.tanh(scores / SOFT_CAP)).astype(jnp.bfloat16)
    weights = weights.reshape(H, clip_count, TOK_CLIP).astype(jnp.float32)
    denominators = lax.optimization_barrier(jnp.sum(weights, axis=2)).T
    split_heads = clip_block.reshape(clip_count, TOK_CLIP, H, HD).astype(jnp.float32)
    numerators = jnp.einsum('hck,ckhd->chd', weights, split_heads)
    return (numerators.reshape(clip_count, D), denominators)

def unit_rows(values):
    norms = jnp.sqrt(lax.optimization_barrier(jnp.sum(values * values, axis=1)) + EPSILON)
    return (values / norms[:, None], norms)

def reference(clip_tokens, clip_video, pool_vectors, out_proj, text_embed, pair_text):
    blocks = clip_tokens.reshape(CLIPS // CLIP_DEV, CLIP_DEV, TOK_CLIP, D)
    numerators, denominators = lax.map(lambda block: clip_partials(block, pool_vectors), blocks)
    numerators = numerators.reshape(CLIPS, D)
    denominators = denominators.reshape(CLIPS, H)
    row_first = jnp.arange(CLIPS, dtype=jnp.int32) // ROW_CLIPS * ROW_VIDEOS
    video_ids = (clip_video + row_first).astype(jnp.int32)
    video_num = jax.ops.segment_sum(numerators, video_ids, VIDEOS)
    video_den = jax.ops.segment_sum(denominators, video_ids, VIDEOS)
    pooled = video_num / jnp.repeat(video_den, HD, axis=1)
    embedding = jnp.dot(pooled, out_proj.astype(jnp.float32), precision=lax.Precision.HIGHEST)
    video_hat, video_norm = unit_rows(embedding)
    text_hat, text_norm = unit_rows(text_embed.astype(jnp.float32))
    video_low = video_hat.astype(jnp.bfloat16)
    text_low = text_hat.astype(jnp.bfloat16)
    logits = LOGIT_SCALE * jnp.dot(video_low, text_low.T, preferred_element_type=jnp.float32)
    exp_all = jnp.exp(logits)
    row_sums = lax.optimization_barrier(jnp.sum(exp_all, axis=1))
    col_sums = lax.optimization_barrier(jnp.sum(exp_all, axis=0))
    onehot = (pair_text[:, None] == jnp.arange(VIDEOS, dtype=jnp.int32)[None, :]).astype(jnp.float32)
    positive = jnp.sum(logits * onehot)
    loss = (jnp.sum(jnp.log(row_sums)) + jnp.sum(jnp.log(col_sums)) - 2.0 * positive) / (2.0 * VIDEOS)
    probe = (exp_all / row_sums[:, None] + exp_all / col_sums[None, :] - 2.0 * onehot).astype(jnp.bfloat16)
    video_dir = LOGIT_SCALE * jnp.dot(probe, text_low, preferred_element_type=jnp.float32)
    text_dir = LOGIT_SCALE * jnp.dot(probe.T, video_low, preferred_element_type=jnp.float32)
    video_grad = (video_dir - lax.optimization_barrier(jnp.sum(video_dir * video_hat, axis=1, keepdims=True)) * video_hat) / video_norm[:, None]
    text_grad = (text_dir - lax.optimization_barrier(jnp.sum(text_dir * text_hat, axis=1, keepdims=True)) * text_hat) / text_norm[:, None]
    return (embedding.astype(jnp.bfloat16), video_grad, text_grad, loss)
```

```python
import jax
import jax.numpy as jnp
import numpy as np
from jax import lax
from jax.experimental import pallas as pl
from jax.experimental.pallas import tpu as pltpu
from jax.sharding import Mesh, PartitionSpec as P

H = 25
HD = 128
D = 3200
E = 768
TOK = 16
CLIPS = 64
SLOTS = 128
SOFT_CAP = 20.0
SCALE = 40.0
EPS = 1e-06
TAIL = D + 128
ETEXT = E + 128
HALF = 1024
ALL = ("xh", "c", "xl", "z", "y")
ROW = ("xl", "z", "y")
WIDE = ("xh", "xl", "y")
CHUNK = 16
TOKS = CHUNK * TOK
TILE = 256
VMEM = pl.BlockSpec(memory_space=pltpu.VMEM)
SMEM = pl.BlockSpec(memory_space=pltpu.SMEM)
f32 = jnp.float32
bf16 = jnp.bfloat16
NT = (((1,), (1,)), ((), ()))
TN = (((0,), (0,)), ((), ()))


def dot(a, b, dims=(((1,), (0,)), ((), ()))):
    return lax.dot_general(a, b, dims, preferred_element_type=f32)


def iota(shape, dim):
    return lax.broadcasted_iota(jnp.int32, shape, dim)


def column_of(row):
    n = row.shape[1]
    eye = iota((n, n), 0) == iota((n, n), 1)
    return jnp.sum(jnp.where(eye, jnp.broadcast_to(row, (n, n)), 0.0), axis=1, keepdims=True)


def clip_kernel(video_ref, token_ref, pool_ref, out_ref, weight_scr, num_scr):
    step = pl.program_id(0)

    @pl.when(step == 0)
    def _():
        weight_scr[...] = jnp.zeros_like(weight_scr)

    x = token_ref[...]
    scores = dot(pool_ref[...], x, NT)
    weights = jnp.exp(SOFT_CAP * jnp.tanh(scores / SOFT_CAP))
    weight_scr[0:H, :] = weights
    weight_scr[32 : 32 + H, :] = weights
    mine = iota((CHUNK, TOKS), 1) // TOK == iota((CHUNK, TOKS), 0)
    rows = pl.ds(step * CHUNK, CHUNK)
    den = dot(mine.astype(f32).astype(bf16), weight_scr[...].astype(bf16), NT)
    den_hi = den.astype(bf16).astype(f32)
    select = iota((CHUNK, CLIPS), 1) == iota((CHUNK, CLIPS), 0) + step * CHUNK
    video = jnp.sum(
        jnp.where(select, jnp.broadcast_to(video_ref[...].astype(f32), (CHUNK, CLIPS)), 0.0),
        axis=1,
        keepdims=True,
    ).astype(jnp.int32)
    lane = iota((CHUNK, 128), 1)
    local = jnp.where(lane - 64 == video % 8, 1.0, 0.0)
    tail = jnp.where(lane < 32, den_hi, jnp.where(lane < 64, den - den_hi, local))
    num_scr[rows, D:TAIL] = tail.astype(bf16)
    for h in range(0, H, 2):
        pair = range(h, min(h + 2, H))
        lhs = jnp.concatenate(
            [
                jnp.where(mine, jnp.broadcast_to(weight_scr[k : k + 1, :], (CHUNK, TOKS)), 0.0)
                for k in pair
            ],
            axis=0,
        ).astype(bf16)
        part = dot(lhs, x[:, h * HD : (h + len(pair)) * HD])
        for n, k in enumerate(pair):
            num_scr[rows, k * HD : (k + 1) * HD] = part[
                n * CHUNK : (n + 1) * CHUNK, n * HD : (n + 1) * HD
            ].astype(bf16)

    @pl.when(step == pl.num_programs(0) - 1)
    def _():
        owner = (video_ref[...] // 8).astype(f32)
        owner_col = column_of(owner)
        before = (owner_col == owner) & (iota((CLIPS, CLIPS), 0) < iota((CLIPS, CLIPS), 1))
        rank = jnp.sum(jnp.where(before, 1.0, 0.0), axis=0, keepdims=True)
        slot = (owner * 2.0 + rank).astype(jnp.int32)
        place = jnp.where(iota((SLOTS, CLIPS), 0) == slot, 1.0, 0.0).astype(bf16)
        out_ref[...] = dot(place, num_scr[...]).astype(bf16)


def clip_sums(clip_tokens, clip_video, pool_vectors):
    tokens = clip_tokens.reshape(CLIPS * TOK, D)
    return pl.pallas_call(
        clip_kernel,
        grid=(CLIPS // CHUNK,),
        in_specs=[
            pl.BlockSpec((1, CLIPS), lambda i: (0, 0)),
            pl.BlockSpec((TOKS, D), lambda i: (i, 0)),
            pl.BlockSpec((H, D), lambda i: (0, 0)),
        ],
        out_specs=pl.BlockSpec((SLOTS, TAIL), lambda i: (0, 0)),
        out_shape=jax.ShapeDtypeStruct((SLOTS, TAIL), bf16),
        scratch_shapes=[pltpu.VMEM((128, TOKS), f32), pltpu.VMEM((CLIPS, TAIL), bf16)],
        compiler_params=pltpu.CompilerParams(vmem_limit_bytes=24 << 20),
        cost_estimate=pl.CostEstimate(
            flops=2 * 1024 * D * 64, bytes_accessed=8 << 20, transcendentals=1 << 17
        ),
    )(clip_video.reshape(1, CLIPS), tokens, pool_vectors)


def embed_kernel(arrived_ref, proj_ref, emb_ref, hat_ref, norm_ref, send_ref):
    assign = arrived_ref[:, D:TAIL].astype(f32).T[64:72, :].astype(bf16)
    sums = dot(assign, arrived_ref[...])
    den = sums[:, D : D + 32] + sums[:, D + 32 : D + 64]
    pooled = jnp.concatenate(
        [sums[:, h * HD : (h + 1) * HD] / den[:, h : h + 1] for h in range(H)], axis=1
    )
    hi = pooled.astype(bf16).astype(f32)
    mid = (pooled - hi).astype(bf16).astype(f32)
    low = pooled - hi - mid
    parts = dot(jnp.concatenate([hi, mid, low], axis=0).astype(bf16), proj_ref[...])
    emb = parts[0:8] + parts[8:16] + parts[16:24]
    norm = jnp.sqrt(jnp.sum(emb * emb, axis=1, keepdims=True) + EPS)
    hat = emb / norm
    emb_ref[...] = emb.astype(bf16)
    hat_ref[...] = hat
    norm_ref[...] = norm
    hat_low = hat.astype(bf16)
    for k in range(8):
        send_ref[k] = hat_low


def embed(arrived, out_proj):
    return pl.pallas_call(
        embed_kernel,
        in_specs=[VMEM, VMEM],
        out_specs=[VMEM] * 4,
        out_shape=[
            jax.ShapeDtypeStruct((8, E), bf16),
            jax.ShapeDtypeStruct((8, E), f32),
            jax.ShapeDtypeStruct((8, 1), f32),
            jax.ShapeDtypeStruct((8, 8, E), bf16),
        ],
        compiler_params=pltpu.CompilerParams(vmem_limit_bytes=24 << 20),
        cost_estimate=pl.CostEstimate(
            flops=2 * 24 * D * E, bytes_accessed=6 << 20, transcendentals=0
        ),
    )(arrived, out_proj)


def logits_kernel(
    place_ref, video_ref, own_ref, other_ref, near_ref,
    payload_ref, rowsum_ref, rows_ref, cols_ref, tile_scr, sum_scr,
):
    base = pl.multiple_of(place_ref[0], 8)
    side = place_ref[1].astype(f32)
    code = own_ref[:, E:ETEXT].astype(f32)
    target = code[:, 0:1] * 64.0 + code[:, 1:2] + 1024.0 * side
    target = jnp.where(target >= 2048.0, target - 2048.0, target)
    videos = video_ref[...]
    positive = jnp.zeros((1, TILE), f32)
    lane = iota((1, TILE), 1).astype(f32)
    for t in range(8):
        ref = own_ref if t < 4 else other_ref
        texts = ref[t % 4 * TILE : (t % 4 + 1) * TILE, 0:E]
        logits = SCALE * dot(videos, texts, NT)
        ex = jnp.exp(logits)
        tile_scr[...] = ex
        payload_ref[:, t * TILE : (t + 1) * TILE] = jnp.sum(ex, axis=0, keepdims=True)
        halves = ex[:, 0:128] + ex[:, 128:TILE]
        if t == 0:
            sum_scr[...] = halves
        else:
            sum_scr[...] += halves
        hit = target - float(t * TILE) == lane
        positive += jnp.sum(jnp.where(hit, logits, 0.0), axis=0, keepdims=True)
        rows_ref[:, t * TILE : (t + 1) * TILE] = tile_scr[pl.ds(base, 8), :]
    rowsum = jnp.sum(sum_scr[...], axis=1, keepdims=True)
    rowsum_ref[...] = rowsum
    cols = jnp.exp(SCALE * dot(videos, near_ref[...], NT))
    cols_ref[...] = cols
    colsum = jnp.sum(cols, axis=0, keepdims=True)
    total = jnp.sum(jnp.log(rowsum), axis=0, keepdims=True) - 2.0 * jnp.sum(
        positive, axis=1, keepdims=True
    )
    payload_ref[:, 2048:2176] = jnp.concatenate([colsum, jnp.zeros((1, 112), f32)], axis=1)
    payload_ref[:, 2176:2304] = jnp.broadcast_to(total, (1, 128))


def all_logits(place, videos, own, other, near):
    return pl.pallas_call(
        logits_kernel,
        in_specs=[SMEM] + [VMEM] * 4,
        out_specs=[VMEM] * 4,
        out_shape=[
            jax.ShapeDtypeStruct((1, 2304), f32),
            jax.ShapeDtypeStruct((HALF, 1), f32),
            jax.ShapeDtypeStruct((8, 2048), f32),
            jax.ShapeDtypeStruct((HALF, 16), f32),
        ],
        scratch_shapes=[pltpu.VMEM((HALF, TILE), f32), pltpu.VMEM((HALF, 128), f32)],
        compiler_params=pltpu.CompilerParams(vmem_limit_bytes=32 << 20),
        cost_estimate=pl.CostEstimate(
            flops=2 * HALF * 2048 * E, bytes_accessed=6 << 20, transcendentals=1 << 21
        ),
    )(place, videos, own, other, near)


def grad_kernel(
    place_ref, mine_ref, theirs_ref, rowsum_ref, rows_ref, cols_ref, video_ref, own_ref, other_ref,
    hat_ref, norm_ref, target_ref, loss_ref, grad_ref, near_ref, far_ref,
):
    base = place_ref[0].astype(f32)
    side = place_ref[1].astype(f32)
    mine, theirs = mine_ref[...], theirs_ref[...]
    colsum = mine[:, 0:2048] + jnp.concatenate([theirs[:, 1024:2048], theirs[:, 0:1024]], axis=1)
    loss = mine[:, 2176:2177] + theirs[:, 2176:2177]
    loss += jnp.sum(jnp.log(colsum), axis=1, keepdims=True)
    loss_ref[...] = loss / 4096.0
    rows = rows_ref[...]
    target = target_ref[...] + 1024.0 * side
    target = jnp.where(target >= 2048.0, target - 2048.0, target)
    hot = jnp.where(target == iota((8, 2048), 1).astype(f32), 2.0, 0.0)
    probe = rows / jnp.sum(rows, axis=1, keepdims=True) + rows / colsum - hot
    probe = probe.astype(bf16)
    direction = SCALE * (
        dot(probe[:, 0:HALF], own_ref[:, 0:E]) + dot(probe[:, HALF:2048], other_ref[:, 0:E])
    )
    hat = hat_ref[...]
    grad_ref[...] = (
        direction - jnp.sum(direction * hat, axis=1, keepdims=True) * hat
    ) / norm_ref[...]
    far = theirs[:, 2048:2176]
    nearsum = mine[:, 2048:2064] + jnp.concatenate([far[:, 8:16], far[:, 0:8]], axis=1)
    code = own_ref[:, E:ETEXT].astype(f32)
    target = code[:, 0:1] * 64.0 + code[:, 1:2] + 1024.0 * side
    target = jnp.where(target >= 2048.0, target - 2048.0, target)
    spot = iota((1, 16), 1)
    place = jnp.where(spot < 8, spot, spot - 8 + HALF).astype(f32) + base
    cols = cols_ref[...]
    hot = jnp.where(target == place, 2.0, 0.0)
    probe = (cols / rowsum_ref[...] + cols / nearsum - hot).astype(bf16)
    text = SCALE * dot(probe, video_ref[...], TN)
    near_ref[...] = text[0:8]
    far_ref[...] = text[8:16]


def gradients(*args):
    return pl.pallas_call(
        grad_kernel,
        in_specs=[SMEM] + [VMEM] * 11,
        out_specs=[VMEM] * 4,
        out_shape=[
            jax.ShapeDtypeStruct((1, 1), f32),
            jax.ShapeDtypeStruct((8, E), f32),
            jax.ShapeDtypeStruct((8, E), f32),
            jax.ShapeDtypeStruct((8, E), f32),
        ],
        compiler_params=pltpu.CompilerParams(vmem_limit_bytes=32 << 20),
        cost_estimate=pl.CostEstimate(
            flops=2 * 32 * 2048 * E, bytes_accessed=8 << 20, transcendentals=2048
        ),
    )(*args)


def unit_rows(values):
    norms = jnp.sqrt(jnp.sum(values * values, axis=1, keepdims=True) + EPS)
    return values / norms, norms


def spread(block):
    n = block.shape[-1]
    column = lax.all_to_all(block, "z", 0, 0, tiled=True).reshape(64, n)
    wide = jnp.broadcast_to(column[None], (16, 64, n))
    return lax.all_to_all(wide, WIDE, 0, 0, tiled=True).reshape(HALF, n)


def swap(x):
    return lax.ppermute(x, "c", [(0, 1), (1, 0)])


def body(clip_tokens, clip_video, pool_vectors, out_proj, text_embed, pair_text):
    xh, c, xl, z, y = (lax.axis_index(a) for a in ALL)
    base = (((xh * 2 + xl) * 4 + y) * 8 + z) * 8
    place = jnp.stack([base, c]).astype(jnp.int32)
    device, row = pair_text // 8, pair_text % 8
    spot = ((device // 128 * 2 + device // 32 % 2) * 4 + device % 4) * 8 + device // 4 % 8
    target = (device // 64 % 2) * HALF + spot * 8 + row
    text_hat, text_norm = unit_rows(text_embed.astype(f32))
    text_low = text_hat.astype(bf16)
    code = jnp.stack([target // 64, target % 64], axis=1).astype(bf16)
    text_row = jnp.concatenate([text_low, jnp.pad(code, ((0, 0), (0, 126)))], axis=1)
    own = spread(jnp.broadcast_to(text_row[None], (8, 8, ETEXT)))
    other = swap(own)
    near = jnp.concatenate([text_low, lax.dynamic_slice(other, (base, 0), (8, E))], axis=0)

    outgoing = clip_sums(clip_tokens, clip_video, pool_vectors)
    arrived = lax.all_to_all(outgoing.reshape(64, 2, TAIL), ROW, 0, 0, tiled=True)
    video_embed, video_hat, video_norm, send = embed(arrived.reshape(SLOTS, TAIL), out_proj)
    videos = spread(send)
    payload, rowsum, rows, cols = all_logits(place, videos, own, other, near)
    theirs = swap(payload)
    loss, video_grad, near_dir, far_dir = gradients(
        place, payload, theirs, rowsum, rows, cols, videos, own, other,
        video_hat, video_norm, target.astype(f32)[:, None],
    )
    text_dir = near_dir + swap(far_dir)
    text_grad = (
        text_dir - jnp.sum(text_dir * text_hat, axis=1, keepdims=True) * text_hat
    ) / text_norm
    return video_embed, video_grad, text_grad, loss.reshape(())


def solution(mesh):
    split = Mesh(mesh.devices.reshape(2, 2, 2, 8, 4), ALL)
    return jax.shard_map(
        body,
        mesh=split,
        in_specs=(P(ALL, None, None), P(ALL), P(), P(), P(ALL, None), P(ALL)),
        out_specs=(P(ALL, None), P(ALL, None), P(ALL, None), P()),
        check_vma=False,
    )
```

```python
import jax
import jax.numpy as jnp
from jax import lax
from jax.experimental import pallas as pl
from jax.experimental.pallas import tpu as pltpu
from jax.sharding import Mesh, PartitionSpec as P

H = 25
HD = 128
D = 3200
E = 768
TOK = 16
CLIPS = 64
SOFT_CAP = 20.0
SCALE = 40.0
EPS = 1e-06
ALL = ("xh", "c", "xl", "z", "y")
ROW = ("xl", "z", "y")
PLANE = ("z", "y")
GROUP = ("xh", "c", "xl")
CHUNK = 16
TOKS = CHUNK * TOK
PARTS = 4
WIDE = 7
SENT = WIDE * HD
TAIL = 4 * HD
TILE = 256
SET = 512
PLANE_ROWS = 256
VMEM = pl.BlockSpec(memory_space=pltpu.VMEM)
f32 = jnp.float32
bf16 = jnp.bfloat16
NT = (((1,), (1,)), ((), ()))
TN = (((0,), (0,)), ((), ()))


def dot(a, b, dims=(((1,), (0,)), ((), ()))):
    return lax.dot_general(a, b, dims, preferred_element_type=f32)


def iota(shape, dim):
    return lax.broadcasted_iota(jnp.int32, shape, dim)


def column_of(row):
    n = row.shape[1]
    eye = iota((n, n), 0) == iota((n, n), 1)
    return jnp.sum(jnp.where(eye, jnp.broadcast_to(row, (n, n)), 0.0), axis=1, keepdims=True)


def unit_rows(values):
    norms = jnp.sqrt(jnp.sum(values * values, axis=1, keepdims=True) + EPS)
    return values / norms, norms


def clip_kernel(
    video_ref, token_ref, pool_ref, text_ref, pair_ref,
    out_ref, hat_ref, norm_ref, weight_scr, num_scr,
):
    step = pl.program_id(0)

    @pl.when(step == 0)
    def _():
        weight_scr[...] = jnp.zeros_like(weight_scr)
        num_scr[...] = jnp.zeros_like(num_scr)
        hat, norm = unit_rows(text_ref[...].astype(f32))
        hat_ref[...] = hat
        norm_ref[...] = norm
        texts = jnp.broadcast_to(hat[None], (CLIPS, 8, E)).reshape(CLIPS * 8, E)
        out_ref[:, SENT : SENT + E] = texts.astype(bf16)

    x = token_ref[...]
    scores = dot(pool_ref[...], x, NT)
    weights = jnp.exp(SOFT_CAP * jnp.tanh(scores / SOFT_CAP))
    weight_scr[0:H, :] = weights
    weight_scr[32 : 32 + H, :] = weights
    mine = iota((CHUNK, TOKS), 1) // TOK == iota((CHUNK, TOKS), 0)
    den = dot(mine.astype(f32).astype(bf16), weight_scr[...].astype(bf16), NT)
    den_hi = den.astype(bf16).astype(f32)
    here = iota((CHUNK, CLIPS), 1) == iota((CHUNK, CLIPS), 0) + step * CHUNK
    video = jnp.broadcast_to(video_ref[...].astype(f32), (CHUNK, CLIPS))
    video = jnp.sum(jnp.where(here, video, 0.0), axis=1, keepdims=True).astype(jnp.int32)
    lane = iota((CHUNK, HD), 1)
    local = jnp.where(lane - 64 == video % 8, 1.0, 0.0)
    tail = jnp.where(lane < 32, den_hi, jnp.where(lane < 64, den - den_hi, local))

    def put(j, value):
        rows = pl.ds(pl.multiple_of(j // WIDE * CLIPS + step * CHUNK, CHUNK), CHUNK)
        num_scr[rows, j % WIDE * HD : (j % WIDE + 1) * HD] = value.astype(bf16)

    put(H, tail)
    for h in range(0, H, 2):
        pair = range(h, min(h + 2, H))
        lhs = jnp.concatenate(
            [
                jnp.where(mine, jnp.broadcast_to(weight_scr[k : k + 1, :], (CHUNK, TOKS)), 0.0)
                for k in pair
            ],
            axis=0,
        ).astype(bf16)
        part = dot(lhs, x[:, h * HD : (h + len(pair)) * HD])
        for n, k in enumerate(pair):
            put(k, part[n * CHUNK : (n + 1) * CHUNK, n * HD : (n + 1) * HD])

    @pl.when(step == pl.num_programs(0) - 1)
    def _():
        owner = (video_ref[...] // 8).astype(f32)
        before = (column_of(owner) == owner) & (
            iota((CLIPS, CLIPS), 0) < iota((CLIPS, CLIPS), 1)
        )
        rank = jnp.sum(jnp.where(before, 1.0, 0.0), axis=0, keepdims=True)
        slot = owner * 2.0 + rank
        slots = jnp.concatenate([slot] * PARTS, axis=1).astype(jnp.int32)
        shape = (CLIPS * 8, PARTS * CLIPS)
        row, col = iota(shape, 0), iota(shape, 1)
        place = (row // PARTS == slots) & (row % PARTS == col // CLIPS)
        out = dot(jnp.where(place, 1.0, 0.0).astype(bf16), num_scr[...])
        pair = pair_ref[...]
        codes = jnp.concatenate(
            [
                jnp.zeros((1, 72), f32),
                (pair // 64).astype(f32),
                (pair % 64).astype(f32),
                jnp.zeros((1, 40), f32),
            ],
            axis=1,
        )
        last = iota((CLIPS * 8, HD), 0) % PARTS == PARTS - 1
        out_ref[:, 0:TAIL] = out[:, 0:TAIL].astype(bf16)
        out_ref[:, TAIL : TAIL + HD] = (
            out[:, TAIL : TAIL + HD] + jnp.where(last, codes, 0.0)
        ).astype(bf16)
        out_ref[:, TAIL + HD : SENT] = out[:, TAIL + HD : SENT].astype(bf16)


def clip_sums(clip_tokens, clip_video, pool_vectors, text_embed, pair_text):
    whole = lambda *shape: pl.BlockSpec(shape, lambda i: (0,) * len(shape))
    return pl.pallas_call(
        clip_kernel,
        grid=(CLIPS // CHUNK,),
        in_specs=[
            whole(1, CLIPS),
            pl.BlockSpec((TOKS, D), lambda i: (i, 0)),
            whole(H, D),
            whole(8, E),
            whole(1, 8),
        ],
        out_specs=[whole(CLIPS * 8, SENT + E), whole(8, E), whole(8, 1)],
        out_shape=[
            jax.ShapeDtypeStruct((CLIPS * 8, SENT + E), bf16),
            jax.ShapeDtypeStruct((8, E), f32),
            jax.ShapeDtypeStruct((8, 1), f32),
        ],
        scratch_shapes=[pltpu.VMEM((128, TOKS), f32), pltpu.VMEM((PARTS * CLIPS, SENT), bf16)],
        compiler_params=pltpu.CompilerParams(vmem_limit_bytes=56 << 20),
        cost_estimate=pl.CostEstimate(
            flops=2 * 1024 * D * 64, bytes_accessed=8 << 20, transcendentals=1 << 17
        ),
    )(
        clip_video.reshape(1, CLIPS),
        clip_tokens.reshape(CLIPS * TOK, D),
        pool_vectors,
        text_embed,
        pair_text.reshape(1, 8),
    )


def embed_kernel(
    arrived_ref, proj_ref, emb_ref, hat_ref, norm_ref, send_ref, text_ref, target_ref
):
    rows = CLIPS * 8
    text_ref[...] = arrived_ref[:, SENT : SENT + E]
    tails = arrived_ref[:, TAIL : TAIL + HD]
    pick = jnp.where(iota((8, HD), 1) - 64 == iota((8, HD), 0), 1.0, 0.0).astype(bf16)
    hot = dot(pick, tails, NT)
    hot = jnp.where(iota((8, rows), 1) % PARTS == PARTS - 1, hot, 0.0)
    assign = jnp.concatenate(
        [hot if p == PARTS - 1 else pltpu.roll(hot, rows - (PARTS - 1 - p), 1) for p in range(PARTS)],
        axis=0,
    )
    sums = dot(assign.astype(bf16), arrived_ref[:, 0:SENT])

    def chunk(j):
        p, q = j // WIDE, j % WIDE
        return sums[p * 8 : (p + 1) * 8, q * HD : (q + 1) * HD]

    den = chunk(H)
    den = den[:, 0:32] + den[:, 32:64]
    pooled = jnp.concatenate([chunk(h) / den[:, h : h + 1] for h in range(H)], axis=1)
    hi = pooled.astype(bf16).astype(f32)
    mid = (pooled - hi).astype(bf16).astype(f32)
    low = pooled - hi - mid
    parts = dot(jnp.concatenate([hi, mid, low], axis=0).astype(bf16), proj_ref[...])
    emb = parts[0:8] + parts[8:16] + parts[16:24]
    emb_ref[...] = emb.astype(bf16)
    hat, norm = unit_rows(emb)
    hat_ref[...] = hat
    norm_ref[...] = norm
    hat_low = hat.astype(bf16)
    for k in range(32):
        send_ref[k] = hat_low
    code = tails.astype(f32).reshape(CLIPS, 8, HD)[:, 3:4, :]
    code = jnp.broadcast_to(code, (CLIPS, 8, HD)).reshape(rows, HD)
    lane, own = iota((rows, HD), 1), iota((rows, HD), 0) % 8
    code = jnp.where(lane - 72 == own, 64.0 * code, jnp.where(lane - 80 == own, code, 0.0))
    target_ref[...] = jnp.sum(code, axis=1, keepdims=True)


def embed(arrived, out_proj):
    return pl.pallas_call(
        embed_kernel,
        in_specs=[VMEM, VMEM],
        out_specs=[VMEM] * 6,
        out_shape=[
            jax.ShapeDtypeStruct((8, E), bf16),
            jax.ShapeDtypeStruct((8, E), f32),
            jax.ShapeDtypeStruct((8, 1), f32),
            jax.ShapeDtypeStruct((32, 8, E), bf16),
            jax.ShapeDtypeStruct((SET, E), bf16),
            jax.ShapeDtypeStruct((SET, 1), f32),
        ],
        compiler_params=pltpu.CompilerParams(vmem_limit_bytes=24 << 20),
        cost_estimate=pl.CostEstimate(
            flops=2 * 24 * D * E, bytes_accessed=6 << 20, transcendentals=0
        ),
    )(arrived, out_proj)


def position():
    xh, c, xl, z, y = (lax.axis_index(a) for a in ALL)
    return xh, c, xl, z * 4 + y


def rows_of(xh, c, k):
    a, b = k // 2, k % 2
    return (xh + a - 2 * a * xh) * 2 + (c + b - 2 * b * c)


def logits_kernel(
    video_ref, target_ref, set0_ref, set1_ref, set2_ref, set3_ref,
    send_ref, own_ref, tile_scr, col_scr,
):
    xh, c, xl, spot = position()
    sets = (set0_ref, set1_ref, set2_ref, set3_ref)
    target = target_ref[pl.ds(pl.multiple_of(xl * PLANE_ROWS, PLANE_ROWS), PLANE_ROWS), :]
    videos = video_ref[...]
    lane = iota((1, TILE), 1).astype(f32)
    base = pl.multiple_of(spot * 8, 8)
    positive = jnp.zeros((1, TILE), f32)
    halves = jnp.zeros((PLANE_ROWS, 128), f32)
    for k, ref in enumerate(sets):
        row = rows_of(xh, c, k)
        for t in range(2):
            tile = row * 2 + t
            logits = SCALE * dot(videos, ref[t * TILE : (t + 1) * TILE, :], NT)
            ex = jnp.exp(logits)
            tile_scr[...] = ex
            col_scr[pl.ds(tile, 1), :] = jnp.sum(ex, axis=0, keepdims=True)
            halves += ex[:, 0:128] + ex[:, 128:TILE]
            hit = target == (tile * TILE).astype(f32) + lane
            positive += jnp.sum(jnp.where(hit, logits, 0.0), axis=0, keepdims=True)
            at = k * SET + t * TILE
            own_ref[:, at : at + TILE] = tile_scr[pl.ds(base, 8), :]
    rowsum = jnp.sum(halves, axis=1, keepdims=True)
    total = jnp.sum(jnp.log(rowsum), axis=0, keepdims=True) - 2.0 * jnp.sum(
        positive, axis=1, keepdims=True
    )
    odd = spot % 2 == 1
    near, groups = [], []
    for k, ref in enumerate(sets):
        for half in range(2):
            at = pl.multiple_of(half * PLANE_ROWS + spot // 2 * 16, 16)
            pair = ref[pl.ds(at, 16), :].astype(f32)
            near.append(jnp.where(odd, pair[8:16], pair[0:8]))
            groups.append(rows_of(xh, c, k) * 2 + half)
    near = jnp.concatenate(near, axis=0).astype(bf16)
    ex = jnp.exp(SCALE * dot(videos, near, NT))
    slot = iota((1, 64), 1)
    group = sum(jnp.where(slot // 8 == n, g, 0) for n, g in enumerate(groups))
    text = ((group * 32 + spot) * 8 + slot % 8).astype(f32)
    first = ex / rowsum - jnp.where(target == text, 2.0, 0.0)
    first_hi = first.astype(bf16).astype(f32)
    ex_hi = ex.astype(bf16).astype(f32)
    terms = jnp.concatenate([first_hi, first - first_hi, ex_hi, ex - ex_hi], axis=1)
    sums = dot(terms.astype(bf16), videos, TN)
    first, second = sums[0:64] + sums[64:128], sums[128:192] + sums[192:256]
    cols = col_scr[...]
    total = jnp.broadcast_to(total, (8, 128))
    for n, g in enumerate(groups):
        send_ref[g, :, 0:E] = first[n * 8 : (n + 1) * 8]
        send_ref[g, :, E : 2 * E] = second[n * 8 : (n + 1) * 8]
        send_ref[g, :, 2 * E : 2 * E + TILE] = cols
        send_ref[g, :, 2 * E + TILE :] = total


def all_logits(videos, target, *sets):
    return pl.pallas_call(
        logits_kernel,
        in_specs=[VMEM] * 6,
        out_specs=[VMEM] * 2,
        out_shape=[
            jax.ShapeDtypeStruct((8, 8, 2 * E + TILE + 128), f32),
            jax.ShapeDtypeStruct((8, 4 * SET), f32),
        ],
        scratch_shapes=[pltpu.VMEM((PLANE_ROWS, TILE), f32), pltpu.VMEM((8, TILE), f32)],
        compiler_params=pltpu.CompilerParams(vmem_limit_bytes=32 << 20),
        cost_estimate=pl.CostEstimate(
            flops=2 * PLANE_ROWS * 2048 * E, bytes_accessed=5 << 20, transcendentals=1 << 19
        ),
    )(videos, target, *sets)


def grad_kernel(
    arrived_ref, own_ref, target_ref, set0_ref, set1_ref, set2_ref, set3_ref,
    video_hat_ref, video_norm_ref, text_hat_ref, text_norm_ref,
    loss_ref, video_grad_ref, text_grad_ref, col_scr,
):
    xh, c, xl, spot = position()
    got = arrived_ref[0]
    for k in range(1, 8):
        got = got + arrived_ref[k]
    cols = got[:, 2 * E : 2 * E + TILE]
    col_scr[...] = cols
    logs = jnp.sum(jnp.sum(jnp.log(cols), axis=0, keepdims=True), axis=1, keepdims=True)
    loss_ref[...] = (logs + got[0:1, 2 * E + TILE : 2 * E + TILE + 1]) / 4096.0

    def project(direction, hat, norm):
        return (direction - jnp.sum(direction * hat, axis=1, keepdims=True) * hat) / norm

    group = (xh * 2 + c) * 2 + xl
    mine = jnp.broadcast_to(col_scr[pl.ds(group, 1), :], (8, TILE))
    here = iota((8, TILE), 1) == spot * 8 + iota((8, TILE), 0)
    mine = jnp.sum(jnp.where(here, mine, 0.0), axis=1, keepdims=True)
    text_dir = SCALE * (got[:, 0:E] + got[:, E : 2 * E] / mine)
    text_grad_ref[...] = project(text_dir, text_hat_ref[...], text_norm_ref[...])

    rows = own_ref[...]
    rowsum = jnp.sum(rows, axis=1, keepdims=True)
    target = target_ref[pl.ds(pl.multiple_of((xl * 32 + spot) * 8, 8), 8), :]
    lane = iota((8, TILE), 1).astype(f32)
    direction = jnp.zeros((8, E), f32)
    for k, ref in enumerate((set0_ref, set1_ref, set2_ref, set3_ref)):
        row = rows_of(xh, c, k)
        for t in range(2):
            tile = row * 2 + t
            at = k * SET + t * TILE
            ex = rows[:, at : at + TILE]
            hot = jnp.where(target == (tile * TILE).astype(f32) + lane, 2.0, 0.0)
            probe = ex / rowsum + ex / col_scr[pl.ds(tile, 1), :] - hot
            direction += dot(probe.astype(bf16), ref[t * TILE : (t + 1) * TILE, :])
    video_grad_ref[...] = project(SCALE * direction, video_hat_ref[...], video_norm_ref[...])


def gradients(*args):
    return pl.pallas_call(
        grad_kernel,
        in_specs=[VMEM] * 11,
        out_specs=[VMEM] * 3,
        out_shape=[
            jax.ShapeDtypeStruct((1, 1), f32),
            jax.ShapeDtypeStruct((8, E), f32),
            jax.ShapeDtypeStruct((8, E), f32),
        ],
        scratch_shapes=[pltpu.VMEM((8, TILE), f32)],
        compiler_params=pltpu.CompilerParams(vmem_limit_bytes=32 << 20),
        cost_estimate=pl.CostEstimate(
            flops=2 * 8 * 2048 * E, bytes_accessed=5 << 20, transcendentals=2048
        ),
    )(*args)


def exchange(x, axes):
    return lax.all_to_all(x, axes, 0, 0, tiled=True)


def swap(x):
    return lax.ppermute(x, "c", [(0, 1), (1, 0)])


def cross(x):
    return lax.ppermute(x, ("xh", "xl"), [(0, 3), (3, 0), (1, 2), (2, 1)])


def body(clip_tokens, clip_video, pool_vectors, out_proj, text_embed, pair_text):
    outgoing, text_hat, text_norm = clip_sums(
        clip_tokens, clip_video, pool_vectors, text_embed, pair_text
    )
    arrived = exchange(outgoing.reshape(CLIPS, 8, SENT + E), ROW)
    video_embed, video_hat, video_norm, send, texts, target = embed(
        arrived.reshape(CLIPS * 8, SENT + E), out_proj
    )
    crossed = cross(texts)
    sets = (texts, swap(texts), crossed, swap(crossed))
    videos = exchange(send, PLANE).reshape(PLANE_ROWS, E)
    terms, own = all_logits(videos, target, *sets)
    loss, video_grad, text_grad = gradients(
        exchange(terms, GROUP), own, target, *sets, video_hat, video_norm, text_hat, text_norm
    )
    return video_embed, video_grad, text_grad, loss.reshape(())


def solution(mesh):
    split = Mesh(mesh.devices.reshape(2, 2, 2, 8, 4), ALL)
    return jax.shard_map(
        body,
        mesh=split,
        in_specs=(P(ALL, None, None), P(ALL), P(), P(), P(ALL, None), P(ALL)),
        out_specs=(P(ALL, None), P(ALL, None), P(ALL, None), P()),
        check_vma=False,
    )
```

```python
import jax
import jax.numpy as jnp
from jax import lax
from jax.experimental import pallas as pl
from jax.experimental.pallas import tpu as pltpu
from jax.sharding import Mesh, PartitionSpec as P

H = 25
HD = 128
D = 3200
E = 768
TOK = 16
CLIPS = 64
SOFT_CAP = 20.0
SCALE = 40.0
EPS = 1e-06
ALL = ("xh", "c", "xl", "z", "y")
ROW = ("xl", "z", "y")
PLANE = ("z", "y")
GROUP = ("xh", "c", "xl")
CHUNK = 32
TOKS = CHUNK * TOK
STEPS = CLIPS // CHUNK
PARTS = 4
WIDE = 7
SENT = WIDE * HD
TAIL = 4 * HD
TILE = 256
SET = 512
PLANE_ROWS = 256
VMEM = pl.BlockSpec(memory_space=pltpu.VMEM)
f32 = jnp.float32
bf16 = jnp.bfloat16
NT = (((1,), (1,)), ((), ()))
TN = (((0,), (0,)), ((), ()))


def dot(a, b, dims=(((1,), (0,)), ((), ()))):
    return lax.dot_general(a, b, dims, preferred_element_type=f32)


def iota(shape, dim):
    return lax.broadcasted_iota(jnp.int32, shape, dim)


def column_of(row):
    n = row.shape[1]
    eye = iota((n, n), 0) == iota((n, n), 1)
    return jnp.sum(jnp.where(eye, jnp.broadcast_to(row, (n, n)), 0.0), axis=1, keepdims=True)


def unit_rows(values):
    norms = jnp.sqrt(jnp.sum(values * values, axis=1, keepdims=True) + EPS)
    return values / norms, norms


def clip_kernel(
    video_hbm, token_hbm, pool_hbm, text_hbm, pair_hbm,
    out_ref, hat_ref, norm_ref,
    video_ref, token_ref, pool_ref, text_ref, pair_ref, weight_scr, num_scr, sems,
):
    small = ((pool_hbm, pool_ref), (video_hbm, video_ref), (text_hbm, text_ref), (pair_hbm, pair_ref))
    chunks = [pl.ds(i * TOKS, TOKS) for i in range(STEPS)]
    loads = [
        pltpu.make_async_copy(token_hbm.at[chunk], token_ref.at[chunk], sems.at[i])
        for i, chunk in enumerate(chunks)
    ]
    early = [
        pltpu.make_async_copy(src, dst, sems.at[STEPS + i]) for i, (src, dst) in enumerate(small)
    ]
    early[0].start()
    loads[0].start()
    for copy in early[1:] + loads[1:]:
        copy.start()
    weight_scr[...] = jnp.zeros_like(weight_scr)
    num_scr[...] = jnp.zeros_like(num_scr)
    mine = iota((CHUNK, TOKS), 1) // TOK == iota((CHUNK, TOKS), 0)
    ones = mine.astype(f32).astype(bf16)
    lane = iota((CHUNK, HD), 1)
    for copy in early[1:]:
        copy.wait()
    videos = video_ref[...].astype(f32)
    hat, norm = unit_rows(text_ref[...].astype(f32))
    hat_ref[...] = hat
    norm_ref[...] = norm
    texts = jnp.broadcast_to(hat[None], (CLIPS, 8, E)).reshape(CLIPS * 8, E)
    out_ref[:, SENT : SENT + E] = texts.astype(bf16)
    early[0].wait()
    pool = pool_ref[...]

    def put(step, j, value):
        at = j // WIDE * CLIPS + step * CHUNK
        num_scr[at : at + CHUNK, j % WIDE * HD : (j % WIDE + 1) * HD] = value.astype(bf16)

    def weigh(step):
        loads[step].wait()
        scores = dot(pool, token_ref[chunks[step], :], NT)
        weights = jnp.exp(SOFT_CAP * jnp.tanh(scores / SOFT_CAP))
        weight_scr[step, 0:H, :] = weights
        weight_scr[step, 32 : 32 + H, :] = weights

    def total(step):
        den = dot(ones, weight_scr[step].astype(bf16), NT)
        den_hi = den.astype(bf16).astype(f32)
        here = iota((CHUNK, CLIPS), 1) == iota((CHUNK, CLIPS), 0) + step * CHUNK
        video = jnp.where(here, jnp.broadcast_to(videos, (CHUNK, CLIPS)), 0.0)
        video = jnp.sum(video, axis=1, keepdims=True).astype(jnp.int32)
        local = jnp.where(lane - 64 == video % 8, 1.0, 0.0)
        tail = jnp.where(lane < 32, den_hi, jnp.where(lane < 64, den - den_hi, local))
        put(step, H, tail)
        for h in range(0, H, 2):
            pair = range(h, min(h + 2, H))
            lhs = jnp.concatenate(
                [
                    jnp.where(
                        mine, jnp.broadcast_to(weight_scr[step, k : k + 1, :], (CHUNK, TOKS)), 0.0
                    )
                    for k in pair
                ],
                axis=0,
            ).astype(bf16)
            part = dot(lhs, token_ref[chunks[step], h * HD : (h + len(pair)) * HD])
            for n, k in enumerate(pair):
                put(step, k, part[n * CHUNK : (n + 1) * CHUNK, n * HD : (n + 1) * HD])

    for step in range(STEPS):
        weigh(step)
        if step:
            total(step - 1)
    total(STEPS - 1)

    owner = (video_ref[...] // 8).astype(f32)
    before = (column_of(owner) == owner) & (iota((CLIPS, CLIPS), 0) < iota((CLIPS, CLIPS), 1))
    rank = jnp.sum(jnp.where(before, 1.0, 0.0), axis=0, keepdims=True)
    slot = owner * 2.0 + rank
    slots = jnp.concatenate([slot] * PARTS, axis=1).astype(jnp.int32)
    shape = (CLIPS * 8, PARTS * CLIPS)
    row, col = iota(shape, 0), iota(shape, 1)
    place = (row // PARTS == slots) & (row % PARTS == col // CLIPS)
    out = dot(jnp.where(place, 1.0, 0.0).astype(bf16), num_scr[...])
    pair = pair_ref[...]
    codes = jnp.concatenate(
        [
            jnp.zeros((1, 72), f32),
            (pair // 64).astype(f32),
            (pair % 64).astype(f32),
            jnp.zeros((1, 40), f32),
        ],
        axis=1,
    )
    last = iota((CLIPS * 8, HD), 0) % PARTS == PARTS - 1
    out_ref[:, 0:TAIL] = out[:, 0:TAIL].astype(bf16)
    out_ref[:, TAIL : TAIL + HD] = (
        out[:, TAIL : TAIL + HD] + jnp.where(last, codes, 0.0)
    ).astype(bf16)
    out_ref[:, TAIL + HD : SENT] = out[:, TAIL + HD : SENT].astype(bf16)


def clip_sums(clip_tokens, clip_video, pool_vectors, text_embed, pair_text):
    args = (
        clip_video.reshape(1, CLIPS),
        clip_tokens.reshape(CLIPS * TOK, D),
        pool_vectors,
        text_embed,
        pair_text.reshape(1, 8),
    )
    return pl.pallas_call(
        clip_kernel,
        in_specs=[pl.BlockSpec(memory_space=pltpu.HBM)] * 5,
        out_specs=[VMEM] * 3,
        out_shape=[
            jax.ShapeDtypeStruct((CLIPS * 8, SENT + E), bf16),
            jax.ShapeDtypeStruct((8, E), f32),
            jax.ShapeDtypeStruct((8, 1), f32),
        ],
        scratch_shapes=[pltpu.VMEM(x.shape, x.dtype) for x in args]
        + [
            pltpu.VMEM((STEPS, 128, TOKS), f32),
            pltpu.VMEM((PARTS * CLIPS, SENT), bf16),
            pltpu.SemaphoreType.DMA((STEPS + 4,)),
        ],
        compiler_params=pltpu.CompilerParams(vmem_limit_bytes=24 << 20),
        cost_estimate=pl.CostEstimate(
            flops=2 * 1024 * D * 64, bytes_accessed=8 << 20, transcendentals=1 << 17
        ),
    )(*(pltpu.with_memory_space_constraint(x, pltpu.HBM) for x in args))


def embed_kernel(
    arrived_ref, proj_ref, emb_ref, hat_ref, norm_ref, send_ref, text_ref, target_ref
):
    rows = CLIPS * 8
    text_ref[...] = arrived_ref[:, SENT : SENT + E]
    tails = arrived_ref[:, TAIL : TAIL + HD]
    pick = jnp.where(iota((8, HD), 1) - 64 == iota((8, HD), 0), 1.0, 0.0).astype(bf16)
    hot = dot(pick, tails, NT)
    hot = jnp.where(iota((8, rows), 1) % PARTS == PARTS - 1, hot, 0.0)
    assign = jnp.concatenate(
        [hot if p == PARTS - 1 else pltpu.roll(hot, rows - (PARTS - 1 - p), 1) for p in range(PARTS)],
        axis=0,
    )
    sums = dot(assign.astype(bf16), arrived_ref[:, 0:SENT])

    def chunk(j):
        p, q = j // WIDE, j % WIDE
        return sums[p * 8 : (p + 1) * 8, q * HD : (q + 1) * HD]

    den = chunk(H)
    den = den[:, 0:32] + den[:, 32:64]
    pooled = jnp.concatenate([chunk(h) / den[:, h : h + 1] for h in range(H)], axis=1)
    hi = pooled.astype(bf16).astype(f32)
    mid = (pooled - hi).astype(bf16).astype(f32)
    low = pooled - hi - mid
    parts = dot(jnp.concatenate([hi, mid, low], axis=0).astype(bf16), proj_ref[...])
    emb = parts[0:8] + parts[8:16] + parts[16:24]
    emb_ref[...] = emb.astype(bf16)
    hat, norm = unit_rows(emb)
    hat_ref[...] = hat
    norm_ref[...] = norm
    hat_low = hat.astype(bf16)
    for k in range(32):
        send_ref[k] = hat_low
    code = tails.astype(f32).reshape(CLIPS, 8, HD)[:, 3:4, :]
    code = jnp.broadcast_to(code, (CLIPS, 8, HD)).reshape(rows, HD)
    lane, own = iota((rows, HD), 1), iota((rows, HD), 0) % 8
    code = jnp.where(lane - 72 == own, 64.0 * code, jnp.where(lane - 80 == own, code, 0.0))
    target_ref[...] = jnp.sum(code, axis=1, keepdims=True)


def embed(arrived, out_proj):
    return pl.pallas_call(
        embed_kernel,
        in_specs=[VMEM, VMEM],
        out_specs=[VMEM] * 6,
        out_shape=[
            jax.ShapeDtypeStruct((8, E), bf16),
            jax.ShapeDtypeStruct((8, E), f32),
            jax.ShapeDtypeStruct((8, 1), f32),
            jax.ShapeDtypeStruct((32, 8, E), bf16),
            jax.ShapeDtypeStruct((SET, E), bf16),
            jax.ShapeDtypeStruct((SET, 1), f32),
        ],
        compiler_params=pltpu.CompilerParams(vmem_limit_bytes=24 << 20),
        cost_estimate=pl.CostEstimate(
            flops=2 * 24 * D * E, bytes_accessed=6 << 20, transcendentals=0
        ),
    )(arrived, out_proj)


def position():
    xh, c, xl, z, y = (lax.axis_index(a) for a in ALL)
    return xh, c, xl, z * 4 + y


def rows_of(xh, c, k):
    a, b = k // 2, k % 2
    return (xh + a - 2 * a * xh) * 2 + (c + b - 2 * b * c)


def logits_kernel(
    video_ref, target_ref, set0_ref, set1_ref, set2_ref, set3_ref,
    send_ref, own_ref, tile_scr, col_scr,
):
    xh, c, xl, spot = position()
    sets = (set0_ref, set1_ref, set2_ref, set3_ref)
    target = target_ref[pl.ds(pl.multiple_of(xl * PLANE_ROWS, PLANE_ROWS), PLANE_ROWS), :]
    videos = video_ref[...]
    lane = iota((1, TILE), 1).astype(f32)
    base = pl.multiple_of(spot * 8, 8)
    positive = jnp.zeros((1, TILE), f32)
    halves = jnp.zeros((PLANE_ROWS, 128), f32)
    for k, ref in enumerate(sets):
        row = rows_of(xh, c, k)
        for t in range(2):
            tile = row * 2 + t
            logits = SCALE * dot(videos, ref[t * TILE : (t + 1) * TILE, :], NT)
            ex = jnp.exp(logits)
            tile_scr[...] = ex
            col_scr[pl.ds(tile, 1), :] = jnp.sum(ex, axis=0, keepdims=True)
            halves += ex[:, 0:128] + ex[:, 128:TILE]
            hit = target == (tile * TILE).astype(f32) + lane
            positive += jnp.sum(jnp.where(hit, logits, 0.0), axis=0, keepdims=True)
            at = k * SET + t * TILE
            own_ref[:, at : at + TILE] = tile_scr[pl.ds(base, 8), :]
    rowsum = jnp.sum(halves, axis=1, keepdims=True)
    total = jnp.sum(jnp.log(rowsum), axis=0, keepdims=True) - 2.0 * jnp.sum(
        positive, axis=1, keepdims=True
    )
    odd = spot % 2 == 1
    near, groups = [], []
    for k, ref in enumerate(sets):
        for half in range(2):
            at = pl.multiple_of(half * PLANE_ROWS + spot // 2 * 16, 16)
            pair = ref[pl.ds(at, 16), :].astype(f32)
            near.append(jnp.where(odd, pair[8:16], pair[0:8]))
            groups.append(rows_of(xh, c, k) * 2 + half)
    near = jnp.concatenate(near, axis=0).astype(bf16)
    ex = jnp.exp(SCALE * dot(videos, near, NT))
    slot = iota((1, 64), 1)
    group = sum(jnp.where(slot // 8 == n, g, 0) for n, g in enumerate(groups))
    text = ((group * 32 + spot) * 8 + slot % 8).astype(f32)
    first = ex / rowsum - jnp.where(target == text, 2.0, 0.0)
    first_hi = first.astype(bf16).astype(f32)
    ex_hi = ex.astype(bf16).astype(f32)
    terms = jnp.concatenate([first_hi, first - first_hi, ex_hi, ex - ex_hi], axis=1)
    sums = dot(terms.astype(bf16), videos, TN)
    first, second = sums[0:64] + sums[64:128], sums[128:192] + sums[192:256]
    cols = col_scr[...]
    total = jnp.broadcast_to(total, (8, 128))
    for n, g in enumerate(groups):
        send_ref[g, :, 0:E] = first[n * 8 : (n + 1) * 8]
        send_ref[g, :, E : 2 * E] = second[n * 8 : (n + 1) * 8]
        send_ref[g, :, 2 * E : 2 * E + TILE] = cols
        send_ref[g, :, 2 * E + TILE :] = total


def all_logits(videos, target, *sets):
    return pl.pallas_call(
        logits_kernel,
        in_specs=[VMEM] * 6,
        out_specs=[VMEM] * 2,
        out_shape=[
            jax.ShapeDtypeStruct((8, 8, 2 * E + TILE + 128), f32),
            jax.ShapeDtypeStruct((8, 4 * SET), f32),
        ],
        scratch_shapes=[pltpu.VMEM((PLANE_ROWS, TILE), f32), pltpu.VMEM((8, TILE), f32)],
        compiler_params=pltpu.CompilerParams(vmem_limit_bytes=32 << 20),
        cost_estimate=pl.CostEstimate(
            flops=2 * PLANE_ROWS * 2048 * E, bytes_accessed=5 << 20, transcendentals=1 << 19
        ),
    )(videos, target, *sets)


def grad_kernel(
    arrived_ref, own_ref, target_ref, set0_ref, set1_ref, set2_ref, set3_ref,
    video_hat_ref, video_norm_ref, text_hat_ref, text_norm_ref,
    loss_ref, video_grad_ref, text_grad_ref, col_scr,
):
    xh, c, xl, spot = position()
    got = arrived_ref[0]
    for k in range(1, 8):
        got = got + arrived_ref[k]
    cols = got[:, 2 * E : 2 * E + TILE]
    col_scr[...] = cols
    logs = jnp.sum(jnp.sum(jnp.log(cols), axis=0, keepdims=True), axis=1, keepdims=True)
    loss_ref[...] = (logs + got[0:1, 2 * E + TILE : 2 * E + TILE + 1]) / 4096.0

    def project(direction, hat, norm):
        return (direction - jnp.sum(direction * hat, axis=1, keepdims=True) * hat) / norm

    group = (xh * 2 + c) * 2 + xl
    mine = jnp.broadcast_to(col_scr[pl.ds(group, 1), :], (8, TILE))
    here = iota((8, TILE), 1) == spot * 8 + iota((8, TILE), 0)
    mine = jnp.sum(jnp.where(here, mine, 0.0), axis=1, keepdims=True)
    text_dir = SCALE * (got[:, 0:E] + got[:, E : 2 * E] / mine)
    text_grad_ref[...] = project(text_dir, text_hat_ref[...], text_norm_ref[...])

    rows = own_ref[...]
    rowsum = jnp.sum(rows, axis=1, keepdims=True)
    target = target_ref[pl.ds(pl.multiple_of((xl * 32 + spot) * 8, 8), 8), :]
    lane = iota((8, TILE), 1).astype(f32)
    direction = jnp.zeros((8, E), f32)
    for k, ref in enumerate((set0_ref, set1_ref, set2_ref, set3_ref)):
        row = rows_of(xh, c, k)
        for t in range(2):
            tile = row * 2 + t
            at = k * SET + t * TILE
            ex = rows[:, at : at + TILE]
            hot = jnp.where(target == (tile * TILE).astype(f32) + lane, 2.0, 0.0)
            probe = ex / rowsum + ex / col_scr[pl.ds(tile, 1), :] - hot
            direction += dot(probe.astype(bf16), ref[t * TILE : (t + 1) * TILE, :])
    video_grad_ref[...] = project(SCALE * direction, video_hat_ref[...], video_norm_ref[...])


def gradients(*args):
    return pl.pallas_call(
        grad_kernel,
        in_specs=[VMEM] * 11,
        out_specs=[VMEM] * 3,
        out_shape=[
            jax.ShapeDtypeStruct((1, 1), f32),
            jax.ShapeDtypeStruct((8, E), f32),
            jax.ShapeDtypeStruct((8, E), f32),
        ],
        scratch_shapes=[pltpu.VMEM((8, TILE), f32)],
        compiler_params=pltpu.CompilerParams(vmem_limit_bytes=32 << 20),
        cost_estimate=pl.CostEstimate(
            flops=2 * 8 * 2048 * E, bytes_accessed=5 << 20, transcendentals=2048
        ),
    )(*args)


def exchange(x, axes):
    return lax.all_to_all(x, axes, 0, 0, tiled=True)


def swap(x):
    return lax.ppermute(x, "c", [(0, 1), (1, 0)])


def cross(x):
    return lax.ppermute(x, ("xh", "xl"), [(0, 3), (3, 0), (1, 2), (2, 1)])


def body(clip_tokens, clip_video, pool_vectors, out_proj, text_embed, pair_text):
    outgoing, text_hat, text_norm = clip_sums(
        clip_tokens, clip_video, pool_vectors, text_embed, pair_text
    )
    arrived = exchange(outgoing.reshape(CLIPS, 8, SENT + E), ROW)
    video_embed, video_hat, video_norm, send, texts, target = embed(
        arrived.reshape(CLIPS * 8, SENT + E), out_proj
    )
    crossed = cross(texts)
    videos, crossed = lax.optimization_barrier((exchange(send, PLANE), crossed))
    videos = videos.reshape(PLANE_ROWS, E)
    sets = (texts, swap(texts), crossed, swap(crossed))
    terms, own = all_logits(videos, target, *sets)
    loss, video_grad, text_grad = gradients(
        exchange(terms, GROUP), own, target, *sets, video_hat, video_norm, text_hat, text_norm
    )
    return video_embed, video_grad, text_grad, loss.reshape(())


def solution(mesh):
    split = Mesh(mesh.devices.reshape(2, 2, 2, 8, 4), ALL)
    return jax.shard_map(
        body,
        mesh=split,
        in_specs=(P(ALL, None, None), P(ALL), P(), P(), P(ALL, None), P(ALL)),
        out_specs=(P(ALL, None), P(ALL, None), P(ALL, None), P()),
        check_vma=False,
    )
```

```python
import jax
import jax.numpy as jnp
from jax import lax
from jax.experimental import pallas as pl
from jax.experimental.pallas import tpu as pltpu
from jax.sharding import Mesh, PartitionSpec as P

H = 25
HD = 128
D = 3200
E = 768
TOK = 16
CLIPS = 64
SOFT_CAP = 20.0
SCALE = 40.0
EPS = 1e-06
ALL = ("xh", "c", "xl", "z", "y")
ROW = ("xl", "z", "y")
PLANE = ("z", "y")
CHUNK = 32
TOKS = CHUNK * TOK
STEPS = CLIPS // CHUNK
PARTS = 4
WIDE = 7
SENT = WIDE * HD
TAIL = 4 * HD
TILE = 256
SET = 512
PLANE_ROWS = 256
SUMS = 2 * E + TILE + 128
VMEM = pl.BlockSpec(memory_space=pltpu.VMEM)
f32 = jnp.float32
bf16 = jnp.bfloat16
NT = (((1,), (1,)), ((), ()))
TN = (((0,), (0,)), ((), ()))


def dot(a, b, dims=(((1,), (0,)), ((), ()))):
    return lax.dot_general(a, b, dims, preferred_element_type=f32)


def iota(shape, dim):
    return lax.broadcasted_iota(jnp.int32, shape, dim)


def column_of(row):
    n = row.shape[1]
    eye = iota((n, n), 0) == iota((n, n), 1)
    return jnp.sum(jnp.where(eye, jnp.broadcast_to(row, (n, n)), 0.0), axis=1, keepdims=True)


def unit_rows(values):
    norms = jnp.sqrt(jnp.sum(values * values, axis=1, keepdims=True) + EPS)
    return values / norms, norms


def clip_kernel(
    video_hbm, token_hbm, pool_hbm, text_hbm, pair_hbm,
    out_ref, hat_ref, norm_ref,
    video_ref, token_ref, pool_ref, text_ref, pair_ref, weight_scr, num_scr, sems,
):
    small = ((pool_hbm, pool_ref), (video_hbm, video_ref), (text_hbm, text_ref), (pair_hbm, pair_ref))
    chunks = [pl.ds(i * TOKS, TOKS) for i in range(STEPS)]
    loads = [
        pltpu.make_async_copy(token_hbm.at[chunk], token_ref.at[chunk], sems.at[i])
        for i, chunk in enumerate(chunks)
    ]
    early = [
        pltpu.make_async_copy(src, dst, sems.at[STEPS + i]) for i, (src, dst) in enumerate(small)
    ]
    early[0].start()
    loads[0].start()
    for copy in early[1:] + loads[1:]:
        copy.start()
    weight_scr[...] = jnp.zeros_like(weight_scr)
    num_scr[...] = jnp.zeros_like(num_scr)
    mine = iota((CHUNK, TOKS), 1) // TOK == iota((CHUNK, TOKS), 0)
    ones = mine.astype(f32).astype(bf16)
    lane = iota((CHUNK, HD), 1)
    for copy in early[1:]:
        copy.wait()
    videos = video_ref[...].astype(f32)
    hat, norm = unit_rows(text_ref[...].astype(f32))
    hat_ref[...] = hat
    norm_ref[...] = norm
    texts = jnp.broadcast_to(hat[None], (CLIPS, 8, E)).reshape(CLIPS * 8, E)
    out_ref[:, SENT : SENT + E] = texts.astype(bf16)
    early[0].wait()
    pool = pool_ref[...]

    def put(step, j, value):
        at = j // WIDE * CLIPS + step * CHUNK
        num_scr[at : at + CHUNK, j % WIDE * HD : (j % WIDE + 1) * HD] = value.astype(bf16)

    def weigh(step):
        loads[step].wait()
        scores = dot(pool, token_ref[chunks[step], :], NT)
        weights = jnp.exp(SOFT_CAP * jnp.tanh(scores / SOFT_CAP))
        weight_scr[step, 0:H, :] = weights
        weight_scr[step, 32 : 32 + H, :] = weights

    def total(step):
        den = dot(ones, weight_scr[step].astype(bf16), NT)
        den_hi = den.astype(bf16).astype(f32)
        here = iota((CHUNK, CLIPS), 1) == iota((CHUNK, CLIPS), 0) + step * CHUNK
        video = jnp.where(here, jnp.broadcast_to(videos, (CHUNK, CLIPS)), 0.0)
        video = jnp.sum(video, axis=1, keepdims=True).astype(jnp.int32)
        local = jnp.where(lane - 64 == video % 8, 1.0, 0.0)
        tail = jnp.where(lane < 32, den_hi, jnp.where(lane < 64, den - den_hi, local))
        put(step, H, tail)
        for h in range(0, H, 2):
            pair = range(h, min(h + 2, H))
            lhs = jnp.concatenate(
                [
                    jnp.where(
                        mine, jnp.broadcast_to(weight_scr[step, k : k + 1, :], (CHUNK, TOKS)), 0.0
                    )
                    for k in pair
                ],
                axis=0,
            ).astype(bf16)
            part = dot(lhs, token_ref[chunks[step], h * HD : (h + len(pair)) * HD])
            for n, k in enumerate(pair):
                put(step, k, part[n * CHUNK : (n + 1) * CHUNK, n * HD : (n + 1) * HD])

    for step in range(STEPS):
        weigh(step)
        if step:
            total(step - 1)
    total(STEPS - 1)

    owner = (video_ref[...] // 8).astype(f32)
    before = (column_of(owner) == owner) & (iota((CLIPS, CLIPS), 0) < iota((CLIPS, CLIPS), 1))
    rank = jnp.sum(jnp.where(before, 1.0, 0.0), axis=0, keepdims=True)
    slot = owner * 2.0 + rank
    slots = jnp.concatenate([slot] * PARTS, axis=1).astype(jnp.int32)
    shape = (CLIPS * 8, PARTS * CLIPS)
    row, col = iota(shape, 0), iota(shape, 1)
    place = (row // PARTS == slots) & (row % PARTS == col // CLIPS)
    out = dot(jnp.where(place, 1.0, 0.0).astype(bf16), num_scr[...])
    pair = pair_ref[...]
    codes = jnp.concatenate(
        [
            jnp.zeros((1, 72), f32),
            (pair // 64).astype(f32),
            (pair % 64).astype(f32),
            jnp.zeros((1, 40), f32),
        ],
        axis=1,
    )
    last = iota((CLIPS * 8, HD), 0) % PARTS == PARTS - 1
    out_ref[:, 0:TAIL] = out[:, 0:TAIL].astype(bf16)
    out_ref[:, TAIL : TAIL + HD] = (
        out[:, TAIL : TAIL + HD] + jnp.where(last, codes, 0.0)
    ).astype(bf16)
    out_ref[:, TAIL + HD : SENT] = out[:, TAIL + HD : SENT].astype(bf16)


def clip_sums(clip_tokens, clip_video, pool_vectors, text_embed, pair_text):
    args = (
        clip_video.reshape(1, CLIPS),
        clip_tokens.reshape(CLIPS * TOK, D),
        pool_vectors,
        text_embed,
        pair_text.reshape(1, 8),
    )
    return pl.pallas_call(
        clip_kernel,
        in_specs=[pl.BlockSpec(memory_space=pltpu.HBM)] * 5,
        out_specs=[VMEM] * 3,
        out_shape=[
            jax.ShapeDtypeStruct((CLIPS * 8, SENT + E), bf16),
            jax.ShapeDtypeStruct((8, E), f32),
            jax.ShapeDtypeStruct((8, 1), f32),
        ],
        scratch_shapes=[pltpu.VMEM(x.shape, x.dtype) for x in args]
        + [
            pltpu.VMEM((STEPS, 128, TOKS), f32),
            pltpu.VMEM((PARTS * CLIPS, SENT), bf16),
            pltpu.SemaphoreType.DMA((STEPS + 4,)),
        ],
        compiler_params=pltpu.CompilerParams(vmem_limit_bytes=24 << 20),
        cost_estimate=pl.CostEstimate(
            flops=2 * 1024 * D * 64, bytes_accessed=8 << 20, transcendentals=1 << 17
        ),
    )(*(pltpu.with_memory_space_constraint(x, pltpu.HBM) for x in args))


def embed_kernel(
    arrived_ref, proj_ref, emb_ref, hat_ref, norm_ref, send_ref, text_ref, target_ref
):
    rows = CLIPS * 8
    text_ref[...] = arrived_ref[:, SENT : SENT + E]
    tails = arrived_ref[:, TAIL : TAIL + HD]
    pick = jnp.where(iota((8, HD), 1) - 64 == iota((8, HD), 0), 1.0, 0.0).astype(bf16)
    hot = dot(pick, tails, NT)
    hot = jnp.where(iota((8, rows), 1) % PARTS == PARTS - 1, hot, 0.0)
    assign = jnp.concatenate(
        [hot if p == PARTS - 1 else pltpu.roll(hot, rows - (PARTS - 1 - p), 1) for p in range(PARTS)],
        axis=0,
    )
    sums = dot(assign.astype(bf16), arrived_ref[:, 0:SENT])

    def chunk(j):
        p, q = j // WIDE, j % WIDE
        return sums[p * 8 : (p + 1) * 8, q * HD : (q + 1) * HD]

    den = chunk(H)
    den = den[:, 0:32] + den[:, 32:64]
    pooled = jnp.concatenate([chunk(h) / den[:, h : h + 1] for h in range(H)], axis=1)
    hi = pooled.astype(bf16).astype(f32)
    mid = (pooled - hi).astype(bf16).astype(f32)
    low = pooled - hi - mid
    parts = dot(jnp.concatenate([hi, mid, low], axis=0).astype(bf16), proj_ref[...])
    emb = parts[0:8] + parts[8:16] + parts[16:24]
    emb_ref[...] = emb.astype(bf16)
    hat, norm = unit_rows(emb)
    hat_ref[...] = hat
    norm_ref[...] = norm
    hat_low = hat.astype(bf16)
    for k in range(32):
        send_ref[k] = hat_low
    code = tails.astype(f32).reshape(CLIPS, 8, HD)[:, 3:4, :]
    code = jnp.broadcast_to(code, (CLIPS, 8, HD)).reshape(rows, HD)
    lane, own = iota((rows, HD), 1), iota((rows, HD), 0) % 8
    code = jnp.where(lane - 72 == own, 64.0 * code, jnp.where(lane - 80 == own, code, 0.0))
    target_ref[...] = jnp.sum(code, axis=1, keepdims=True)


def embed(arrived, out_proj):
    return pl.pallas_call(
        embed_kernel,
        in_specs=[VMEM, VMEM],
        out_specs=[VMEM] * 6,
        out_shape=[
            jax.ShapeDtypeStruct((8, E), bf16),
            jax.ShapeDtypeStruct((8, E), f32),
            jax.ShapeDtypeStruct((8, 1), f32),
            jax.ShapeDtypeStruct((32, 8, E), bf16),
            jax.ShapeDtypeStruct((SET, E), bf16),
            jax.ShapeDtypeStruct((SET, 1), f32),
        ],
        compiler_params=pltpu.CompilerParams(vmem_limit_bytes=24 << 20),
        cost_estimate=pl.CostEstimate(
            flops=2 * 24 * D * E, bytes_accessed=6 << 20, transcendentals=0
        ),
    )(arrived, out_proj)


def position():
    xh, c, xl, z, y = (lax.axis_index(a) for a in ALL)
    return xh, c, xl, z * 4 + y


def rows_of(xh, c, k):
    a, b = k // 2, k % 2
    return (xh + a - 2 * a * xh) * 2 + (c + b - 2 * b * c)


def score(videos, target, ref, row, own_ref, at, tile_scr, cols_ref, halves, positive, base):
    lane = iota((1, TILE), 1).astype(f32)
    for t in range(2):
        tile = row * 2 + t
        logits = SCALE * dot(videos, ref[t * TILE : (t + 1) * TILE, :], NT)
        ex = jnp.exp(logits)
        tile_scr[...] = ex
        cols_ref[pl.ds(tile, 1), :] = jnp.sum(ex, axis=0, keepdims=True)
        halves += ex[:, 0:128] + ex[:, 128:TILE]
        hit = target == (tile * TILE).astype(f32) + lane
        positive += jnp.sum(jnp.where(hit, logits, 0.0), axis=0, keepdims=True)
        own_ref[:, at + t * TILE : at + (t + 1) * TILE] = tile_scr[pl.ds(base, 8), :]
    return halves, positive


def plane_rows(target_ref, xl):
    return target_ref[pl.ds(pl.multiple_of(xl * PLANE_ROWS, PLANE_ROWS), PLANE_ROWS), :]


def first_kernel(
    video_ref, target_ref, set0_ref, set1_ref, set2_ref,
    own_ref, cols_ref, halves_ref, positive_ref, tile_scr,
):
    xh, c, xl, spot = position()
    target = plane_rows(target_ref, xl)
    videos = video_ref[...]
    base = pl.multiple_of(spot * 8, 8)
    cols_ref[...] = jnp.zeros_like(cols_ref)
    halves, positive = jnp.zeros((PLANE_ROWS, 128), f32), jnp.zeros((1, TILE), f32)
    for k, ref in enumerate((set0_ref, set1_ref, set2_ref)):
        halves, positive = score(
            videos, target, ref, rows_of(xh, c, k), own_ref, k * SET, tile_scr, cols_ref,
            halves, positive, base,
        )
    halves_ref[...] = halves
    positive_ref[...] = positive


def second_kernel(
    video_ref, target_ref, set0_ref, set1_ref, set2_ref, set3_ref, cols_ref, halves_ref, positive_ref,
    keep_ref, send_ref, own_ref, tile_scr, col_scr,
):
    xh, c, xl, spot = position()
    target = plane_rows(target_ref, xl)
    videos = video_ref[...]
    base = pl.multiple_of(spot * 8, 8)
    sets = (set0_ref, set1_ref, set2_ref, set3_ref)
    odd = spot % 2 == 1
    near, groups = [], []
    for k, ref in enumerate(sets):
        for half in range(2):
            at = pl.multiple_of(half * PLANE_ROWS + spot // 2 * 16, 16)
            pair = ref[pl.ds(at, 16), :].astype(f32)
            near.append(jnp.where(odd, pair[8:16], pair[0:8]))
            groups.append(rows_of(xh, c, k) * 2 + half)
    near = jnp.concatenate(near, axis=0).astype(bf16)
    near = jnp.exp(SCALE * dot(videos, near, NT))
    col_scr[...] = cols_ref[...]
    halves, positive = score(
        videos, target, set3_ref, rows_of(xh, c, 3), own_ref, 0, tile_scr, col_scr,
        halves_ref[...], positive_ref[...], base,
    )
    rowsum = jnp.sum(halves, axis=1, keepdims=True)
    total = jnp.sum(jnp.log(rowsum), axis=0, keepdims=True) - 2.0 * jnp.sum(
        positive, axis=1, keepdims=True
    )
    slot = iota((1, 64), 1)
    group = sum(jnp.where(slot // 8 == n, g, 0) for n, g in enumerate(groups))
    text = ((group * 32 + spot) * 8 + slot % 8).astype(f32)
    first = near / rowsum - jnp.where(target == text, 2.0, 0.0)
    first_hi = first.astype(bf16).astype(f32)
    near_hi = near.astype(bf16).astype(f32)
    terms = jnp.concatenate([first_hi, first - first_hi, near_hi, near - near_hi], axis=1)
    sums = dot(terms.astype(bf16), videos, TN)
    first, second = sums[0:64] + sums[64:128], sums[128:192] + sums[192:256]
    cols = col_scr[...]
    total = jnp.broadcast_to(total, (8, 128))
    for k in range(4):
        for half in range(2):
            n = k * 2 + half
            there = (xh + k // 2 - 2 * (k // 2) * xh) * 2 + half
            step = (there - (xh * 2 + xl) + 4) % 4
            out_ref = send_ref if k % 2 else keep_ref
            out_ref[step, :, 0:E] = first[n * 8 : (n + 1) * 8]
            out_ref[step, :, E : 2 * E] = second[n * 8 : (n + 1) * 8]
            out_ref[step, :, 2 * E : 2 * E + TILE] = cols
            out_ref[step, :, 2 * E + TILE :] = total


def first_logits(videos, target, *sets):
    return pl.pallas_call(
        first_kernel,
        in_specs=[VMEM] * 5,
        out_specs=[VMEM] * 4,
        out_shape=[
            jax.ShapeDtypeStruct((8, 3 * SET), f32),
            jax.ShapeDtypeStruct((8, TILE), f32),
            jax.ShapeDtypeStruct((PLANE_ROWS, 128), f32),
            jax.ShapeDtypeStruct((1, TILE), f32),
        ],
        scratch_shapes=[pltpu.VMEM((PLANE_ROWS, TILE), f32)],
        compiler_params=pltpu.CompilerParams(vmem_limit_bytes=24 << 20),
        cost_estimate=pl.CostEstimate(
            flops=2 * PLANE_ROWS * 1536 * E, bytes_accessed=3 << 20, transcendentals=3 << 17
        ),
    )(videos, target, *sets)


def second_logits(*args):
    return pl.pallas_call(
        second_kernel,
        in_specs=[VMEM] * 9,
        out_specs=[VMEM] * 3,
        out_shape=[
            jax.ShapeDtypeStruct((4, 8, SUMS), f32),
            jax.ShapeDtypeStruct((4, 8, SUMS), f32),
            jax.ShapeDtypeStruct((8, SET), f32),
        ],
        scratch_shapes=[pltpu.VMEM((PLANE_ROWS, TILE), f32), pltpu.VMEM((8, TILE), f32)],
        compiler_params=pltpu.CompilerParams(vmem_limit_bytes=24 << 20),
        cost_estimate=pl.CostEstimate(
            flops=2 * PLANE_ROWS * 1024 * E, bytes_accessed=3 << 20, transcendentals=1 << 17
        ),
    )(*args)


def add_kernel(keep_ref, got_ref, *out_refs):
    for k, out_ref in enumerate(out_refs):
        out_ref[...] = keep_ref[k] + got_ref[k]


def add_parts(keep, got):
    return pl.pallas_call(
        add_kernel,
        in_specs=[VMEM] * 2,
        out_specs=[VMEM] * 4,
        out_shape=[jax.ShapeDtypeStruct((8, SUMS), f32)] * 4,
        compiler_params=pltpu.CompilerParams(vmem_limit_bytes=16 << 20),
        cost_estimate=pl.CostEstimate(flops=1 << 16, bytes_accessed=1 << 19, transcendentals=0),
    )(keep, got)


def grad_kernel(
    part0_ref, part1_ref, part2_ref, part3_ref, own_ref, last_ref, target_ref,
    set0_ref, set1_ref, set2_ref, set3_ref, video_hat_ref, video_norm_ref,
    text_hat_ref, text_norm_ref, loss_ref, video_grad_ref, text_grad_ref, col_scr,
):
    xh, c, xl, spot = position()
    got = (part0_ref[...] + part1_ref[...]) + (part2_ref[...] + part3_ref[...])
    cols = got[:, 2 * E : 2 * E + TILE]
    col_scr[...] = cols
    logs = jnp.sum(jnp.sum(jnp.log(cols), axis=0, keepdims=True), axis=1, keepdims=True)
    loss_ref[...] = (logs + got[0:1, 2 * E + TILE : 2 * E + TILE + 1]) / 4096.0

    def project(direction, hat, norm):
        return (direction - jnp.sum(direction * hat, axis=1, keepdims=True) * hat) / norm

    group = (xh * 2 + c) * 2 + xl
    mine = jnp.broadcast_to(col_scr[pl.ds(group, 1), :], (8, TILE))
    here = iota((8, TILE), 1) == spot * 8 + iota((8, TILE), 0)
    mine = jnp.sum(jnp.where(here, mine, 0.0), axis=1, keepdims=True)
    text_dir = SCALE * (got[:, 0:E] + got[:, E : 2 * E] / mine)
    text_grad_ref[...] = project(text_dir, text_hat_ref[...], text_norm_ref[...])

    rows = jnp.concatenate([own_ref[...], last_ref[...]], axis=1)
    rowsum = jnp.sum(rows, axis=1, keepdims=True)
    target = target_ref[pl.ds(pl.multiple_of((xl * 32 + spot) * 8, 8), 8), :]
    lane = iota((8, TILE), 1).astype(f32)
    direction = jnp.zeros((8, E), f32)
    for k, ref in enumerate((set0_ref, set1_ref, set2_ref, set3_ref)):
        row = rows_of(xh, c, k)
        for t in range(2):
            tile = row * 2 + t
            at = k * SET + t * TILE
            ex = rows[:, at : at + TILE]
            hot = jnp.where(target == (tile * TILE).astype(f32) + lane, 2.0, 0.0)
            probe = ex / rowsum + ex / col_scr[pl.ds(tile, 1), :] - hot
            direction += dot(probe.astype(bf16), ref[t * TILE : (t + 1) * TILE, :])
    video_grad_ref[...] = project(SCALE * direction, video_hat_ref[...], video_norm_ref[...])


def gradients(*args):
    return pl.pallas_call(
        grad_kernel,
        in_specs=[VMEM] * 15,
        out_specs=[VMEM] * 3,
        out_shape=[
            jax.ShapeDtypeStruct((1, 1), f32),
            jax.ShapeDtypeStruct((8, E), f32),
            jax.ShapeDtypeStruct((8, E), f32),
        ],
        scratch_shapes=[pltpu.VMEM((8, TILE), f32)],
        compiler_params=pltpu.CompilerParams(vmem_limit_bytes=32 << 20),
        cost_estimate=pl.CostEstimate(
            flops=2 * 8 * 2048 * E, bytes_accessed=5 << 20, transcendentals=2048
        ),
    )(*args)


def exchange(x, axes):
    return lax.all_to_all(x, axes, 0, 0, tiled=True)


def swap(x):
    return lax.ppermute(x, "c", [(0, 1), (1, 0)])


def turn(x, step):
    return lax.ppermute(x, ("xh", "xl"), [(k, (k + step) % 4) for k in range(4)])


def cross(x):
    return lax.ppermute(x, ("xh", "xl"), [(0, 3), (3, 0), (1, 2), (2, 1)])


def body(clip_tokens, clip_video, pool_vectors, out_proj, text_embed, pair_text):
    outgoing, text_hat, text_norm = clip_sums(
        clip_tokens, clip_video, pool_vectors, text_embed, pair_text
    )
    arrived = exchange(outgoing.reshape(CLIPS, 8, SENT + E), ROW)
    video_embed, video_hat, video_norm, send, texts, target = embed(
        arrived.reshape(CLIPS * 8, SENT + E), out_proj
    )
    crossed = cross(texts)
    videos, crossed = lax.optimization_barrier((exchange(send, PLANE), crossed))
    videos = videos.reshape(PLANE_ROWS, E)
    sets = (texts, swap(texts), crossed, swap(crossed))
    own, cols, halves, positive = first_logits(videos, target, *sets[0:3])
    keep, send, last = second_logits(videos, target, *sets, cols, halves, positive)
    parts = add_parts(keep, swap(send))
    parts = [parts[0], turn(parts[1], 1), turn(parts[3], 3), turn(parts[2], 2)]
    loss, video_grad, text_grad = gradients(
        *parts, own, last, target, *sets, video_hat, video_norm, text_hat, text_norm
    )
    return video_embed, video_grad, text_grad, loss.reshape(())


def solution(mesh):
    split = Mesh(mesh.devices.reshape(2, 2, 2, 8, 4), ALL)
    return jax.shard_map(
        body,
        mesh=split,
        in_specs=(P(ALL, None, None), P(ALL), P(), P(), P(ALL, None), P(ALL)),
        out_specs=(P(ALL, None), P(ALL, None), P(ALL, None), P()),
        check_vma=False,
    )
```

```python
import jax
import jax.numpy as jnp
from jax import lax
from jax.experimental import pallas as pl
from jax.experimental.pallas import tpu as pltpu
from jax.sharding import Mesh, PartitionSpec as P

H = 25
HD = 128
D = 3200
E = 768
TOK = 16
CLIPS = 64
SOFT_CAP = 20.0
SCALE = 40.0
EPS = 1e-06
ALL = ("xh", "c", "xl", "z", "y")
ROW = ("xl", "z", "y")
PLANE = ("z", "y")
CHUNK = 32
TOKS = CHUNK * TOK
STEPS = CLIPS // CHUNK
PARTS = 4
WIDE = 7
SENT = WIDE * HD
TAIL = 4 * HD
TILE = 256
SET = 512
PLANE_ROWS = 256
SUMS = 2 * E + TILE + 128
PIECE = E // 2
VMEM = pl.BlockSpec(memory_space=pltpu.VMEM)
f32 = jnp.float32
bf16 = jnp.bfloat16
NT = (((1,), (1,)), ((), ()))
TN = (((0,), (0,)), ((), ()))


def dot(a, b, dims=(((1,), (0,)), ((), ()))):
    return lax.dot_general(a, b, dims, preferred_element_type=f32)


def iota(shape, dim):
    return lax.broadcasted_iota(jnp.int32, shape, dim)


def column_of(row):
    n = row.shape[1]
    eye = iota((n, n), 0) == iota((n, n), 1)
    return jnp.sum(jnp.where(eye, jnp.broadcast_to(row, (n, n)), 0.0), axis=1, keepdims=True)


def unit_rows(values):
    norms = jnp.sqrt(jnp.sum(values * values, axis=1, keepdims=True) + EPS)
    return values / norms, norms


def clip_kernel(
    video_hbm, token_hbm, pool_hbm, text_hbm, pair_hbm,
    out_ref, hat_ref, norm_ref,
    video_ref, token_ref, pool_ref, text_ref, pair_ref, weight_scr, num_scr, sems,
):
    small = ((pool_hbm, pool_ref), (video_hbm, video_ref), (text_hbm, text_ref), (pair_hbm, pair_ref))
    chunks = [pl.ds(i * TOKS, TOKS) for i in range(STEPS)]
    loads = [
        pltpu.make_async_copy(token_hbm.at[chunk], token_ref.at[chunk], sems.at[i])
        for i, chunk in enumerate(chunks)
    ]
    early = [
        pltpu.make_async_copy(src, dst, sems.at[STEPS + i]) for i, (src, dst) in enumerate(small)
    ]
    early[0].start()
    loads[0].start()
    for copy in early[1:] + loads[1:]:
        copy.start()
    weight_scr[...] = jnp.zeros_like(weight_scr)
    num_scr[...] = jnp.zeros_like(num_scr)
    mine = iota((CHUNK, TOKS), 1) // TOK == iota((CHUNK, TOKS), 0)
    ones = mine.astype(f32).astype(bf16)
    lane = iota((CHUNK, HD), 1)
    for copy in early[1:]:
        copy.wait()
    videos = video_ref[...].astype(f32)
    hat, norm = unit_rows(text_ref[...].astype(f32))
    hat_ref[...] = hat
    norm_ref[...] = norm
    for k in range(2):
        texts = hat[None, :, k * PIECE : (k + 1) * PIECE]
        texts = jnp.broadcast_to(texts, (CLIPS // 2, 8, PIECE)).reshape(CLIPS * 4, PIECE)
        out_ref[k * CLIPS * 4 : (k + 1) * CLIPS * 4, SENT : SENT + PIECE] = texts.astype(bf16)
    early[0].wait()
    pool = pool_ref[...]

    def put(step, j, value):
        at = j // WIDE * CLIPS + step * CHUNK
        num_scr[at : at + CHUNK, j % WIDE * HD : (j % WIDE + 1) * HD] = value.astype(bf16)

    def weigh(step):
        loads[step].wait()
        scores = dot(pool, token_ref[chunks[step], :], NT)
        weights = jnp.exp(SOFT_CAP * jnp.tanh(scores / SOFT_CAP))
        weight_scr[step, 0:H, :] = weights
        weight_scr[step, 32 : 32 + H, :] = weights

    def total(step):
        den = dot(ones, weight_scr[step].astype(bf16), NT)
        den_hi = den.astype(bf16).astype(f32)
        here = iota((CHUNK, CLIPS), 1) == iota((CHUNK, CLIPS), 0) + step * CHUNK
        video = jnp.where(here, jnp.broadcast_to(videos, (CHUNK, CLIPS)), 0.0)
        video = jnp.sum(video, axis=1, keepdims=True).astype(jnp.int32)
        local = jnp.where(lane - 64 == video % 8, 1.0, 0.0)
        tail = jnp.where(lane < 32, den_hi, jnp.where(lane < 64, den - den_hi, local))
        put(step, H, tail)
        for h in range(0, H, 2):
            pair = range(h, min(h + 2, H))
            lhs = jnp.concatenate(
                [
                    jnp.where(
                        mine, jnp.broadcast_to(weight_scr[step, k : k + 1, :], (CHUNK, TOKS)), 0.0
                    )
                    for k in pair
                ],
                axis=0,
            ).astype(bf16)
            part = dot(lhs, token_ref[chunks[step], h * HD : (h + len(pair)) * HD])
            for n, k in enumerate(pair):
                put(step, k, part[n * CHUNK : (n + 1) * CHUNK, n * HD : (n + 1) * HD])

    for step in range(STEPS):
        weigh(step)
        if step:
            total(step - 1)
    total(STEPS - 1)

    owner = (video_ref[...] // 8).astype(f32)
    before = (column_of(owner) == owner) & (iota((CLIPS, CLIPS), 0) < iota((CLIPS, CLIPS), 1))
    rank = jnp.sum(jnp.where(before, 1.0, 0.0), axis=0, keepdims=True)
    slot = owner * 2.0 + rank
    slots = jnp.concatenate([slot] * PARTS, axis=1).astype(jnp.int32)
    shape = (CLIPS * 8, PARTS * CLIPS)
    row, col = iota(shape, 0), iota(shape, 1)
    place = (row // PARTS == slots) & (row % PARTS == col // CLIPS)
    out = dot(jnp.where(place, 1.0, 0.0).astype(bf16), num_scr[...])
    pair = pair_ref[...]
    codes = jnp.concatenate(
        [
            jnp.zeros((1, 72), f32),
            (pair // 64).astype(f32),
            (pair % 64).astype(f32),
            jnp.zeros((1, 40), f32),
        ],
        axis=1,
    )
    last = iota((CLIPS * 8, HD), 0) % PARTS == PARTS - 1
    out_ref[:, 0:TAIL] = out[:, 0:TAIL].astype(bf16)
    out_ref[:, TAIL : TAIL + HD] = (
        out[:, TAIL : TAIL + HD] + jnp.where(last, codes, 0.0)
    ).astype(bf16)
    out_ref[:, TAIL + HD : SENT] = out[:, TAIL + HD : SENT].astype(bf16)


def clip_sums(clip_tokens, clip_video, pool_vectors, text_embed, pair_text):
    args = (
        clip_video.reshape(1, CLIPS),
        clip_tokens.reshape(CLIPS * TOK, D),
        pool_vectors,
        text_embed,
        pair_text.reshape(1, 8),
    )
    return pl.pallas_call(
        clip_kernel,
        in_specs=[pl.BlockSpec(memory_space=pltpu.HBM)] * 5,
        out_specs=[VMEM] * 3,
        out_shape=[
            jax.ShapeDtypeStruct((CLIPS * 8, SENT + PIECE), bf16),
            jax.ShapeDtypeStruct((8, E), f32),
            jax.ShapeDtypeStruct((8, 1), f32),
        ],
        scratch_shapes=[pltpu.VMEM(x.shape, x.dtype) for x in args]
        + [
            pltpu.VMEM((STEPS, 128, TOKS), f32),
            pltpu.VMEM((PARTS * CLIPS, SENT), bf16),
            pltpu.SemaphoreType.DMA((STEPS + 4,)),
        ],
        compiler_params=pltpu.CompilerParams(vmem_limit_bytes=24 << 20),
        cost_estimate=pl.CostEstimate(
            flops=2 * 1024 * D * 64, bytes_accessed=8 << 20, transcendentals=1 << 17
        ),
    )(*(pltpu.with_memory_space_constraint(x, pltpu.HBM) for x in args))


def embed_kernel(
    arrived_ref, proj_ref, emb_ref, hat_ref, norm_ref, send_ref, text_ref, target_ref
):
    rows = CLIPS * 8
    text_ref[...] = arrived_ref[:, SENT : SENT + PIECE]
    tails = arrived_ref[:, TAIL : TAIL + HD]
    pick = jnp.where(iota((8, HD), 1) - 64 == iota((8, HD), 0), 1.0, 0.0).astype(bf16)
    hot = dot(pick, tails, NT)
    hot = jnp.where(iota((8, rows), 1) % PARTS == PARTS - 1, hot, 0.0)
    assign = jnp.concatenate(
        [hot if p == PARTS - 1 else pltpu.roll(hot, rows - (PARTS - 1 - p), 1) for p in range(PARTS)],
        axis=0,
    )
    sums = dot(assign.astype(bf16), arrived_ref[:, 0:SENT])

    def chunk(j):
        p, q = j // WIDE, j % WIDE
        return sums[p * 8 : (p + 1) * 8, q * HD : (q + 1) * HD]

    den = chunk(H)
    den = den[:, 0:32] + den[:, 32:64]
    pooled = jnp.concatenate([chunk(h) / den[:, h : h + 1] for h in range(H)], axis=1)
    hi = pooled.astype(bf16).astype(f32)
    mid = (pooled - hi).astype(bf16).astype(f32)
    low = pooled - hi - mid
    parts = dot(jnp.concatenate([hi, mid, low], axis=0).astype(bf16), proj_ref[...])
    emb = parts[0:8] + parts[8:16] + parts[16:24]
    emb_ref[...] = emb.astype(bf16)
    hat, norm = unit_rows(emb)
    hat_ref[...] = hat
    norm_ref[...] = norm
    hat_low = hat.astype(bf16)
    for k in range(32):
        send_ref[k] = hat_low
    code = tails.astype(f32).reshape(CLIPS, 8, HD)[:, 3:4, :]
    code = jnp.broadcast_to(code, (CLIPS, 8, HD)).reshape(rows, HD)
    lane, own = iota((rows, HD), 1), iota((rows, HD), 0) % 8
    code = jnp.where(lane - 72 == own, 64.0 * code, jnp.where(lane - 80 == own, code, 0.0))
    target_ref[...] = jnp.sum(code, axis=1, keepdims=True)


def embed(arrived, out_proj):
    return pl.pallas_call(
        embed_kernel,
        in_specs=[VMEM, VMEM],
        out_specs=[VMEM] * 6,
        out_shape=[
            jax.ShapeDtypeStruct((8, E), bf16),
            jax.ShapeDtypeStruct((8, E), f32),
            jax.ShapeDtypeStruct((8, 1), f32),
            jax.ShapeDtypeStruct((32, 8, E), bf16),
            jax.ShapeDtypeStruct((SET, PIECE), bf16),
            jax.ShapeDtypeStruct((SET, 1), f32),
        ],
        compiler_params=pltpu.CompilerParams(vmem_limit_bytes=24 << 20),
        cost_estimate=pl.CostEstimate(
            flops=2 * 24 * D * E, bytes_accessed=6 << 20, transcendentals=0
        ),
    )(arrived, out_proj)


def position():
    xh, c, xl, z, y = (lax.axis_index(a) for a in ALL)
    return xh, c, xl, z * 4 + y


def other(a, flip):
    return a + flip - 2 * flip * a


def row_of(xh, c, k):
    return other(xh, k // 2) * 2 + other(c, k % 2)


def halves_of(ref, xl):
    return (
        ref[:, pl.ds(pl.multiple_of(xl * PIECE, 128), PIECE)],
        ref[:, pl.ds(pl.multiple_of((1 - xl) * PIECE, 128), PIECE)],
    )


def score(videos, target, pieces, row, own_ref, at, tile_scr, cols_ref, sums, positive, base):
    lane = iota((1, TILE), 1).astype(f32)
    for t in range(2):
        tile = row * 2 + t
        rows = slice(t * TILE, (t + 1) * TILE)
        logits = SCALE * (
            dot(videos[0], pieces[0][rows, :], NT) + dot(videos[1], pieces[1][rows, :], NT)
        )
        ex = jnp.exp(logits)
        tile_scr[...] = ex
        cols_ref[pl.ds(tile, 1), :] = jnp.sum(ex, axis=0, keepdims=True)
        sums += ex[:, 0:128] + ex[:, 128:TILE]
        hit = target == (tile * TILE).astype(f32) + lane
        positive += jnp.sum(jnp.where(hit, logits, 0.0), axis=0, keepdims=True)
        own_ref[:, at + t * TILE : at + (t + 1) * TILE] = tile_scr[pl.ds(base, 8), :]
    return sums, positive


def plane_rows(target_ref, xl):
    return target_ref[pl.ds(pl.multiple_of(xl * PLANE_ROWS, PLANE_ROWS), PLANE_ROWS), :]


def first_kernel(
    video_ref, target_ref, set0_ref, set0b_ref, set2_ref, set2b_ref,
    own_ref, cols_ref, sums_ref, positive_ref, tile_scr,
):
    xh, c, xl, spot = position()
    target = plane_rows(target_ref, xl)
    videos = halves_of(video_ref, xl)
    base = pl.multiple_of(spot * 8, 8)
    cols_ref[...] = jnp.zeros_like(cols_ref)
    sums, positive = jnp.zeros((PLANE_ROWS, 128), f32), jnp.zeros((1, TILE), f32)
    for n, pieces in enumerate(((set0_ref, set0b_ref), (set2_ref, set2b_ref))):
        sums, positive = score(
            videos, target, pieces, row_of(xh, c, 2 * n), own_ref, n * SET, tile_scr, cols_ref,
            sums, positive, base,
        )
    sums_ref[...] = sums
    positive_ref[...] = positive


def second_kernel(
    video_ref, target_ref, set0_ref, set0b_ref, set2_ref, set2b_ref, set1_ref, set1b_ref, set3_ref,
    set3b_ref, cols_ref, sums_ref, positive_ref,
    keep_ref, send_ref, own_ref, tile_scr, col_scr,
):
    xh, c, xl, spot = position()
    target = plane_rows(target_ref, xl)
    videos = halves_of(video_ref, xl)
    base = pl.multiple_of(spot * 8, 8)
    sets = (
        (set0_ref, set0b_ref), (set1_ref, set1b_ref), (set2_ref, set2b_ref), (set3_ref, set3b_ref)
    )
    col_scr[...] = cols_ref[...]
    sums, positive = sums_ref[...], positive_ref[...]
    for n, k in enumerate((1, 3)):
        sums, positive = score(
            videos, target, sets[k], row_of(xh, c, k), own_ref, n * SET, tile_scr, col_scr,
            sums, positive, base,
        )
    odd = spot % 2 == 1
    logits, groups = 0.0, []
    for part in range(2):
        near = []
        for k in range(4):
            for half in range(2):
                at = pl.multiple_of(half * PLANE_ROWS + spot // 2 * 16, 16)
                pair = sets[k][part][pl.ds(at, 16), :].astype(f32)
                near.append(jnp.where(odd, pair[8:16], pair[0:8]))
        near = jnp.concatenate(near, axis=0).astype(bf16)
        logits += dot(videos[part], near, NT)
    near = jnp.exp(SCALE * logits)
    rowsum = jnp.sum(sums, axis=1, keepdims=True)
    total = jnp.sum(jnp.log(rowsum), axis=0, keepdims=True) - 2.0 * jnp.sum(
        positive, axis=1, keepdims=True
    )
    slot = iota((1, 64), 1)
    group = sum(
        jnp.where(slot // 8 == n, row_of(xh, c, n // 2) * 2 + n % 2, 0) for n in range(8)
    )
    text = ((group * 32 + spot) * 8 + slot % 8).astype(f32)
    first = near / rowsum - jnp.where(target == text, 2.0, 0.0)
    first_hi = first.astype(bf16).astype(f32)
    near_hi = near.astype(bf16).astype(f32)
    terms = jnp.concatenate([first_hi, first - first_hi, near_hi, near - near_hi], axis=1)
    sums = dot(terms.astype(bf16), video_ref[...], TN)
    first, second = sums[0:64] + sums[64:128], sums[128:192] + sums[192:256]
    cols = col_scr[...]
    total = jnp.broadcast_to(total, (8, 128))
    for k in range(4):
        for half in range(2):
            n = k * 2 + half
            step = k // 2 * 2 + other(xl, half)
            out_ref = send_ref if k % 2 else keep_ref
            out_ref[step, :, 0:E] = first[n * 8 : (n + 1) * 8]
            out_ref[step, :, E : 2 * E] = second[n * 8 : (n + 1) * 8]
            out_ref[step, :, 2 * E : 2 * E + TILE] = cols
            out_ref[step, :, 2 * E + TILE :] = total


def first_logits(*args):
    return pl.pallas_call(
        first_kernel,
        in_specs=[VMEM] * 6,
        out_specs=[VMEM] * 4,
        out_shape=[
            jax.ShapeDtypeStruct((8, 2 * SET), f32),
            jax.ShapeDtypeStruct((8, TILE), f32),
            jax.ShapeDtypeStruct((PLANE_ROWS, 128), f32),
            jax.ShapeDtypeStruct((1, TILE), f32),
        ],
        scratch_shapes=[pltpu.VMEM((PLANE_ROWS, TILE), f32)],
        compiler_params=pltpu.CompilerParams(vmem_limit_bytes=24 << 20),
        cost_estimate=pl.CostEstimate(
            flops=2 * PLANE_ROWS * 1024 * E, bytes_accessed=2 << 20, transcendentals=1 << 18
        ),
    )(*args)


def second_logits(*args):
    return pl.pallas_call(
        second_kernel,
        in_specs=[VMEM] * 13,
        out_specs=[VMEM] * 3,
        out_shape=[
            jax.ShapeDtypeStruct((4, 8, SUMS), f32),
            jax.ShapeDtypeStruct((4, 8, SUMS), f32),
            jax.ShapeDtypeStruct((8, 2 * SET), f32),
        ],
        scratch_shapes=[pltpu.VMEM((PLANE_ROWS, TILE), f32), pltpu.VMEM((8, TILE), f32)],
        compiler_params=pltpu.CompilerParams(vmem_limit_bytes=24 << 20),
        cost_estimate=pl.CostEstimate(
            flops=2 * PLANE_ROWS * 1536 * E, bytes_accessed=4 << 20, transcendentals=1 << 18
        ),
    )(*args)


def add_kernel(keep_ref, got_ref, *out_refs):
    for k, out_ref in enumerate(out_refs):
        out_ref[...] = keep_ref[k] + got_ref[k]


def add_parts(keep, got):
    return pl.pallas_call(
        add_kernel,
        in_specs=[VMEM] * 2,
        out_specs=[VMEM] * 4,
        out_shape=[jax.ShapeDtypeStruct((8, SUMS), f32)] * 4,
        compiler_params=pltpu.CompilerParams(vmem_limit_bytes=16 << 20),
        cost_estimate=pl.CostEstimate(flops=1 << 16, bytes_accessed=1 << 19, transcendentals=0),
    )(keep, got)


def grad_kernel(
    part0_ref, part1_ref, part2_ref, part3_ref, own_ref, last_ref, target_ref,
    set0_ref, set0b_ref, set2_ref, set2b_ref, set1_ref, set1b_ref, set3_ref, set3b_ref,
    video_hat_ref, video_norm_ref, text_hat_ref, text_norm_ref, loss_ref, video_grad_ref, text_grad_ref, col_scr,
):
    xh, c, xl, spot = position()
    got = (part0_ref[...] + part1_ref[...]) + (part2_ref[...] + part3_ref[...])
    cols = got[:, 2 * E : 2 * E + TILE]
    col_scr[...] = cols
    logs = jnp.sum(jnp.sum(jnp.log(cols), axis=0, keepdims=True), axis=1, keepdims=True)
    loss_ref[...] = (logs + got[0:1, 2 * E + TILE : 2 * E + TILE + 1]) / 4096.0

    def project(direction, hat, norm):
        return (direction - jnp.sum(direction * hat, axis=1, keepdims=True) * hat) / norm

    group = (xh * 2 + c) * 2 + xl
    mine = jnp.broadcast_to(col_scr[pl.ds(group, 1), :], (8, TILE))
    here = iota((8, TILE), 1) == spot * 8 + iota((8, TILE), 0)
    mine = jnp.sum(jnp.where(here, mine, 0.0), axis=1, keepdims=True)
    text_dir = SCALE * (got[:, 0:E] + got[:, E : 2 * E] / mine)
    text_grad_ref[...] = project(text_dir, text_hat_ref[...], text_norm_ref[...])

    rows = jnp.concatenate([own_ref[...], last_ref[...]], axis=1)
    rowsum = jnp.sum(rows, axis=1, keepdims=True)
    target = target_ref[pl.ds(pl.multiple_of((xl * 32 + spot) * 8, 8), 8), :]
    lane = iota((8, TILE), 1).astype(f32)
    direction = [jnp.zeros((8, PIECE), f32)] * 2
    sets = ((set0_ref, set0b_ref), (set2_ref, set2b_ref), (set1_ref, set1b_ref), (set3_ref, set3b_ref))
    for n, k in enumerate((0, 2, 1, 3)):
        row = row_of(xh, c, k)
        for t in range(2):
            tile = row * 2 + t
            at = n * SET + t * TILE
            ex = rows[:, at : at + TILE]
            hot = jnp.where(target == (tile * TILE).astype(f32) + lane, 2.0, 0.0)
            probe = ex / rowsum + ex / col_scr[pl.ds(tile, 1), :] - hot
            probe = probe.astype(bf16)
            direction = [
                total + dot(probe, ref[t * TILE : (t + 1) * TILE, :])
                for total, ref in zip(direction, sets[n])
            ]
    low = xl == 0
    direction = jnp.concatenate(
        [
            jnp.where(low, direction[0], direction[1]),
            jnp.where(low, direction[1], direction[0]),
        ],
        axis=1,
    )
    video_grad_ref[...] = project(SCALE * direction, video_hat_ref[...], video_norm_ref[...])


def gradients(*args):
    return pl.pallas_call(
        grad_kernel,
        in_specs=[VMEM] * 19,
        out_specs=[VMEM] * 3,
        out_shape=[
            jax.ShapeDtypeStruct((1, 1), f32),
            jax.ShapeDtypeStruct((8, E), f32),
            jax.ShapeDtypeStruct((8, E), f32),
        ],
        scratch_shapes=[pltpu.VMEM((8, TILE), f32)],
        compiler_params=pltpu.CompilerParams(vmem_limit_bytes=32 << 20),
        cost_estimate=pl.CostEstimate(
            flops=2 * 8 * 2048 * E, bytes_accessed=5 << 20, transcendentals=2048
        ),
    )(*args)


def exchange(x, axes):
    return lax.all_to_all(x, axes, 0, 0, tiled=True)


def swap(x):
    return lax.ppermute(x, "c", [(0, 1), (1, 0)])


def along(x, step):
    return lax.ppermute(x, ("xh", "xl"), [(k, k ^ step) for k in range(4)])


def body(clip_tokens, clip_video, pool_vectors, out_proj, text_embed, pair_text):
    outgoing, text_hat, text_norm = clip_sums(
        clip_tokens, clip_video, pool_vectors, text_embed, pair_text
    )
    arrived = exchange(outgoing.reshape(CLIPS, 8, SENT + PIECE), ROW)
    video_embed, video_hat, video_norm, send, texts, target = embed(
        arrived.reshape(CLIPS * 8, SENT + PIECE), out_proj
    )
    moved = [along(texts, step) for step in (2, 3, 1)]
    videos, *moved = lax.optimization_barrier((exchange(send, PLANE), *moved))
    videos = videos.reshape(PLANE_ROWS, E)
    mine = (texts, moved[2], moved[0], moved[1])
    theirs = tuple(swap(x) for x in mine)
    own, cols, sums, positive = first_logits(videos, target, *mine)
    keep, send, last = second_logits(videos, target, *mine, *theirs, cols, sums, positive)
    parts = add_parts(keep, swap(send))
    parts = [parts[0]] + [along(parts[step], step) for step in (2, 3, 1)]
    loss, video_grad, text_grad = gradients(
        *parts, own, last, target, *mine, *theirs, video_hat, video_norm, text_hat, text_norm
    )
    return video_embed, video_grad, text_grad, loss.reshape(())


def solution(mesh):
    split = Mesh(mesh.devices.reshape(2, 2, 2, 8, 4), ALL)
    return jax.shard_map(
        body,
        mesh=split,
        in_specs=(P(ALL, None, None), P(ALL), P(), P(), P(ALL, None), P(ALL)),
        out_specs=(P(ALL, None), P(ALL, None), P(ALL, None), P()),
        check_vma=False,
    )
```

```python
import jax
import jax.numpy as jnp
from jax import lax
from jax.experimental import pallas as pl
from jax.experimental.pallas import tpu as pltpu
from jax.sharding import Mesh, PartitionSpec as P

H = 25
HD = 128
D = 3200
E = 768
TOK = 16
CLIPS = 64
SOFT_CAP = 20.0
SCALE = 40.0
EPS = 1e-06
ALL = ("xh", "c", "xl", "z", "y")
ROW = ("xl", "z", "y")
PLANE = ("z", "y")
CHUNK = 32
TOKS = CHUNK * TOK
STEPS = CLIPS // CHUNK
PARTS = 4
WIDE = 7
SENT = WIDE * HD
TAIL = 4 * HD
TILE = 256
SET = 512
PLANE_ROWS = 256
SUMS = 2 * E + TILE + 128
PIECE = E // 2
VMEM = pl.BlockSpec(memory_space=pltpu.VMEM)
f32 = jnp.float32
bf16 = jnp.bfloat16
NT = (((1,), (1,)), ((), ()))
TN = (((0,), (0,)), ((), ()))


def dot(a, b, dims=(((1,), (0,)), ((), ()))):
    return lax.dot_general(a, b, dims, preferred_element_type=f32)


def iota(shape, dim):
    return lax.broadcasted_iota(jnp.int32, shape, dim)


def column_of(row):
    n = row.shape[1]
    eye = iota((n, n), 0) == iota((n, n), 1)
    return jnp.sum(jnp.where(eye, jnp.broadcast_to(row, (n, n)), 0.0), axis=1, keepdims=True)


def unit_rows(values):
    norms = jnp.sqrt(jnp.sum(values * values, axis=1, keepdims=True) + EPS)
    return values / norms, norms


def clip_kernel(
    video_hbm, token_hbm, pool_hbm, text_hbm, pair_hbm,
    out_ref, hat_ref, norm_ref,
    video_ref, token_ref, pool_ref, text_ref, pair_ref, weight_scr, num_scr, sems,
):
    small = ((pool_hbm, pool_ref), (video_hbm, video_ref), (text_hbm, text_ref), (pair_hbm, pair_ref))
    chunks = [pl.ds(i * TOKS, TOKS) for i in range(STEPS)]
    loads = [
        pltpu.make_async_copy(token_hbm.at[chunk], token_ref.at[chunk], sems.at[i])
        for i, chunk in enumerate(chunks)
    ]
    early = [
        pltpu.make_async_copy(src, dst, sems.at[STEPS + i]) for i, (src, dst) in enumerate(small)
    ]
    early[0].start()
    loads[0].start()
    for copy in early[1:] + loads[1:]:
        copy.start()
    weight_scr[...] = jnp.zeros_like(weight_scr)
    num_scr[...] = jnp.zeros_like(num_scr)
    mine = iota((CHUNK, TOKS), 1) // TOK == iota((CHUNK, TOKS), 0)
    ones = mine.astype(f32).astype(bf16)
    lane = iota((CHUNK, HD), 1)
    for copy in early[1:]:
        copy.wait()
    videos = video_ref[...].astype(f32)
    hat, norm = unit_rows(text_ref[...].astype(f32))
    hat_ref[...] = hat
    norm_ref[...] = norm
    for k in range(2):
        texts = hat[None, :, k * PIECE : (k + 1) * PIECE]
        texts = jnp.broadcast_to(texts, (CLIPS // 2, 8, PIECE)).reshape(CLIPS * 4, PIECE)
        out_ref[k * CLIPS * 4 : (k + 1) * CLIPS * 4, SENT : SENT + PIECE] = texts.astype(bf16)
    early[0].wait()
    pool = pool_ref[...]

    def put(step, j, value):
        at = j // WIDE * CLIPS + step * CHUNK
        num_scr[at : at + CHUNK, j % WIDE * HD : (j % WIDE + 1) * HD] = value.astype(bf16)

    def weigh(step):
        loads[step].wait()
        scores = dot(pool, token_ref[chunks[step], :], NT)
        weights = jnp.exp(SOFT_CAP * jnp.tanh(scores / SOFT_CAP))
        weight_scr[step, 0:H, :] = weights
        weight_scr[step, 32 : 32 + H, :] = weights

    def total(step):
        den = dot(ones, weight_scr[step].astype(bf16), NT)
        den_hi = den.astype(bf16).astype(f32)
        here = iota((CHUNK, CLIPS), 1) == iota((CHUNK, CLIPS), 0) + step * CHUNK
        video = jnp.where(here, jnp.broadcast_to(videos, (CHUNK, CLIPS)), 0.0)
        video = jnp.sum(video, axis=1, keepdims=True).astype(jnp.int32)
        local = jnp.where(lane - 64 == video % 8, 1.0, 0.0)
        tail = jnp.where(lane < 32, den_hi, jnp.where(lane < 64, den - den_hi, local))
        put(step, H, tail)
        for h in range(0, H, 2):
            pair = range(h, min(h + 2, H))
            lhs = jnp.concatenate(
                [
                    jnp.where(
                        mine, jnp.broadcast_to(weight_scr[step, k : k + 1, :], (CHUNK, TOKS)), 0.0
                    )
                    for k in pair
                ],
                axis=0,
            ).astype(bf16)
            part = dot(lhs, token_ref[chunks[step], h * HD : (h + len(pair)) * HD])
            for n, k in enumerate(pair):
                put(step, k, part[n * CHUNK : (n + 1) * CHUNK, n * HD : (n + 1) * HD])

    for step in range(STEPS):
        weigh(step)
        if step:
            total(step - 1)
    total(STEPS - 1)

    owner = (video_ref[...] // 8).astype(f32)
    before = (column_of(owner) == owner) & (iota((CLIPS, CLIPS), 0) < iota((CLIPS, CLIPS), 1))
    rank = jnp.sum(jnp.where(before, 1.0, 0.0), axis=0, keepdims=True)
    slot = owner * 2.0 + rank
    slots = jnp.concatenate([slot] * PARTS, axis=1).astype(jnp.int32)
    shape = (CLIPS * 8, PARTS * CLIPS)
    row, col = iota(shape, 0), iota(shape, 1)
    place = (row // PARTS == slots) & (row % PARTS == col // CLIPS)
    out = dot(jnp.where(place, 1.0, 0.0).astype(bf16), num_scr[...])
    pair = pair_ref[...]
    codes = jnp.concatenate(
        [
            jnp.zeros((1, 72), f32),
            (pair // 64).astype(f32),
            (pair % 64).astype(f32),
            jnp.zeros((1, 40), f32),
        ],
        axis=1,
    )
    last = iota((CLIPS * 8, HD), 0) % PARTS == PARTS - 1
    out_ref[:, 0:TAIL] = out[:, 0:TAIL].astype(bf16)
    out_ref[:, TAIL : TAIL + HD] = (
        out[:, TAIL : TAIL + HD] + jnp.where(last, codes, 0.0)
    ).astype(bf16)
    out_ref[:, TAIL + HD : SENT] = out[:, TAIL + HD : SENT].astype(bf16)


def clip_sums(clip_tokens, clip_video, pool_vectors, text_embed, pair_text):
    args = (
        clip_video.reshape(1, CLIPS),
        clip_tokens.reshape(CLIPS * TOK, D),
        pool_vectors,
        text_embed,
        pair_text.reshape(1, 8),
    )
    return pl.pallas_call(
        clip_kernel,
        in_specs=[pl.BlockSpec(memory_space=pltpu.HBM)] * 5,
        out_specs=[VMEM] * 3,
        out_shape=[
            jax.ShapeDtypeStruct((CLIPS * 8, SENT + PIECE), bf16),
            jax.ShapeDtypeStruct((8, E), f32),
            jax.ShapeDtypeStruct((8, 1), f32),
        ],
        scratch_shapes=[pltpu.VMEM(x.shape, x.dtype) for x in args]
        + [
            pltpu.VMEM((STEPS, 128, TOKS), f32),
            pltpu.VMEM((PARTS * CLIPS, SENT), bf16),
            pltpu.SemaphoreType.DMA((STEPS + 4,)),
        ],
        compiler_params=pltpu.CompilerParams(vmem_limit_bytes=24 << 20),
        cost_estimate=pl.CostEstimate(
            flops=2 * 1024 * D * 64, bytes_accessed=8 << 20, transcendentals=1 << 17
        ),
    )(*(pltpu.with_memory_space_constraint(x, pltpu.HBM) for x in args))


def embed_kernel(
    arrived_ref, proj_ref, emb_ref, hat_ref, norm_ref, send_ref, target_ref
):
    rows = CLIPS * 8
    tails = arrived_ref[:, TAIL : TAIL + HD]
    pick = jnp.where(iota((8, HD), 1) - 64 == iota((8, HD), 0), 1.0, 0.0).astype(bf16)
    hot = dot(pick, tails, NT)
    hot = jnp.where(iota((8, rows), 1) % PARTS == PARTS - 1, hot, 0.0)
    assign = jnp.concatenate(
        [hot if p == PARTS - 1 else pltpu.roll(hot, rows - (PARTS - 1 - p), 1) for p in range(PARTS)],
        axis=0,
    )
    sums = dot(assign.astype(bf16), arrived_ref[:, 0:SENT])

    def chunk(j):
        p, q = j // WIDE, j % WIDE
        return sums[p * 8 : (p + 1) * 8, q * HD : (q + 1) * HD]

    den = chunk(H)
    den = den[:, 0:32] + den[:, 32:64]
    pooled = jnp.concatenate([chunk(h) / den[:, h : h + 1] for h in range(H)], axis=1)
    hi = pooled.astype(bf16).astype(f32)
    mid = (pooled - hi).astype(bf16).astype(f32)
    low = pooled - hi - mid
    parts = dot(jnp.concatenate([hi, mid, low], axis=0).astype(bf16), proj_ref[...])
    emb = parts[0:8] + parts[8:16] + parts[16:24]
    emb_ref[...] = emb.astype(bf16)
    hat, norm = unit_rows(emb)
    hat_ref[...] = hat
    norm_ref[...] = norm
    hat_low = hat.astype(bf16)
    for k in range(32):
        send_ref[k] = hat_low
    code = tails.astype(f32).reshape(CLIPS, 8, HD)[:, 3:4, :]
    code = jnp.broadcast_to(code, (CLIPS, 8, HD)).reshape(rows, HD)
    lane, own = iota((rows, HD), 1), iota((rows, HD), 0) % 8
    code = jnp.where(lane - 72 == own, 64.0 * code, jnp.where(lane - 80 == own, code, 0.0))
    target_ref[...] = jnp.sum(code, axis=1, keepdims=True)


def embed(arrived, out_proj):
    return pl.pallas_call(
        embed_kernel,
        in_specs=[VMEM, VMEM],
        out_specs=[VMEM] * 5,
        out_shape=[
            jax.ShapeDtypeStruct((8, E), bf16),
            jax.ShapeDtypeStruct((8, E), f32),
            jax.ShapeDtypeStruct((8, 1), f32),
            jax.ShapeDtypeStruct((32, 8, E), bf16),
            jax.ShapeDtypeStruct((SET, 1), f32),
        ],
        compiler_params=pltpu.CompilerParams(vmem_limit_bytes=24 << 20),
        cost_estimate=pl.CostEstimate(
            flops=2 * 24 * D * E, bytes_accessed=6 << 20, transcendentals=0
        ),
    )(arrived, out_proj)


def text_kernel(arrived_ref, text_ref):
    text_ref[...] = arrived_ref[:, SENT : SENT + PIECE]


def text_piece(arrived):
    return pl.pallas_call(
        text_kernel,
        in_specs=[VMEM],
        out_specs=VMEM,
        out_shape=jax.ShapeDtypeStruct((SET, PIECE), bf16),
        compiler_params=pltpu.CompilerParams(vmem_limit_bytes=16 << 20),
        cost_estimate=pl.CostEstimate(flops=0, bytes_accessed=1 << 20, transcendentals=0),
    )(arrived)


def position():
    xh, c, xl, z, y = (lax.axis_index(a) for a in ALL)
    return xh, c, xl, z * 4 + y


def other(a, flip):
    return a + flip - 2 * flip * a


def row_of(xh, c, k):
    return other(xh, k // 2) * 2 + other(c, k % 2)


def halves_of(ref, xl):
    return (
        ref[:, pl.ds(pl.multiple_of(xl * PIECE, 128), PIECE)],
        ref[:, pl.ds(pl.multiple_of((1 - xl) * PIECE, 128), PIECE)],
    )


def score(videos, target, pieces, row, own_ref, at, tile_scr, cols_ref, sums, positive, base):
    lane = iota((1, TILE), 1).astype(f32)
    for t in range(2):
        tile = row * 2 + t
        rows = slice(t * TILE, (t + 1) * TILE)
        logits = SCALE * (
            dot(videos[0], pieces[0][rows, :], NT) + dot(videos[1], pieces[1][rows, :], NT)
        )
        ex = jnp.exp(logits)
        tile_scr[...] = ex
        cols_ref[pl.ds(tile, 1), :] = jnp.sum(ex, axis=0, keepdims=True)
        sums += ex[:, 0:128] + ex[:, 128:TILE]
        hit = target == (tile * TILE).astype(f32) + lane
        positive += jnp.sum(jnp.where(hit, logits, 0.0), axis=0, keepdims=True)
        own_ref[:, at + t * TILE : at + (t + 1) * TILE] = tile_scr[pl.ds(base, 8), :]
    return sums, positive


def plane_rows(target_ref, xl):
    return target_ref[pl.ds(pl.multiple_of(xl * PLANE_ROWS, PLANE_ROWS), PLANE_ROWS), :]


def first_kernel(
    video_ref, target_ref, set0_ref, set0b_ref, set2_ref, set2b_ref,
    own_ref, cols_ref, sums_ref, positive_ref, tile_scr,
):
    xh, c, xl, spot = position()
    target = plane_rows(target_ref, xl)
    videos = halves_of(video_ref, xl)
    base = pl.multiple_of(spot * 8, 8)
    cols_ref[...] = jnp.zeros_like(cols_ref)
    sums, positive = jnp.zeros((PLANE_ROWS, 128), f32), jnp.zeros((1, TILE), f32)
    for n, pieces in enumerate(((set0_ref, set0b_ref), (set2_ref, set2b_ref))):
        sums, positive = score(
            videos, target, pieces, row_of(xh, c, 2 * n), own_ref, n * SET, tile_scr, cols_ref,
            sums, positive, base,
        )
    sums_ref[...] = sums
    positive_ref[...] = positive


def second_kernel(
    video_ref, target_ref, set0_ref, set0b_ref, set2_ref, set2b_ref, set1_ref, set1b_ref, set3_ref,
    set3b_ref, cols_ref, sums_ref, positive_ref,
    keep_ref, send_ref, own_ref, tile_scr, col_scr,
):
    xh, c, xl, spot = position()
    target = plane_rows(target_ref, xl)
    videos = halves_of(video_ref, xl)
    base = pl.multiple_of(spot * 8, 8)
    sets = (
        (set0_ref, set0b_ref), (set1_ref, set1b_ref), (set2_ref, set2b_ref), (set3_ref, set3b_ref)
    )
    col_scr[...] = cols_ref[...]
    sums, positive = sums_ref[...], positive_ref[...]
    for n, k in enumerate((1, 3)):
        sums, positive = score(
            videos, target, sets[k], row_of(xh, c, k), own_ref, n * SET, tile_scr, col_scr,
            sums, positive, base,
        )
    odd = spot % 2 == 1
    logits, groups = 0.0, []
    for part in range(2):
        near = []
        for k in range(4):
            for half in range(2):
                at = pl.multiple_of(half * PLANE_ROWS + spot // 2 * 16, 16)
                pair = sets[k][part][pl.ds(at, 16), :].astype(f32)
                near.append(jnp.where(odd, pair[8:16], pair[0:8]))
        near = jnp.concatenate(near, axis=0).astype(bf16)
        logits += dot(videos[part], near, NT)
    near = jnp.exp(SCALE * logits)
    rowsum = jnp.sum(sums, axis=1, keepdims=True)
    total = jnp.sum(jnp.log(rowsum), axis=0, keepdims=True) - 2.0 * jnp.sum(
        positive, axis=1, keepdims=True
    )
    slot = iota((1, 64), 1)
    group = sum(
        jnp.where(slot // 8 == n, row_of(xh, c, n // 2) * 2 + n % 2, 0) for n in range(8)
    )
    text = ((group * 32 + spot) * 8 + slot % 8).astype(f32)
    first = near / rowsum - jnp.where(target == text, 2.0, 0.0)
    first_hi = first.astype(bf16).astype(f32)
    near_hi = near.astype(bf16).astype(f32)
    terms = jnp.concatenate([first_hi, first - first_hi, near_hi, near - near_hi], axis=1)
    sums = dot(terms.astype(bf16), video_ref[...], TN)
    first, second = sums[0:64] + sums[64:128], sums[128:192] + sums[192:256]
    cols = col_scr[...]
    total = jnp.broadcast_to(total, (8, 128))
    for k in range(4):
        for half in range(2):
            n = k * 2 + half
            step = k // 2 * 2 + other(xl, half)
            out_ref = send_ref if k % 2 else keep_ref
            out_ref[step, :, 0:E] = first[n * 8 : (n + 1) * 8]
            out_ref[step, :, E : 2 * E] = second[n * 8 : (n + 1) * 8]
            out_ref[step, :, 2 * E : 2 * E + TILE] = cols
            out_ref[step, :, 2 * E + TILE :] = total


def first_logits(*args):
    return pl.pallas_call(
        first_kernel,
        in_specs=[VMEM] * 6,
        out_specs=[VMEM] * 4,
        out_shape=[
            jax.ShapeDtypeStruct((8, 2 * SET), f32),
            jax.ShapeDtypeStruct((8, TILE), f32),
            jax.ShapeDtypeStruct((PLANE_ROWS, 128), f32),
            jax.ShapeDtypeStruct((1, TILE), f32),
        ],
        scratch_shapes=[pltpu.VMEM((PLANE_ROWS, TILE), f32)],
        compiler_params=pltpu.CompilerParams(vmem_limit_bytes=24 << 20),
        cost_estimate=pl.CostEstimate(
            flops=2 * PLANE_ROWS * 1024 * E, bytes_accessed=2 << 20, transcendentals=1 << 18
        ),
    )(*args)


def second_logits(*args):
    return pl.pallas_call(
        second_kernel,
        in_specs=[VMEM] * 13,
        out_specs=[VMEM] * 3,
        out_shape=[
            jax.ShapeDtypeStruct((4, 8, SUMS), f32),
            jax.ShapeDtypeStruct((4, 8, SUMS), f32),
            jax.ShapeDtypeStruct((8, 2 * SET), f32),
        ],
        scratch_shapes=[pltpu.VMEM((PLANE_ROWS, TILE), f32), pltpu.VMEM((8, TILE), f32)],
        compiler_params=pltpu.CompilerParams(vmem_limit_bytes=24 << 20),
        cost_estimate=pl.CostEstimate(
            flops=2 * PLANE_ROWS * 1536 * E, bytes_accessed=4 << 20, transcendentals=1 << 18
        ),
    )(*args)


def add_kernel(keep_ref, got_ref, *out_refs):
    for k, out_ref in enumerate(out_refs):
        out_ref[...] = keep_ref[k] + got_ref[k]


def add_parts(keep, got):
    return pl.pallas_call(
        add_kernel,
        in_specs=[VMEM] * 2,
        out_specs=[VMEM] * 4,
        out_shape=[jax.ShapeDtypeStruct((8, SUMS), f32)] * 4,
        compiler_params=pltpu.CompilerParams(vmem_limit_bytes=16 << 20),
        cost_estimate=pl.CostEstimate(flops=1 << 16, bytes_accessed=1 << 19, transcendentals=0),
    )(keep, got)


def grad_kernel(
    part0_ref, part1_ref, part2_ref, part3_ref, own_ref, last_ref, target_ref,
    set0_ref, set0b_ref, set2_ref, set2b_ref, set1_ref, set1b_ref, set3_ref, set3b_ref,
    video_hat_ref, video_norm_ref, text_hat_ref, text_norm_ref, loss_ref, video_grad_ref, text_grad_ref, col_scr,
):
    xh, c, xl, spot = position()
    got = (part0_ref[...] + part1_ref[...]) + (part2_ref[...] + part3_ref[...])
    cols = got[:, 2 * E : 2 * E + TILE]
    col_scr[...] = cols
    logs = jnp.sum(jnp.sum(jnp.log(cols), axis=0, keepdims=True), axis=1, keepdims=True)
    loss_ref[...] = (logs + got[0:1, 2 * E + TILE : 2 * E + TILE + 1]) / 4096.0

    def project(direction, hat, norm):
        return (direction - jnp.sum(direction * hat, axis=1, keepdims=True) * hat) / norm

    group = (xh * 2 + c) * 2 + xl
    mine = jnp.broadcast_to(col_scr[pl.ds(group, 1), :], (8, TILE))
    here = iota((8, TILE), 1) == spot * 8 + iota((8, TILE), 0)
    mine = jnp.sum(jnp.where(here, mine, 0.0), axis=1, keepdims=True)
    text_dir = SCALE * (got[:, 0:E] + got[:, E : 2 * E] / mine)
    text_grad_ref[...] = project(text_dir, text_hat_ref[...], text_norm_ref[...])

    rows = jnp.concatenate([own_ref[...], last_ref[...]], axis=1)
    rowsum = jnp.sum(rows, axis=1, keepdims=True)
    target = target_ref[pl.ds(pl.multiple_of((xl * 32 + spot) * 8, 8), 8), :]
    lane = iota((8, TILE), 1).astype(f32)
    direction = [jnp.zeros((8, PIECE), f32)] * 2
    sets = ((set0_ref, set0b_ref), (set2_ref, set2b_ref), (set1_ref, set1b_ref), (set3_ref, set3b_ref))
    for n, k in enumerate((0, 2, 1, 3)):
        row = row_of(xh, c, k)
        for t in range(2):
            tile = row * 2 + t
            at = n * SET + t * TILE
            ex = rows[:, at : at + TILE]
            hot = jnp.where(target == (tile * TILE).astype(f32) + lane, 2.0, 0.0)
            probe = ex / rowsum + ex / col_scr[pl.ds(tile, 1), :] - hot
            probe = probe.astype(bf16)
            direction = [
                total + dot(probe, ref[t * TILE : (t + 1) * TILE, :])
                for total, ref in zip(direction, sets[n])
            ]
    low = xl == 0
    direction = jnp.concatenate(
        [
            jnp.where(low, direction[0], direction[1]),
            jnp.where(low, direction[1], direction[0]),
        ],
        axis=1,
    )
    video_grad_ref[...] = project(SCALE * direction, video_hat_ref[...], video_norm_ref[...])


def gradients(*args):
    return pl.pallas_call(
        grad_kernel,
        in_specs=[VMEM] * 19,
        out_specs=[VMEM] * 3,
        out_shape=[
            jax.ShapeDtypeStruct((1, 1), f32),
            jax.ShapeDtypeStruct((8, E), f32),
            jax.ShapeDtypeStruct((8, E), f32),
        ],
        scratch_shapes=[pltpu.VMEM((8, TILE), f32)],
        compiler_params=pltpu.CompilerParams(vmem_limit_bytes=32 << 20),
        cost_estimate=pl.CostEstimate(
            flops=2 * 8 * 2048 * E, bytes_accessed=5 << 20, transcendentals=2048
        ),
    )(*args)


def exchange(x, axes):
    return lax.all_to_all(x, axes, 0, 0, tiled=True)


def swap(x):
    return lax.ppermute(x, "c", [(0, 1), (1, 0)])


def along(x, step):
    return lax.ppermute(x, ("xh", "xl"), [(k, k ^ step) for k in range(4)])


def body(clip_tokens, clip_video, pool_vectors, out_proj, text_embed, pair_text):
    outgoing, text_hat, text_norm = clip_sums(
        clip_tokens, clip_video, pool_vectors, text_embed, pair_text
    )
    arrived = exchange(outgoing.reshape(CLIPS, 8, SENT + PIECE), ROW)
    arrived = arrived.reshape(CLIPS * 8, SENT + PIECE)
    texts = text_piece(arrived)
    moved = [along(texts, step) for step in (2, 3, 1)]
    video_embed, video_hat, video_norm, send, target = embed(arrived, out_proj)
    videos, *moved = lax.optimization_barrier((exchange(send, PLANE), *moved))
    videos = videos.reshape(PLANE_ROWS, E)
    mine = (texts, moved[2], moved[0], moved[1])
    theirs = tuple(swap(x) for x in mine)
    own, cols, sums, positive = first_logits(videos, target, *mine)
    keep, send, last = second_logits(videos, target, *mine, *theirs, cols, sums, positive)
    parts = add_parts(keep, swap(send))
    parts = [parts[0]] + [along(parts[step], step) for step in (2, 3, 1)]
    loss, video_grad, text_grad = gradients(
        *parts, own, last, target, *mine, *theirs, video_hat, video_norm, text_hat, text_norm
    )
    return video_embed, video_grad, text_grad, loss.reshape(())


def solution(mesh):
    split = Mesh(mesh.devices.reshape(2, 2, 2, 8, 4), ALL)
    return jax.shard_map(
        body,
        mesh=split,
        in_specs=(P(ALL, None, None), P(ALL), P(), P(), P(ALL, None), P(ALL)),
        out_specs=(P(ALL, None), P(ALL, None), P(ALL, None), P()),
        check_vma=False,
    )
```

```python
import jax
import jax.numpy as jnp
from jax import lax
from jax.experimental import pallas as pl
from jax.experimental.pallas import tpu as pltpu
from jax.sharding import Mesh, PartitionSpec as P

H = 25
HD = 128
D = 3200
E = 768
TOK = 16
CLIPS = 64
SOFT_CAP = 20.0
SCALE = 40.0
EPS = 1e-06
ALL = ("xh", "c", "xl", "z", "y")
ROW = ("xl", "z", "y")
PLANE = ("z", "y")
CHUNK = 32
TOKS = CHUNK * TOK
STEPS = CLIPS // CHUNK
PARTS = 4
WIDE = 7
SENT = WIDE * HD
TAIL = 4 * HD
TILE = 256
SET = CLIPS * 8
PLANE_ROWS = 256
SUMS = 2 * E + TILE + 128
PIECE = E // 2
VMEM = pl.BlockSpec(memory_space=pltpu.VMEM)
f32 = jnp.float32
bf16 = jnp.bfloat16
NT = (((1,), (1,)), ((), ()))
TN = (((0,), (0,)), ((), ()))


def dot(a, b, dims=(((1,), (0,)), ((), ()))):
    return lax.dot_general(a, b, dims, preferred_element_type=f32)


def iota(shape, dim):
    return lax.broadcasted_iota(jnp.int32, shape, dim)


def column_of(row):
    n = row.shape[1]
    eye = iota((n, n), 0) == iota((n, n), 1)
    return jnp.sum(jnp.where(eye, jnp.broadcast_to(row, (n, n)), 0.0), axis=1, keepdims=True)


def unit_rows(values):
    norms = jnp.sqrt(jnp.sum(values * values, axis=1, keepdims=True) + EPS)
    return values / norms, norms


def label_of(xh, xl, y):
    return (2 * xh + xl + 2 * y) % 4


def clip_kernel(
    video_hbm, token_hbm, pool_hbm, text_hbm, pair_hbm,
    num_ref, slot_ref, code_ref, hat_ref, norm_ref,
    video_ref, token_ref, pool_ref, text_ref, pair_ref, weight_scr, sems,
):
    small = ((pool_hbm, pool_ref), (video_hbm, video_ref), (text_hbm, text_ref), (pair_hbm, pair_ref))
    chunks = [pl.ds(i * TOKS, TOKS) for i in range(STEPS)]
    loads = [
        pltpu.make_async_copy(token_hbm.at[chunk], token_ref.at[chunk], sems.at[i])
        for i, chunk in enumerate(chunks)
    ]
    early = [
        pltpu.make_async_copy(src, dst, sems.at[STEPS + i]) for i, (src, dst) in enumerate(small)
    ]
    early[0].start()
    loads[0].start()
    for copy in early[1:] + loads[1:]:
        copy.start()
    weight_scr[...] = jnp.zeros_like(weight_scr)
    num_ref[...] = jnp.zeros_like(num_ref)
    mine = iota((CHUNK, TOKS), 1) // TOK == iota((CHUNK, TOKS), 0)
    ones = mine.astype(f32).astype(bf16)
    lane = iota((CHUNK, HD), 1)
    for copy in early[1:]:
        copy.wait()
    videos = video_ref[...].astype(f32)
    hat, norm = unit_rows(text_ref[...].astype(f32))
    hat_ref[...] = hat
    norm_ref[...] = norm
    early[0].wait()
    pool = pool_ref[...]

    def put(step, j, value):
        at = j // WIDE * CLIPS + step * CHUNK
        num_ref[at : at + CHUNK, j % WIDE * HD : (j % WIDE + 1) * HD] = value.astype(bf16)

    def weigh(step):
        loads[step].wait()
        scores = dot(pool, token_ref[chunks[step], :], NT)
        weights = jnp.exp(SOFT_CAP * jnp.tanh(scores / SOFT_CAP))
        weight_scr[step, 0:H, :] = weights
        weight_scr[step, 32 : 32 + H, :] = weights

    def total(step):
        den = dot(ones, weight_scr[step].astype(bf16), NT)
        den_hi = den.astype(bf16).astype(f32)
        here = iota((CHUNK, CLIPS), 1) == iota((CHUNK, CLIPS), 0) + step * CHUNK
        video = jnp.where(here, jnp.broadcast_to(videos, (CHUNK, CLIPS)), 0.0)
        video = jnp.sum(video, axis=1, keepdims=True).astype(jnp.int32)
        local = jnp.where(lane - 64 == video % 8, 1.0, 0.0)
        tail = jnp.where(lane < 32, den_hi, jnp.where(lane < 64, den - den_hi, local))
        put(step, H, tail)
        for h in range(0, H, 2):
            pair = range(h, min(h + 2, H))
            lhs = jnp.concatenate(
                [
                    jnp.where(
                        mine, jnp.broadcast_to(weight_scr[step, k : k + 1, :], (CHUNK, TOKS)), 0.0
                    )
                    for k in pair
                ],
                axis=0,
            ).astype(bf16)
            part = dot(lhs, token_ref[chunks[step], h * HD : (h + len(pair)) * HD])
            for n, k in enumerate(pair):
                put(step, k, part[n * CHUNK : (n + 1) * CHUNK, n * HD : (n + 1) * HD])

    for step in range(STEPS):
        weigh(step)
        if step:
            total(step - 1)
    total(STEPS - 1)

    owner = (video_ref[...] // 8).astype(f32)
    before = (column_of(owner) == owner) & (iota((CLIPS, CLIPS), 0) < iota((CLIPS, CLIPS), 1))
    rank = jnp.sum(jnp.where(before, 1.0, 0.0), axis=0, keepdims=True)
    slot = owner * 2.0 + rank
    slot_ref[...] = jnp.concatenate([slot] * PARTS, axis=1)
    pair = pair_ref[...]
    code_ref[...] = jnp.concatenate(
        [
            jnp.zeros((1, 72), f32),
            (pair // 64).astype(f32),
            (pair % 64).astype(f32),
            jnp.zeros((1, 40), f32),
        ],
        axis=1,
    )


def pack_kernel(num_ref, slot_ref, code_ref, hat_ref, far_ref, out_ref):
    xh = lax.axis_index("xh")
    shape = (CLIPS * 8, PARTS * CLIPS)
    row, col = iota(shape, 0), iota(shape, 1)
    place = (row // PARTS == slot_ref[...].astype(jnp.int32)) & (row % PARTS == col // CLIPS)
    out = dot(jnp.where(place, 1.0, 0.0).astype(bf16), num_ref[...])
    last = iota((CLIPS * 8, HD), 0) % PARTS == PARTS - 1
    out_ref[:, 0:TAIL] = out[:, 0:TAIL].astype(bf16)
    out_ref[:, TAIL : TAIL + HD] = (
        out[:, TAIL : TAIL + HD] + jnp.where(last, code_ref[...], 0.0)
    ).astype(bf16)
    out_ref[:, TAIL + HD : SENT] = out[:, TAIL + HD : SENT].astype(bf16)
    near = hat_ref[...]
    far, _ = unit_rows(far_ref[...].astype(f32))
    low = xh == 0
    texts = jnp.concatenate([jnp.where(low, near, far), jnp.where(low, far, near)], axis=0)
    row, col = iota((CLIPS * 8, 16), 0), iota((CLIPS * 8, 16), 1)
    dest = row // 8
    label = label_of(xh, dest // 32, dest % 4)
    pick = row % 4 // 2 * 8 + 2 * label + row % 2 == col
    texts = dot(jnp.where(pick, 1.0, 0.0).astype(bf16), texts.astype(bf16))
    upper = iota((CLIPS * 8, PIECE), 0) % 8 < 4
    out_ref[:, SENT : SENT + PIECE] = jnp.where(
        upper, texts[:, 0:PIECE], texts[:, PIECE:E]
    ).astype(bf16)


def pack(*args):
    return pl.pallas_call(
        pack_kernel,
        in_specs=[VMEM] * 5,
        out_specs=VMEM,
        out_shape=jax.ShapeDtypeStruct((CLIPS * 8, SENT + PIECE), bf16),
        compiler_params=pltpu.CompilerParams(vmem_limit_bytes=24 << 20),
        cost_estimate=pl.CostEstimate(
            flops=2 * 512 * 256 * SENT, bytes_accessed=2 << 20, transcendentals=0
        ),
    )(*args)


def clip_sums(clip_tokens, clip_video, pool_vectors, text_embed, pair_text):
    args = (
        clip_video.reshape(1, CLIPS),
        clip_tokens.reshape(CLIPS * TOK, D),
        pool_vectors,
        text_embed,
        pair_text.reshape(1, 8),
    )
    return pl.pallas_call(
        clip_kernel,
        in_specs=[pl.BlockSpec(memory_space=pltpu.HBM)] * 5,
        out_specs=[VMEM] * 5,
        out_shape=[
            jax.ShapeDtypeStruct((PARTS * CLIPS, SENT), bf16),
            jax.ShapeDtypeStruct((1, PARTS * CLIPS), f32),
            jax.ShapeDtypeStruct((1, HD), f32),
            jax.ShapeDtypeStruct((8, E), f32),
            jax.ShapeDtypeStruct((8, 1), f32),
        ],
        scratch_shapes=[pltpu.VMEM(x.shape, x.dtype) for x in args]
        + [
            pltpu.VMEM((STEPS, 128, TOKS), f32),
            pltpu.SemaphoreType.DMA((STEPS + 4,)),
        ],
        compiler_params=pltpu.CompilerParams(vmem_limit_bytes=24 << 20),
        cost_estimate=pl.CostEstimate(
            flops=2 * 1024 * D * 64, bytes_accessed=8 << 20, transcendentals=1 << 17
        ),
    )(*(pltpu.with_memory_space_constraint(x, pltpu.HBM) for x in args))


def embed_kernel(
    arrived_ref, proj_ref, emb_ref, hat_ref, norm_ref, send_ref, target_ref
):
    rows = CLIPS * 8
    tails = arrived_ref[:, TAIL : TAIL + HD]
    pick = jnp.where(iota((8, HD), 1) - 64 == iota((8, HD), 0), 1.0, 0.0).astype(bf16)
    hot = dot(pick, tails, NT)
    hot = jnp.where(iota((8, rows), 1) % PARTS == PARTS - 1, hot, 0.0)
    assign = jnp.concatenate(
        [hot if p == PARTS - 1 else pltpu.roll(hot, rows - (PARTS - 1 - p), 1) for p in range(PARTS)],
        axis=0,
    )
    sums = dot(assign.astype(bf16), arrived_ref[:, 0:SENT])

    def chunk(j):
        p, q = j // WIDE, j % WIDE
        return sums[p * 8 : (p + 1) * 8, q * HD : (q + 1) * HD]

    den = chunk(H)
    den = den[:, 0:32] + den[:, 32:64]
    pooled = jnp.concatenate([chunk(h) / den[:, h : h + 1] for h in range(H)], axis=1)
    hi = pooled.astype(bf16).astype(f32)
    mid = (pooled - hi).astype(bf16).astype(f32)
    low = pooled - hi - mid
    parts = dot(jnp.concatenate([hi, mid, low], axis=0).astype(bf16), proj_ref[...])
    emb = parts[0:8] + parts[8:16] + parts[16:24]
    emb_ref[...] = emb.astype(bf16)
    hat, norm = unit_rows(emb)
    hat_ref[...] = hat
    norm_ref[...] = norm
    hat_low = hat.astype(bf16)
    for k in range(32):
        send_ref[k] = hat_low
    code = tails.astype(f32).reshape(CLIPS, 8, HD)[:, 3:4, :]
    code = jnp.broadcast_to(code, (CLIPS, 8, HD)).reshape(rows, HD)
    lane, own = iota((rows, HD), 1), iota((rows, HD), 0) % 8
    code = jnp.where(lane - 72 == own, 64.0 * code, jnp.where(lane - 80 == own, code, 0.0))
    target_ref[...] = jnp.sum(code, axis=1, keepdims=True)


def embed(arrived, out_proj):
    return pl.pallas_call(
        embed_kernel,
        in_specs=[VMEM, VMEM],
        out_specs=[VMEM] * 5,
        out_shape=[
            jax.ShapeDtypeStruct((8, E), bf16),
            jax.ShapeDtypeStruct((8, E), f32),
            jax.ShapeDtypeStruct((8, 1), f32),
            jax.ShapeDtypeStruct((32, 8, E), bf16),
            jax.ShapeDtypeStruct((SET, 1), f32),
        ],
        compiler_params=pltpu.CompilerParams(vmem_limit_bytes=24 << 20),
        cost_estimate=pl.CostEstimate(
            flops=2 * 24 * D * E, bytes_accessed=6 << 20, transcendentals=0
        ),
    )(arrived, out_proj)


def text_kernel(arrived_ref, text_ref):
    halves = arrived_ref[:, SENT : SENT + PIECE]
    row, col = iota((TILE, CLIPS * 8), 0), iota((TILE, CLIPS * 8), 1)
    for part in range(2):
        pick = row // 4 * 8 + part * 4 + row % 4 == col
        texts = dot(jnp.where(pick, 1.0, 0.0).astype(bf16), halves)
        text_ref[:, part * PIECE : (part + 1) * PIECE] = texts.astype(bf16)


def text_piece(arrived):
    return pl.pallas_call(
        text_kernel,
        in_specs=[VMEM],
        out_specs=VMEM,
        out_shape=jax.ShapeDtypeStruct((TILE, E), bf16),
        compiler_params=pltpu.CompilerParams(vmem_limit_bytes=16 << 20),
        cost_estimate=pl.CostEstimate(
            flops=4 * 256 * 512 * PIECE, bytes_accessed=1 << 20, transcendentals=0
        ),
    )(arrived)


def position():
    xh, c, xl, z, y = (lax.axis_index(a) for a in ALL)
    return xh, c, xl, z * 4 + y


def other(a, flip):
    return a + flip - 2 * flip * a


def row_of(xh, c, k):
    return other(xh, k // 2) * 2 + other(c, k % 2)


def tile_of(xh, c, xl, spot, k):
    y = spot % 4
    label = (
        label_of(xh, xl, y),
        label_of(xh, 1 - xl, y),
        label_of(1 - xh, 1 - xl, y),
        label_of(xh, xl, y + 1),
    )[k % 4]
    return other(c, k // 4) * 4 + label


def texts_of(tile, j):
    row = j % 4 // 2 * 2 + tile // 4
    return ((row * 64 + j // 4) * 8 + tile % 4 * 2 + j % 2).astype(f32)


def score(videos, target, pieces, tiles, own_ref, tile_scr, cols_ref, sums, positive, base):
    for n, (ref, tile) in enumerate(zip(pieces, tiles)):
        logits = SCALE * dot(videos, ref[...], NT)
        ex = jnp.exp(logits)
        tile_scr[...] = ex
        cols_ref[pl.ds(tile, 1), :] = jnp.sum(ex, axis=0, keepdims=True)
        sums += ex[:, 0:128] + ex[:, 128:TILE]
        hit = target == texts_of(tile, iota((1, TILE), 1))
        positive += jnp.sum(jnp.where(hit, logits, 0.0), axis=0, keepdims=True)
        own_ref[:, n * TILE : (n + 1) * TILE] = tile_scr[pl.ds(base, 8), :]
    return sums, positive


def plane_rows(target_ref, xl):
    return target_ref[pl.ds(pl.multiple_of(xl * PLANE_ROWS, PLANE_ROWS), PLANE_ROWS), :]


def first_kernel(
    video_ref, target_ref, set0_ref, set1_ref, set2_ref, set3_ref,
    own_ref, cols_ref, sums_ref, positive_ref, tile_scr,
):
    xh, c, xl, spot = position()
    cols_ref[...] = jnp.zeros_like(cols_ref)
    sums_ref[...], positive_ref[...] = score(
        video_ref[...], plane_rows(target_ref, xl), (set0_ref, set1_ref, set2_ref, set3_ref),
        [tile_of(xh, c, xl, spot, k) for k in range(4)], own_ref, tile_scr, cols_ref,
        jnp.zeros((PLANE_ROWS, 128), f32), jnp.zeros((1, TILE), f32), pl.multiple_of(spot * 8, 8),
    )


def second_kernel(
    video_ref, target_ref, set0_ref, set1_ref, set2_ref, set3_ref, set4_ref, set5_ref, set6_ref,
    set7_ref, cols_ref, sums_ref, positive_ref,
    keep_ref, send_ref, own_ref, tile_scr, col_scr,
):
    xh, c, xl, spot = position()
    target = plane_rows(target_ref, xl)
    videos = video_ref[...]
    pieces = (set0_ref, set1_ref, set2_ref, set3_ref, set4_ref, set5_ref, set6_ref, set7_ref)
    tiles = [tile_of(xh, c, xl, spot, k) for k in range(8)]
    col_scr[...] = cols_ref[...]
    sums, positive = score(
        videos, target, pieces[4:8], tiles[4:8], own_ref, tile_scr, col_scr,
        sums_ref[...], positive_ref[...], pl.multiple_of(spot * 8, 8),
    )

    def near_texts(slot):
        group = sum(
            jnp.where(slot // 8 == n, row_of(xh, c, n // 2) * 2 + n % 2, 0) for n in range(8)
        )
        return ((group * 32 + spot) * 8 + slot % 8).astype(f32)

    column = near_texts(iota((64, 1), 0))
    near = jnp.zeros((64, E), f32)
    for ref, tile in zip(pieces, tiles):
        pick = column == texts_of(tile, iota((1, TILE), 1))
        near += dot(jnp.where(pick, 1.0, 0.0).astype(bf16), ref[...])
    near = jnp.exp(SCALE * dot(videos, near.astype(bf16), NT))
    rowsum = jnp.sum(sums, axis=1, keepdims=True)
    total = jnp.sum(jnp.log(rowsum), axis=0, keepdims=True) - 2.0 * jnp.sum(
        positive, axis=1, keepdims=True
    )
    text = near_texts(iota((1, 64), 1))
    first = near / rowsum - jnp.where(target == text, 2.0, 0.0)
    first_hi = first.astype(bf16).astype(f32)
    near_hi = near.astype(bf16).astype(f32)
    terms = jnp.concatenate([first_hi, first - first_hi, near_hi, near - near_hi], axis=1)
    sums = dot(terms.astype(bf16), videos, TN)
    first, second = sums[0:64] + sums[64:128], sums[128:192] + sums[192:256]
    cols = col_scr[...]
    total = jnp.broadcast_to(total, (8, 128))
    for k in range(4):
        for half in range(2):
            n = k * 2 + half
            step = k // 2 * 2 + other(xl, half)
            out_ref = send_ref if k % 2 else keep_ref
            out_ref[step, :, 0:E] = first[n * 8 : (n + 1) * 8]
            out_ref[step, :, E : 2 * E] = second[n * 8 : (n + 1) * 8]
            out_ref[step, :, 2 * E : 2 * E + TILE] = cols
            out_ref[step, :, 2 * E + TILE :] = total


def first_logits(*args):
    return pl.pallas_call(
        first_kernel,
        in_specs=[VMEM] * 6,
        out_specs=[VMEM] * 4,
        out_shape=[
            jax.ShapeDtypeStruct((8, 2 * SET), f32),
            jax.ShapeDtypeStruct((8, TILE), f32),
            jax.ShapeDtypeStruct((PLANE_ROWS, 128), f32),
            jax.ShapeDtypeStruct((1, TILE), f32),
        ],
        scratch_shapes=[pltpu.VMEM((PLANE_ROWS, TILE), f32)],
        compiler_params=pltpu.CompilerParams(vmem_limit_bytes=24 << 20),
        cost_estimate=pl.CostEstimate(
            flops=2 * PLANE_ROWS * 1024 * E, bytes_accessed=2 << 20, transcendentals=1 << 18
        ),
    )(*args)


def second_logits(*args):
    return pl.pallas_call(
        second_kernel,
        in_specs=[VMEM] * 13,
        out_specs=[VMEM] * 3,
        out_shape=[
            jax.ShapeDtypeStruct((4, 8, SUMS), f32),
            jax.ShapeDtypeStruct((4, 8, SUMS), f32),
            jax.ShapeDtypeStruct((8, 2 * SET), f32),
        ],
        scratch_shapes=[pltpu.VMEM((PLANE_ROWS, TILE), f32), pltpu.VMEM((8, TILE), f32)],
        compiler_params=pltpu.CompilerParams(vmem_limit_bytes=24 << 20),
        cost_estimate=pl.CostEstimate(
            flops=2 * PLANE_ROWS * 1536 * E, bytes_accessed=4 << 20, transcendentals=1 << 18
        ),
    )(*args)


def add_kernel(keep_ref, got_ref, *out_refs):
    for k, out_ref in enumerate(out_refs):
        out_ref[...] = keep_ref[k] + got_ref[k]


def add_parts(keep, got):
    return pl.pallas_call(
        add_kernel,
        in_specs=[VMEM] * 2,
        out_specs=[VMEM] * 4,
        out_shape=[jax.ShapeDtypeStruct((8, SUMS), f32)] * 4,
        compiler_params=pltpu.CompilerParams(vmem_limit_bytes=16 << 20),
        cost_estimate=pl.CostEstimate(flops=1 << 16, bytes_accessed=1 << 19, transcendentals=0),
    )(keep, got)


def grad_kernel(
    part0_ref, part1_ref, part2_ref, part3_ref, own_ref, last_ref, target_ref,
    set0_ref, set1_ref, set2_ref, set3_ref, set4_ref, set5_ref, set6_ref, set7_ref,
    video_hat_ref, video_norm_ref, text_hat_ref, text_norm_ref, loss_ref, video_grad_ref, text_grad_ref, col_scr,
):
    xh, c, xl, spot = position()
    got = (part0_ref[...] + part1_ref[...]) + (part2_ref[...] + part3_ref[...])
    cols = got[:, 2 * E : 2 * E + TILE]
    col_scr[...] = cols
    logs = jnp.sum(jnp.sum(jnp.log(cols), axis=0, keepdims=True), axis=1, keepdims=True)
    loss_ref[...] = (logs + got[0:1, 2 * E + TILE : 2 * E + TILE + 1]) / 4096.0

    def project(direction, hat, norm):
        return (direction - jnp.sum(direction * hat, axis=1, keepdims=True) * hat) / norm

    at = (xl * 32 + spot) * 4 + xh * 2
    lane = iota((4, TILE), 1) - at
    mine = jnp.where(c == 0, cols[0:4], cols[4:8])
    pair = [jnp.sum(jnp.where(lane == n, mine, 0.0), axis=1, keepdims=True) for n in range(2)]
    row = iota((8, 1), 0)
    mine = sum(
        jnp.where(row == n, pair[n % 2][n // 2 : n // 2 + 1], 0.0) for n in range(8)
    )
    text_dir = SCALE * (got[:, 0:E] + got[:, E : 2 * E] / mine)
    text_grad_ref[...] = project(text_dir, text_hat_ref[...], text_norm_ref[...])

    rows = jnp.concatenate([own_ref[...], last_ref[...]], axis=1)
    rowsum = jnp.sum(rows, axis=1, keepdims=True)
    target = target_ref[pl.ds(pl.multiple_of((xl * 32 + spot) * 8, 8), 8), :]
    direction = jnp.zeros((8, E), f32)
    pieces = (set0_ref, set1_ref, set2_ref, set3_ref, set4_ref, set5_ref, set6_ref, set7_ref)
    for k, ref in enumerate(pieces):
        tile = tile_of(xh, c, xl, spot, k)
        ex = rows[:, k * TILE : (k + 1) * TILE]
        hot = jnp.where(target == texts_of(tile, iota((1, TILE), 1)), 2.0, 0.0)
        probe = ex / rowsum + ex / col_scr[pl.ds(tile, 1), :] - hot
        direction += dot(probe.astype(bf16), ref[...])
    video_grad_ref[...] = project(SCALE * direction, video_hat_ref[...], video_norm_ref[...])


def gradients(*args):
    return pl.pallas_call(
        grad_kernel,
        in_specs=[VMEM] * 19,
        out_specs=[VMEM] * 3,
        out_shape=[
            jax.ShapeDtypeStruct((1, 1), f32),
            jax.ShapeDtypeStruct((8, E), f32),
            jax.ShapeDtypeStruct((8, E), f32),
        ],
        scratch_shapes=[pltpu.VMEM((8, TILE), f32)],
        compiler_params=pltpu.CompilerParams(vmem_limit_bytes=32 << 20),
        cost_estimate=pl.CostEstimate(
            flops=2 * 8 * 2048 * E, bytes_accessed=5 << 20, transcendentals=2048
        ),
    )(*args)


def exchange(x, axes):
    return lax.all_to_all(x, axes, 0, 0, tiled=True)


def swap(x):
    return lax.ppermute(x, "c", [(0, 1), (1, 0)])


def along(x, step):
    return lax.ppermute(x, ("xh", "xl"), [(k, k ^ step) for k in range(4)])


def turn_y(x):
    return lax.ppermute(x, "y", [(k, k ^ 1) for k in range(4)])


def body(clip_tokens, clip_video, pool_vectors, out_proj, text_embed, pair_text):
    far_text = along(text_embed, 2)
    *sums, text_hat, text_norm = clip_sums(
        clip_tokens, clip_video, pool_vectors, text_embed, pair_text
    )
    outgoing = pack(*sums, text_hat, far_text)
    arrived = exchange(outgoing.reshape(CLIPS, 8, SENT + PIECE), ROW)
    arrived = arrived.reshape(CLIPS * 8, SENT + PIECE)
    texts = text_piece(arrived)
    moved = [turn_y(texts), along(texts, 3), along(texts, 1)]
    video_embed, video_hat, video_norm, send, target = embed(arrived, out_proj)
    videos, moved[0] = lax.optimization_barrier((exchange(send, PLANE), moved[0]))
    videos = videos.reshape(PLANE_ROWS, E)
    mine = (texts, moved[2], moved[1], moved[0])
    theirs = tuple(swap(x) for x in mine)
    own, cols, sums, positive = first_logits(videos, target, *mine)
    keep, send, last = second_logits(videos, target, *mine, *theirs, cols, sums, positive)
    parts = add_parts(keep, swap(send))
    parts = [parts[0]] + [along(parts[step], step) for step in (2, 3, 1)]
    loss, video_grad, text_grad = gradients(
        *parts, own, last, target, *mine, *theirs, video_hat, video_norm, text_hat, text_norm
    )
    return video_embed, video_grad, text_grad, loss.reshape(())


def solution(mesh):
    split = Mesh(mesh.devices.reshape(2, 2, 2, 8, 4), ALL)
    return jax.shard_map(
        body,
        mesh=split,
        in_specs=(P(ALL, None, None), P(ALL), P(), P(), P(ALL, None), P(ALL)),
        out_specs=(P(ALL, None), P(ALL, None), P(ALL, None), P()),
        check_vma=False,
    )
```

```python
import jax
import jax.numpy as jnp
from jax import lax
from jax.experimental import pallas as pl
from jax.experimental.pallas import tpu as pltpu
from jax.sharding import Mesh, PartitionSpec as P

H = 25
HD = 128
D = 3200
E = 768
TOK = 16
CLIPS = 64
SOFT_CAP = 20.0
SCALE = 40.0
EPS = 1e-06
ALL = ("xh", "c", "xl", "z", "y")
ROW = ("xl", "z", "y")
PLANE = ("z", "y")
CHUNK = 32
TOKS = CHUNK * TOK
STEPS = CLIPS // CHUNK
PARTS = 4
WIDE = 7
SENT = WIDE * HD
TAIL = 4 * HD
TILE = 256
SET = CLIPS * 8
PLANE_ROWS = 256
SUMS = 2 * E + TILE + 128
PIECE = E // 2
VMEM = pl.BlockSpec(memory_space=pltpu.VMEM)
f32 = jnp.float32
bf16 = jnp.bfloat16
NT = (((1,), (1,)), ((), ()))
TN = (((0,), (0,)), ((), ()))


def dot(a, b, dims=(((1,), (0,)), ((), ()))):
    return lax.dot_general(a, b, dims, preferred_element_type=f32)


def iota(shape, dim):
    return lax.broadcasted_iota(jnp.int32, shape, dim)


def column_of(row):
    n = row.shape[1]
    eye = iota((n, n), 0) == iota((n, n), 1)
    return jnp.sum(jnp.where(eye, jnp.broadcast_to(row, (n, n)), 0.0), axis=1, keepdims=True)


def unit_rows(values):
    norms = jnp.sqrt(jnp.sum(values * values, axis=1, keepdims=True) + EPS)
    return values / norms, norms


def label_of(xh, xl, y):
    return (2 * xh + xl + 2 * y) % 4


def clip_kernel(
    video_hbm, token_hbm, pool_hbm, text_hbm, pair_hbm,
    num_ref, slot_ref, code_ref, hat_ref,
    video_ref, token_ref, pool_ref, text_ref, pair_ref, weight_scr, sems,
):
    small = ((pool_hbm, pool_ref), (video_hbm, video_ref), (text_hbm, text_ref), (pair_hbm, pair_ref))
    chunks = [pl.ds(i * TOKS, TOKS) for i in range(STEPS)]
    loads = [
        pltpu.make_async_copy(token_hbm.at[chunk], token_ref.at[chunk], sems.at[i])
        for i, chunk in enumerate(chunks)
    ]
    early = [
        pltpu.make_async_copy(src, dst, sems.at[STEPS + i]) for i, (src, dst) in enumerate(small)
    ]
    early[0].start()
    loads[0].start()
    for copy in early[1:] + loads[1:]:
        copy.start()
    weight_scr[...] = jnp.zeros_like(weight_scr)
    num_ref[...] = jnp.zeros_like(num_ref)
    mine = iota((CHUNK, TOKS), 1) // TOK == iota((CHUNK, TOKS), 0)
    ones = mine.astype(f32).astype(bf16)
    lane = iota((CHUNK, HD), 1)
    for copy in early[1:]:
        copy.wait()
    videos = video_ref[...].astype(f32)
    hat_ref[...], _ = unit_rows(text_ref[...].astype(f32))
    early[0].wait()
    pool = pool_ref[...]

    def put(step, j, value):
        at = j // WIDE * CLIPS + step * CHUNK
        num_ref[at : at + CHUNK, j % WIDE * HD : (j % WIDE + 1) * HD] = value.astype(bf16)

    def weigh(step):
        loads[step].wait()
        scores = dot(pool, token_ref[chunks[step], :], NT)
        weights = jnp.exp(SOFT_CAP * jnp.tanh(scores / SOFT_CAP))
        weight_scr[step, 0:H, :] = weights
        weight_scr[step, 32 : 32 + H, :] = weights

    def total(step):
        den = dot(ones, weight_scr[step].astype(bf16), NT)
        den_hi = den.astype(bf16).astype(f32)
        here = iota((CHUNK, CLIPS), 1) == iota((CHUNK, CLIPS), 0) + step * CHUNK
        video = jnp.where(here, jnp.broadcast_to(videos, (CHUNK, CLIPS)), 0.0)
        video = jnp.sum(video, axis=1, keepdims=True).astype(jnp.int32)
        local = jnp.where(lane - 64 == video % 8, 1.0, 0.0)
        tail = jnp.where(lane < 32, den_hi, jnp.where(lane < 64, den - den_hi, local))
        put(step, H, tail)
        for h in range(0, H, 2):
            pair = range(h, min(h + 2, H))
            lhs = jnp.concatenate(
                [
                    jnp.where(
                        mine, jnp.broadcast_to(weight_scr[step, k : k + 1, :], (CHUNK, TOKS)), 0.0
                    )
                    for k in pair
                ],
                axis=0,
            ).astype(bf16)
            part = dot(lhs, token_ref[chunks[step], h * HD : (h + len(pair)) * HD])
            for n, k in enumerate(pair):
                put(step, k, part[n * CHUNK : (n + 1) * CHUNK, n * HD : (n + 1) * HD])

    for step in range(STEPS):
        weigh(step)
        if step:
            total(step - 1)
    total(STEPS - 1)

    owner = (video_ref[...] // 8).astype(f32)
    before = (column_of(owner) == owner) & (iota((CLIPS, CLIPS), 0) < iota((CLIPS, CLIPS), 1))
    rank = jnp.sum(jnp.where(before, 1.0, 0.0), axis=0, keepdims=True)
    slot = owner * 2.0 + rank
    slot_ref[...] = jnp.concatenate([slot] * PARTS, axis=1)
    pair = pair_ref[...]
    code_ref[...] = jnp.concatenate(
        [
            jnp.zeros((1, 72), f32),
            (pair // 64).astype(f32),
            (pair % 64).astype(f32),
            jnp.zeros((1, 40), f32),
        ],
        axis=1,
    )


def pack_kernel(num_ref, slot_ref, code_ref, hat_ref, far_ref, out_ref):
    xh = lax.axis_index("xh")
    shape = (CLIPS * 8, PARTS * CLIPS)
    row, col = iota(shape, 0), iota(shape, 1)
    place = (row // PARTS == slot_ref[...].astype(jnp.int32)) & (row % PARTS == col // CLIPS)
    out = dot(jnp.where(place, 1.0, 0.0).astype(bf16), num_ref[...])
    last = iota((CLIPS * 8, HD), 0) % PARTS == PARTS - 1
    out_ref[:, 0:TAIL] = out[:, 0:TAIL].astype(bf16)
    out_ref[:, TAIL : TAIL + HD] = (
        out[:, TAIL : TAIL + HD] + jnp.where(last, code_ref[...], 0.0)
    ).astype(bf16)
    out_ref[:, TAIL + HD : SENT] = out[:, TAIL + HD : SENT].astype(bf16)
    near = hat_ref[...]
    far, _ = unit_rows(far_ref[...].astype(f32))
    low = xh == 0
    texts = jnp.concatenate([jnp.where(low, near, far), jnp.where(low, far, near)], axis=0)
    row, col = iota((CLIPS * 8, 16), 0), iota((CLIPS * 8, 16), 1)
    dest = row // 8
    label = label_of(xh, dest // 32, dest % 4)
    pick = row % 4 // 2 * 8 + 2 * label + row % 2 == col
    texts = dot(jnp.where(pick, 1.0, 0.0).astype(bf16), texts.astype(bf16))
    upper = iota((CLIPS * 8, PIECE), 0) % 8 < 4
    out_ref[:, SENT : SENT + PIECE] = jnp.where(
        upper, texts[:, 0:PIECE], texts[:, PIECE:E]
    ).astype(bf16)


def pack(*args):
    return pl.pallas_call(
        pack_kernel,
        in_specs=[VMEM] * 5,
        out_specs=VMEM,
        out_shape=jax.ShapeDtypeStruct((CLIPS * 8, SENT + PIECE), bf16),
        compiler_params=pltpu.CompilerParams(vmem_limit_bytes=16 << 20),
        cost_estimate=pl.CostEstimate(
            flops=2 * 512 * 256 * SENT, bytes_accessed=2 << 20, transcendentals=0
        ),
    )(*args)


def clip_sums(clip_tokens, clip_video, pool_vectors, text_embed, pair_text):
    args = (
        clip_video.reshape(1, CLIPS),
        clip_tokens.reshape(CLIPS * TOK, D),
        pool_vectors,
        text_embed,
        pair_text.reshape(1, 8),
    )
    return pl.pallas_call(
        clip_kernel,
        in_specs=[pl.BlockSpec(memory_space=pltpu.HBM)] * 5,
        out_specs=[VMEM] * 4,
        out_shape=[
            jax.ShapeDtypeStruct((PARTS * CLIPS, SENT), bf16),
            jax.ShapeDtypeStruct((1, PARTS * CLIPS), f32),
            jax.ShapeDtypeStruct((1, HD), f32),
            jax.ShapeDtypeStruct((8, E), f32),
        ],
        scratch_shapes=[pltpu.VMEM(x.shape, x.dtype) for x in args]
        + [
            pltpu.VMEM((STEPS, 128, TOKS), f32),
            pltpu.SemaphoreType.DMA((STEPS + 4,)),
        ],
        compiler_params=pltpu.CompilerParams(vmem_limit_bytes=16 << 20),
        cost_estimate=pl.CostEstimate(
            flops=2 * 1024 * D * 64, bytes_accessed=8 << 20, transcendentals=1 << 17
        ),
    )(*(pltpu.with_memory_space_constraint(x, pltpu.HBM) for x in args))


def embed_kernel(
    arrived_ref, proj_ref, emb_ref, hat_ref, norm_ref, send_ref
):
    rows = CLIPS * 8
    tails = arrived_ref[:, TAIL : TAIL + HD]
    pick = jnp.where(iota((8, HD), 1) - 64 == iota((8, HD), 0), 1.0, 0.0).astype(bf16)
    hot = dot(pick, tails, NT)
    hot = jnp.where(iota((8, rows), 1) % PARTS == PARTS - 1, hot, 0.0)
    assign = jnp.concatenate(
        [hot if p == PARTS - 1 else pltpu.roll(hot, rows - (PARTS - 1 - p), 1) for p in range(PARTS)],
        axis=0,
    )
    sums = dot(assign.astype(bf16), arrived_ref[:, 0:SENT])

    def chunk(j):
        p, q = j // WIDE, j % WIDE
        return sums[p * 8 : (p + 1) * 8, q * HD : (q + 1) * HD]

    den = chunk(H)
    den = den[:, 0:32] + den[:, 32:64]
    pooled = jnp.concatenate([chunk(h) / den[:, h : h + 1] for h in range(H)], axis=1)
    hi = pooled.astype(bf16).astype(f32)
    mid = (pooled - hi).astype(bf16).astype(f32)
    low = pooled - hi - mid
    parts = dot(jnp.concatenate([hi, mid, low], axis=0).astype(bf16), proj_ref[...])
    emb = parts[0:8] + parts[8:16] + parts[16:24]
    emb_ref[...] = emb.astype(bf16)
    hat, norm = unit_rows(emb)
    hat_ref[...] = hat
    norm_ref[...] = norm
    hat_low = hat.astype(bf16)
    for k in range(32):
        send_ref[k] = hat_low


def embed(arrived, out_proj):
    return pl.pallas_call(
        embed_kernel,
        in_specs=[VMEM, VMEM],
        out_specs=[VMEM] * 4,
        out_shape=[
            jax.ShapeDtypeStruct((8, E), bf16),
            jax.ShapeDtypeStruct((8, E), f32),
            jax.ShapeDtypeStruct((8, 1), f32),
            jax.ShapeDtypeStruct((32, 8, E), bf16),
        ],
        compiler_params=pltpu.CompilerParams(vmem_limit_bytes=16 << 20),
        cost_estimate=pl.CostEstimate(
            flops=2 * 24 * D * E, bytes_accessed=6 << 20, transcendentals=0
        ),
    )(arrived, out_proj)


def text_kernel(arrived_ref, hat_ref, norm_ref, text_ref, target_ref, hat_out, norm_out):
    hat_out[...] = hat_ref[...]
    norm_out[...] = norm_ref[...]
    halves = arrived_ref[:, SENT : SENT + PIECE]
    row, col = iota((TILE, CLIPS * 8), 0), iota((TILE, CLIPS * 8), 1)
    for part in range(2):
        pick = row // 4 * 8 + part * 4 + row % 4 == col
        texts = dot(jnp.where(pick, 1.0, 0.0).astype(bf16), halves)
        text_ref[:, part * PIECE : (part + 1) * PIECE] = texts.astype(bf16)
    rows = CLIPS * 8
    code = arrived_ref[:, TAIL : TAIL + HD].astype(f32).reshape(CLIPS, 8, HD)[:, 3:4, :]
    code = jnp.broadcast_to(code, (CLIPS, 8, HD)).reshape(rows, HD)
    lane, own = iota((rows, HD), 1), iota((rows, HD), 0) % 8
    code = jnp.where(lane - 72 == own, 64.0 * code, jnp.where(lane - 80 == own, code, 0.0))
    target_ref[...] = jnp.sum(code, axis=1, keepdims=True)


def text_piece(*args):
    return pl.pallas_call(
        text_kernel,
        in_specs=[VMEM] * 3,
        out_specs=[VMEM] * 4,
        out_shape=[
            jax.ShapeDtypeStruct((TILE, E), bf16),
            jax.ShapeDtypeStruct((SET, 1), f32),
            jax.ShapeDtypeStruct((8, E), f32),
            jax.ShapeDtypeStruct((8, 1), f32),
        ],
        compiler_params=pltpu.CompilerParams(vmem_limit_bytes=16 << 20),
        cost_estimate=pl.CostEstimate(
            flops=4 * 256 * 512 * PIECE, bytes_accessed=1 << 20, transcendentals=0
        ),
    )(*args)


def position():
    xh, c, xl, z, y = (lax.axis_index(a) for a in ALL)
    return xh, c, xl, z * 4 + y


def other(a, flip):
    return a + flip - 2 * flip * a


def row_of(xh, c, k):
    return other(xh, k // 2) * 2 + other(c, k % 2)


def tile_of(xh, c, xl, spot, k):
    y = spot % 4
    label = (
        label_of(xh, xl, y),
        label_of(xh, 1 - xl, y),
        label_of(1 - xh, 1 - xl, y),
        label_of(xh, xl, y + 1),
    )[k % 4]
    return other(c, k // 4) * 4 + label


def texts_of(tile, j):
    row = j % 4 // 2 * 2 + tile // 4
    return ((row * 64 + j // 4) * 8 + tile % 4 * 2 + j % 2).astype(f32)


def score(videos, target, pieces, tiles, own_ref, tile_scr, cols_ref, sums, positive, base):
    for n, (ref, tile) in enumerate(zip(pieces, tiles)):
        logits = SCALE * dot(videos, ref[...], NT)
        ex = jnp.exp(logits)
        tile_scr[...] = ex
        cols_ref[pl.ds(tile, 1), :] = jnp.sum(ex, axis=0, keepdims=True)
        sums += ex[:, 0:128] + ex[:, 128:TILE]
        hit = target == texts_of(tile, iota((1, TILE), 1))
        positive += jnp.sum(jnp.where(hit, logits, 0.0), axis=0, keepdims=True)
        own_ref[:, n * TILE : (n + 1) * TILE] = tile_scr[pl.ds(base, 8), :]
    return sums, positive


def plane_rows(target_ref, xl):
    return target_ref[pl.ds(pl.multiple_of(xl * PLANE_ROWS, PLANE_ROWS), PLANE_ROWS), :]


def first_kernel(
    video_ref, target_ref, set0_ref, set1_ref, set2_ref, set3_ref, hat_ref, norm_ref,
    own_ref, cols_ref, sums_ref, positive_ref, hat_out, norm_out, tile_scr,
):
    xh, c, xl, spot = position()
    hat_out[...] = hat_ref[...]
    norm_out[...] = norm_ref[...]
    cols_ref[...] = jnp.zeros_like(cols_ref)
    sums_ref[...], positive_ref[...] = score(
        video_ref[...], plane_rows(target_ref, xl), (set0_ref, set1_ref, set2_ref, set3_ref),
        [tile_of(xh, c, xl, spot, k) for k in range(4)], own_ref, tile_scr, cols_ref,
        jnp.zeros((PLANE_ROWS, 128), f32), jnp.zeros((1, TILE), f32), pl.multiple_of(spot * 8, 8),
    )


def second_kernel(
    video_ref, target_ref, set0_ref, set1_ref, set2_ref, set3_ref, set4_ref, set5_ref, set6_ref,
    set7_ref, cols_ref, sums_ref, positive_ref,
    keep_ref, send_ref, own_ref, tile_scr, col_scr,
):
    xh, c, xl, spot = position()
    target = plane_rows(target_ref, xl)
    videos = video_ref[...]
    pieces = (set0_ref, set1_ref, set2_ref, set3_ref, set4_ref, set5_ref, set6_ref, set7_ref)
    tiles = [tile_of(xh, c, xl, spot, k) for k in range(8)]
    col_scr[...] = cols_ref[...]
    sums, positive = score(
        videos, target, pieces[4:8], tiles[4:8], own_ref, tile_scr, col_scr,
        sums_ref[...], positive_ref[...], pl.multiple_of(spot * 8, 8),
    )

    def near_texts(slot):
        group = sum(
            jnp.where(slot // 8 == n, row_of(xh, c, n // 2) * 2 + n % 2, 0) for n in range(8)
        )
        return ((group * 32 + spot) * 8 + slot % 8).astype(f32)

    blocks = [
        ref[pl.ds(pl.multiple_of(half * 128 + spot // 4 * 16, 16), 16), :]
        for ref in pieces
        for half in range(2)
    ]
    col = iota((1, TILE), 1)
    tile = sum(jnp.where(col // 32 == k, tiles[k], 0) for k in range(8))
    held = texts_of(tile, col % 32 // 16 * 128 + spot // 4 * 16 + col % 16)
    pick = near_texts(iota((64, 1), 0)) == held
    near = dot(jnp.where(pick, 1.0, 0.0).astype(bf16), jnp.concatenate(blocks, axis=0))
    near = jnp.exp(SCALE * dot(videos, near.astype(bf16), NT))
    rowsum = jnp.sum(sums, axis=1, keepdims=True)
    total = jnp.sum(jnp.log(rowsum), axis=0, keepdims=True) - 2.0 * jnp.sum(
        positive, axis=1, keepdims=True
    )
    text = near_texts(iota((1, 64), 1))
    first = near / rowsum - jnp.where(target == text, 2.0, 0.0)
    first_hi = first.astype(bf16).astype(f32)
    near_hi = near.astype(bf16).astype(f32)
    terms = jnp.concatenate([first_hi, first - first_hi, near_hi, near - near_hi], axis=1)
    sums = dot(terms.astype(bf16), videos, TN)
    first, second = sums[0:64] + sums[64:128], sums[128:192] + sums[192:256]
    cols = col_scr[...]
    total = jnp.broadcast_to(total, (8, 128))
    for k in range(4):
        for half in range(2):
            n = k * 2 + half
            step = k // 2 * 2 + other(xl, half)
            out_ref = send_ref if k % 2 else keep_ref
            out_ref[step, :, 0:E] = first[n * 8 : (n + 1) * 8]
            out_ref[step, :, E : 2 * E] = second[n * 8 : (n + 1) * 8]
            out_ref[step, :, 2 * E : 2 * E + TILE] = cols
            out_ref[step, :, 2 * E + TILE :] = total


def first_logits(*args):
    return pl.pallas_call(
        first_kernel,
        in_specs=[VMEM] * 8,
        out_specs=[VMEM] * 6,
        out_shape=[
            jax.ShapeDtypeStruct((8, 2 * SET), f32),
            jax.ShapeDtypeStruct((8, TILE), f32),
            jax.ShapeDtypeStruct((PLANE_ROWS, 128), f32),
            jax.ShapeDtypeStruct((1, TILE), f32),
            jax.ShapeDtypeStruct((8, E), f32),
            jax.ShapeDtypeStruct((8, 1), f32),
        ],
        scratch_shapes=[pltpu.VMEM((PLANE_ROWS, TILE), f32)],
        compiler_params=pltpu.CompilerParams(vmem_limit_bytes=16 << 20),
        cost_estimate=pl.CostEstimate(
            flops=2 * PLANE_ROWS * 1024 * E, bytes_accessed=2 << 20, transcendentals=1 << 18
        ),
    )(*args)


def second_logits(*args):
    return pl.pallas_call(
        second_kernel,
        in_specs=[VMEM] * 13,
        out_specs=[VMEM] * 3,
        out_shape=[
            jax.ShapeDtypeStruct((4, 8, SUMS), f32),
            jax.ShapeDtypeStruct((4, 8, SUMS), f32),
            jax.ShapeDtypeStruct((8, 2 * SET), f32),
        ],
        scratch_shapes=[pltpu.VMEM((PLANE_ROWS, TILE), f32), pltpu.VMEM((8, TILE), f32)],
        compiler_params=pltpu.CompilerParams(vmem_limit_bytes=16 << 20),
        cost_estimate=pl.CostEstimate(
            flops=2 * PLANE_ROWS * 1536 * E, bytes_accessed=4 << 20, transcendentals=1 << 18
        ),
    )(*args)


def add_kernel(keep_ref, got_ref, *out_refs):
    for k, out_ref in enumerate(out_refs):
        out_ref[...] = keep_ref[k] + got_ref[k]


def add_parts(keep, got):
    return pl.pallas_call(
        add_kernel,
        in_specs=[VMEM] * 2,
        out_specs=[VMEM] * 4,
        out_shape=[jax.ShapeDtypeStruct((8, SUMS), f32)] * 4,
        compiler_params=pltpu.CompilerParams(vmem_limit_bytes=16 << 20),
        cost_estimate=pl.CostEstimate(flops=1 << 16, bytes_accessed=1 << 19, transcendentals=0),
    )(keep, got)


def grad_kernel(
    part0_ref, part1_ref, part2_ref, part3_ref, own_ref, last_ref, target_ref,
    set0_ref, set1_ref, set2_ref, set3_ref, set4_ref, set5_ref, set6_ref, set7_ref,
    video_hat_ref, video_norm_ref, text_ref, loss_ref, video_grad_ref, text_grad_ref, col_scr,
):
    xh, c, xl, spot = position()
    got = (part0_ref[...] + part1_ref[...]) + (part2_ref[...] + part3_ref[...])
    cols = got[:, 2 * E : 2 * E + TILE]
    col_scr[...] = cols
    logs = jnp.sum(jnp.sum(jnp.log(cols), axis=0, keepdims=True), axis=1, keepdims=True)
    loss_ref[...] = (logs + got[0:1, 2 * E + TILE : 2 * E + TILE + 1]) / 4096.0

    def project(direction, hat, norm):
        return (direction - jnp.sum(direction * hat, axis=1, keepdims=True) * hat) / norm

    at = (xl * 32 + spot) * 4 + xh * 2
    lane = iota((4, TILE), 1) - at
    mine = jnp.where(c == 0, cols[0:4], cols[4:8])
    pair = [jnp.sum(jnp.where(lane == n, mine, 0.0), axis=1, keepdims=True) for n in range(2)]
    row = iota((8, 1), 0)
    mine = sum(
        jnp.where(row == n, pair[n % 2][n // 2 : n // 2 + 1], 0.0) for n in range(8)
    )
    text_dir = SCALE * (got[:, 0:E] + got[:, E : 2 * E] / mine)
    text_grad_ref[...] = project(text_dir, *unit_rows(text_ref[...].astype(f32)))

    rows = jnp.concatenate([own_ref[...], last_ref[...]], axis=1)
    rowsum = jnp.sum(rows, axis=1, keepdims=True)
    target = target_ref[pl.ds(pl.multiple_of((xl * 32 + spot) * 8, 8), 8), :]
    direction = jnp.zeros((8, E), f32)
    pieces = (set0_ref, set1_ref, set2_ref, set3_ref, set4_ref, set5_ref, set6_ref, set7_ref)
    for k, ref in enumerate(pieces):
        tile = tile_of(xh, c, xl, spot, k)
        ex = rows[:, k * TILE : (k + 1) * TILE]
        hot = jnp.where(target == texts_of(tile, iota((1, TILE), 1)), 2.0, 0.0)
        probe = ex / rowsum + ex / col_scr[pl.ds(tile, 1), :] - hot
        direction += dot(probe.astype(bf16), ref[...])
    video_grad_ref[...] = project(SCALE * direction, video_hat_ref[...], video_norm_ref[...])


def gradients(*args):
    return pl.pallas_call(
        grad_kernel,
        in_specs=[VMEM] * 18,
        out_specs=[VMEM] * 3,
        out_shape=[
            jax.ShapeDtypeStruct((1, 1), f32),
            jax.ShapeDtypeStruct((8, E), f32),
            jax.ShapeDtypeStruct((8, E), f32),
        ],
        scratch_shapes=[pltpu.VMEM((8, TILE), f32)],
        compiler_params=pltpu.CompilerParams(vmem_limit_bytes=12 << 20),
        cost_estimate=pl.CostEstimate(
            flops=2 * 8 * 2048 * E, bytes_accessed=5 << 20, transcendentals=2048
        ),
    )(*args)


def exchange(x, axes):
    return lax.all_to_all(x, axes, 0, 0, tiled=True)


def swap(x):
    return lax.ppermute(x, "c", [(0, 1), (1, 0)])


def along(x, step):
    return lax.ppermute(x, ("xh", "xl"), [(k, k ^ step) for k in range(4)])


def turn_y(x):
    return lax.ppermute(x, "y", [(k, k ^ 1) for k in range(4)])


def body(clip_tokens, clip_video, pool_vectors, out_proj, text_embed, pair_text):
    far_text = along(text_embed, 2)
    *sums, text_hat = clip_sums(
        clip_tokens, clip_video, pool_vectors, text_embed, pair_text
    )
    outgoing = pack(*sums, text_hat, far_text)
    arrived = exchange(outgoing.reshape(CLIPS, 8, SENT + PIECE), ROW)
    arrived = arrived.reshape(CLIPS * 8, SENT + PIECE)
    video_embed, video_hat, video_norm, send = embed(arrived, out_proj)
    texts, target, video_hat, video_norm = text_piece(arrived, video_hat, video_norm)
    moved = [turn_y(texts), along(texts, 3), along(texts, 1)]
    videos, moved[0] = lax.optimization_barrier((exchange(send, PLANE), moved[0]))
    videos = videos.reshape(PLANE_ROWS, E)
    mine = (texts, moved[2], moved[1], moved[0])
    theirs = tuple(swap(x) for x in mine)
    own, cols, sums, positive, video_hat, video_norm = first_logits(
        videos, target, *mine, video_hat, video_norm
    )
    keep, send, last = second_logits(videos, target, *mine, *theirs, cols, sums, positive)
    parts = add_parts(keep, swap(send))
    parts = [parts[0]] + [along(parts[step], step) for step in (2, 3, 1)]
    loss, video_grad, text_grad = gradients(
        *parts, own, last, target, *mine, *theirs, video_hat, video_norm, text_embed
    )
    return video_embed, video_grad, text_grad, loss.reshape(())


def solution(mesh):
    split = Mesh(mesh.devices.reshape(2, 2, 2, 8, 4), ALL)
    return jax.shard_map(
        body,
        mesh=split,
        in_specs=(P(ALL, None, None), P(ALL), P(), P(), P(ALL, None), P(ALL)),
        out_specs=(P(ALL, None), P(ALL, None), P(ALL, None), P()),
        check_vma=False,
    )
```

```python
import jax
import jax.numpy as jnp
from jax import lax
from jax.experimental import pallas as pl
from jax.experimental.pallas import tpu as pltpu
from jax.sharding import Mesh, PartitionSpec as P

H = 25
HD = 128
D = 3200
E = 768
TOK = 16
CLIPS = 64
SOFT_CAP = 20.0
SCALE = 40.0
EPS = 1e-06
ALL = ("xh", "c", "xl", "z", "y")
ROW = ("xl", "z", "y")
PLANE = ("z", "y")
CHUNK = 32
TOKS = CHUNK * TOK
STEPS = CLIPS // CHUNK
PARTS = 4
WIDE = 7
SENT = WIDE * HD
TAIL = 4 * HD
TILE = 256
SET = CLIPS * 8
PLANE_ROWS = 256
SUMS = 2 * E + TILE + 128
PIECE = E // 2
VMEM = pl.BlockSpec(memory_space=pltpu.VMEM)
f32 = jnp.float32
bf16 = jnp.bfloat16
NT = (((1,), (1,)), ((), ()))
TN = (((0,), (0,)), ((), ()))


def dot(a, b, dims=(((1,), (0,)), ((), ()))):
    return lax.dot_general(a, b, dims, preferred_element_type=f32)


def iota(shape, dim):
    return lax.broadcasted_iota(jnp.int32, shape, dim)


def column_of(row):
    n = row.shape[1]
    eye = iota((n, n), 0) == iota((n, n), 1)
    return jnp.sum(jnp.where(eye, jnp.broadcast_to(row, (n, n)), 0.0), axis=1, keepdims=True)


def unit_rows(values):
    norms = jnp.sqrt(jnp.sum(values * values, axis=1, keepdims=True) + EPS)
    return values / norms, norms


def label_of(xh, xl, y):
    return (2 * xh + xl + 2 * y) % 4


def clip_kernel(
    video_hbm, token_hbm, pool_hbm, text_hbm, pair_hbm,
    num_ref, slot_ref, code_ref, hat_ref,
    video_ref, token_ref, pool_ref, text_ref, pair_ref, weight_scr, sems,
):
    small = ((pool_hbm, pool_ref), (video_hbm, video_ref), (text_hbm, text_ref), (pair_hbm, pair_ref))
    chunks = [pl.ds(i * TOKS, TOKS) for i in range(STEPS)]
    loads = [
        pltpu.make_async_copy(token_hbm.at[chunk], token_ref.at[chunk], sems.at[i])
        for i, chunk in enumerate(chunks)
    ]
    early = [
        pltpu.make_async_copy(src, dst, sems.at[STEPS + i]) for i, (src, dst) in enumerate(small)
    ]
    early[0].start()
    loads[0].start()
    for copy in early[1:] + loads[1:]:
        copy.start()
    weight_scr[...] = jnp.zeros_like(weight_scr)
    num_ref[...] = jnp.zeros_like(num_ref)
    mine = iota((CHUNK, TOKS), 1) // TOK == iota((CHUNK, TOKS), 0)
    ones = mine.astype(f32).astype(bf16)
    lane = iota((CHUNK, HD), 1)
    for copy in early[1:]:
        copy.wait()
    videos = video_ref[...].astype(f32)
    hat_ref[...], _ = unit_rows(text_ref[...].astype(f32))
    early[0].wait()
    pool = pool_ref[...]

    def put(step, j, value):
        at = j // WIDE * CLIPS + step * CHUNK
        num_ref[at : at + CHUNK, j % WIDE * HD : (j % WIDE + 1) * HD] = value.astype(bf16)

    def weigh(step):
        loads[step].wait()
        scores = dot(pool, token_ref[chunks[step], :], NT)
        weights = jnp.exp(SOFT_CAP * jnp.tanh(scores / SOFT_CAP))
        weight_scr[step, 0:H, :] = weights
        weight_scr[step, 32 : 32 + H, :] = weights

    def total(step):
        den = dot(ones, weight_scr[step].astype(bf16), NT)
        den_hi = den.astype(bf16).astype(f32)
        here = iota((CHUNK, CLIPS), 1) == iota((CHUNK, CLIPS), 0) + step * CHUNK
        video = jnp.where(here, jnp.broadcast_to(videos, (CHUNK, CLIPS)), 0.0)
        video = jnp.sum(video, axis=1, keepdims=True).astype(jnp.int32)
        local = jnp.where(lane - 64 == video % 8, 1.0, 0.0)
        tail = jnp.where(lane < 32, den_hi, jnp.where(lane < 64, den - den_hi, local))
        put(step, H, tail)
        for h in range(0, H, 2):
            pair = range(h, min(h + 2, H))
            lhs = jnp.concatenate(
                [
                    jnp.where(
                        mine, jnp.broadcast_to(weight_scr[step, k : k + 1, :], (CHUNK, TOKS)), 0.0
                    )
                    for k in pair
                ],
                axis=0,
            ).astype(bf16)
            part = dot(lhs, token_ref[chunks[step], h * HD : (h + len(pair)) * HD])
            for n, k in enumerate(pair):
                put(step, k, part[n * CHUNK : (n + 1) * CHUNK, n * HD : (n + 1) * HD])

    for step in range(STEPS):
        weigh(step)
        if step:
            total(step - 1)
    total(STEPS - 1)

    owner = (video_ref[...] // 8).astype(f32)
    before = (column_of(owner) == owner) & (iota((CLIPS, CLIPS), 0) < iota((CLIPS, CLIPS), 1))
    rank = jnp.sum(jnp.where(before, 1.0, 0.0), axis=0, keepdims=True)
    slot = owner * 2.0 + rank
    slot_ref[...] = jnp.concatenate([slot] * PARTS, axis=1)
    pair = pair_ref[...]
    code_ref[...] = jnp.concatenate(
        [
            jnp.zeros((1, 72), f32),
            (pair // 64).astype(f32),
            (pair % 64).astype(f32),
            jnp.zeros((1, 40), f32),
        ],
        axis=1,
    )


def pack_kernel(num_ref, slot_ref, code_ref, hat_ref, far_ref, out_ref):
    xh = lax.axis_index("xh")
    shape = (CLIPS * 8, PARTS * CLIPS)
    row, col = iota(shape, 0), iota(shape, 1)
    place = (row // PARTS == slot_ref[...].astype(jnp.int32)) & (row % PARTS == col // CLIPS)
    out = dot(jnp.where(place, 1.0, 0.0).astype(bf16), num_ref[...])
    last = iota((CLIPS * 8, HD), 0) % PARTS == PARTS - 1
    out_ref[:, 0:TAIL] = out[:, 0:TAIL].astype(bf16)
    out_ref[:, TAIL : TAIL + HD] = (
        out[:, TAIL : TAIL + HD] + jnp.where(last, code_ref[...], 0.0)
    ).astype(bf16)
    out_ref[:, TAIL + HD : SENT] = out[:, TAIL + HD : SENT].astype(bf16)
    near = hat_ref[...]
    far, _ = unit_rows(far_ref[...].astype(f32))
    low = xh == 0
    texts = jnp.concatenate([jnp.where(low, near, far), jnp.where(low, far, near)], axis=0)
    row, col = iota((CLIPS * 8, 16), 0), iota((CLIPS * 8, 16), 1)
    dest = row // 8
    label = label_of(xh, dest // 32, dest % 4)
    pick = row % 4 // 2 * 8 + 2 * label + row % 2 == col
    texts = dot(jnp.where(pick, 1.0, 0.0).astype(bf16), texts.astype(bf16))
    upper = iota((CLIPS * 8, PIECE), 0) % 8 < 4
    out_ref[:, SENT : SENT + PIECE] = jnp.where(
        upper, texts[:, 0:PIECE], texts[:, PIECE:E]
    ).astype(bf16)


def pack(*args):
    return pl.pallas_call(
        pack_kernel,
        in_specs=[VMEM] * 5,
        out_specs=VMEM,
        out_shape=jax.ShapeDtypeStruct((CLIPS * 8, SENT + PIECE), bf16),
        compiler_params=pltpu.CompilerParams(vmem_limit_bytes=16 << 20),
        cost_estimate=pl.CostEstimate(
            flops=2 * 512 * 256 * SENT, bytes_accessed=2 << 20, transcendentals=0
        ),
    )(*args)


def clip_sums(clip_tokens, clip_video, pool_vectors, text_embed, pair_text):
    args = (
        clip_video.reshape(1, CLIPS),
        clip_tokens.reshape(CLIPS * TOK, D),
        pool_vectors,
        text_embed,
        pair_text.reshape(1, 8),
    )
    return pl.pallas_call(
        clip_kernel,
        in_specs=[pl.BlockSpec(memory_space=pltpu.HBM)] * 5,
        out_specs=[VMEM] * 4,
        out_shape=[
            jax.ShapeDtypeStruct((PARTS * CLIPS, SENT), bf16),
            jax.ShapeDtypeStruct((1, PARTS * CLIPS), f32),
            jax.ShapeDtypeStruct((1, HD), f32),
            jax.ShapeDtypeStruct((8, E), f32),
        ],
        scratch_shapes=[pltpu.VMEM(x.shape, x.dtype) for x in args]
        + [
            pltpu.VMEM((STEPS, 128, TOKS), f32),
            pltpu.SemaphoreType.DMA((STEPS + 4,)),
        ],
        compiler_params=pltpu.CompilerParams(vmem_limit_bytes=16 << 20),
        cost_estimate=pl.CostEstimate(
            flops=2 * 1024 * D * 64, bytes_accessed=8 << 20, transcendentals=1 << 17
        ),
    )(*(pltpu.with_memory_space_constraint(x, pltpu.HBM) for x in args))


def embed_kernel(
    arrived_ref, proj_ref, emb_ref, hat_ref, norm_ref, send_ref
):
    rows = CLIPS * 8
    tails = arrived_ref[:, TAIL : TAIL + HD]
    pick = jnp.where(iota((8, HD), 1) - 64 == iota((8, HD), 0), 1.0, 0.0).astype(bf16)
    hot = dot(pick, tails, NT)
    hot = jnp.where(iota((8, rows), 1) % PARTS == PARTS - 1, hot, 0.0)
    assign = jnp.concatenate(
        [hot if p == PARTS - 1 else pltpu.roll(hot, rows - (PARTS - 1 - p), 1) for p in range(PARTS)],
        axis=0,
    )
    sums = dot(assign.astype(bf16), arrived_ref[:, 0:SENT])

    def chunk(j):
        p, q = j // WIDE, j % WIDE
        return sums[p * 8 : (p + 1) * 8, q * HD : (q + 1) * HD]

    den = chunk(H)
    den = den[:, 0:32] + den[:, 32:64]
    pooled = jnp.concatenate([chunk(h) / den[:, h : h + 1] for h in range(H)], axis=1)
    hi = pooled.astype(bf16).astype(f32)
    mid = (pooled - hi).astype(bf16).astype(f32)
    low = pooled - hi - mid
    parts = dot(jnp.concatenate([hi, mid, low], axis=0).astype(bf16), proj_ref[...])
    emb = parts[0:8] + parts[8:16] + parts[16:24]
    emb_ref[...] = emb.astype(bf16)
    hat, norm = unit_rows(emb)
    hat_ref[...] = hat
    norm_ref[...] = norm
    hat_low = hat.astype(bf16)
    for k in range(32):
        send_ref[k] = hat_low


def embed(arrived, out_proj):
    return pl.pallas_call(
        embed_kernel,
        in_specs=[VMEM, VMEM],
        out_specs=[VMEM] * 4,
        out_shape=[
            jax.ShapeDtypeStruct((8, E), bf16),
            jax.ShapeDtypeStruct((8, E), f32),
            jax.ShapeDtypeStruct((8, 1), f32),
            jax.ShapeDtypeStruct((32, 8, E), bf16),
        ],
        compiler_params=pltpu.CompilerParams(vmem_limit_bytes=16 << 20),
        cost_estimate=pl.CostEstimate(
            flops=2 * 24 * D * E, bytes_accessed=6 << 20, transcendentals=0
        ),
    )(arrived, out_proj)


def text_kernel(arrived_ref, hat_ref, norm_ref, text_ref, target_ref, hat_out, norm_out):
    hat_out[...] = hat_ref[...]
    norm_out[...] = norm_ref[...]
    halves = arrived_ref[:, SENT : SENT + PIECE]
    row, col = iota((TILE, CLIPS * 8), 0), iota((TILE, CLIPS * 8), 1)
    for part in range(2):
        pick = row // 4 * 8 + part * 4 + row % 4 == col
        texts = dot(jnp.where(pick, 1.0, 0.0).astype(bf16), halves)
        text_ref[:, part * PIECE : (part + 1) * PIECE] = texts.astype(bf16)
    rows = CLIPS * 8
    code = arrived_ref[:, TAIL : TAIL + HD].astype(f32).reshape(CLIPS, 8, HD)[:, 3:4, :]
    code = jnp.broadcast_to(code, (CLIPS, 8, HD)).reshape(rows, HD)
    lane, own = iota((rows, HD), 1), iota((rows, HD), 0) % 8
    code = jnp.where(lane - 72 == own, 64.0 * code, jnp.where(lane - 80 == own, code, 0.0))
    target_ref[...] = jnp.sum(code, axis=1, keepdims=True)


def text_piece(*args):
    return pl.pallas_call(
        text_kernel,
        in_specs=[VMEM] * 3,
        out_specs=[VMEM] * 4,
        out_shape=[
            jax.ShapeDtypeStruct((TILE, E), bf16),
            jax.ShapeDtypeStruct((SET, 1), f32),
            jax.ShapeDtypeStruct((8, E), f32),
            jax.ShapeDtypeStruct((8, 1), f32),
        ],
        compiler_params=pltpu.CompilerParams(vmem_limit_bytes=16 << 20),
        cost_estimate=pl.CostEstimate(
            flops=4 * 256 * 512 * PIECE, bytes_accessed=1 << 20, transcendentals=0
        ),
    )(*args)


def position():
    xh, c, xl, z, y = (lax.axis_index(a) for a in ALL)
    return xh, c, xl, z * 4 + y


def other(a, flip):
    return a + flip - 2 * flip * a


def row_of(xh, c, k):
    return other(xh, k // 2) * 2 + other(c, k % 2)


def tile_of(xh, c, xl, spot, k):
    y = spot % 4
    label = (
        label_of(xh, xl, y),
        label_of(xh, 1 - xl, y),
        label_of(1 - xh, 1 - xl, y),
        label_of(xh, xl, y + 1),
    )[k % 4]
    return other(c, k // 4) * 4 + label


def texts_of(tile, j):
    row = j % 4 // 2 * 2 + tile // 4
    return ((row * 64 + j // 4) * 8 + tile % 4 * 2 + j % 2).astype(f32)


def score(videos, target, pieces, tiles, own_ref, tile_scr, cols_ref, sums, positive, base):
    for n, (ref, tile) in enumerate(zip(pieces, tiles)):
        logits = SCALE * dot(videos, ref[...], NT)
        ex = jnp.exp(logits)
        tile_scr[...] = ex
        cols_ref[pl.ds(tile, 1), :] = jnp.sum(ex, axis=0, keepdims=True)
        sums += ex[:, 0:128] + ex[:, 128:TILE]
        hit = target == texts_of(tile, iota((1, TILE), 1))
        positive += jnp.sum(jnp.where(hit, logits, 0.0), axis=0, keepdims=True)
        own_ref[:, n * TILE : (n + 1) * TILE] = tile_scr[pl.ds(base, 8), :]
    return sums, positive


def plane_rows(target_ref, xl):
    return target_ref[pl.ds(pl.multiple_of(xl * PLANE_ROWS, PLANE_ROWS), PLANE_ROWS), :]


def near_texts(slot, flip):
    xh, c, _, spot = position()
    group = sum(
        jnp.where(slot // 8 == n, row_of(xh, c, n // 2 * 2 + flip) * 2 + n % 2, 0)
        for n in range(4)
    )
    return ((group * 32 + spot) * 8 + slot % 8).astype(f32)


def near_exps(videos, pieces, tiles, flip):
    spot = position()[3]
    blocks = [
        ref[pl.ds(pl.multiple_of(half * 128 + spot // 4 * 16, 16), 16), :]
        for ref in pieces
        for half in range(2)
    ]
    col = iota((1, 128), 1)
    tile = sum(jnp.where(col // 32 == k, tiles[k], 0) for k in range(4))
    held = texts_of(tile, col % 32 // 16 * 128 + spot // 4 * 16 + col % 16)
    pick = near_texts(iota((32, 1), 0), flip) == held
    near = dot(jnp.where(pick, 1.0, 0.0).astype(bf16), jnp.concatenate(blocks, axis=0))
    return jnp.exp(SCALE * dot(videos, near.astype(bf16), NT))


def near_sums(near, rowsum, target, videos, flip, cols, total, out_ref):
    first = near / rowsum - jnp.where(target == near_texts(iota((1, 32), 1), flip), 2.0, 0.0)
    first_hi = first.astype(bf16).astype(f32)
    near_hi = near.astype(bf16).astype(f32)
    terms = jnp.concatenate([first_hi, first - first_hi, near_hi, near - near_hi], axis=1)
    sums = dot(terms.astype(bf16), videos, TN)
    first, second = sums[0:32] + sums[32:64], sums[64:96] + sums[96:128]
    xl = position()[2]
    for n in range(4):
        step = n // 2 * 2 + other(xl, n % 2)
        out_ref[step, :, 0:E] = first[n * 8 : (n + 1) * 8]
        out_ref[step, :, E : 2 * E] = second[n * 8 : (n + 1) * 8]
        out_ref[step, :, 2 * E : 2 * E + TILE] = cols
        out_ref[step, :, 2 * E + TILE :] = total


def first_kernel(
    video_ref, target_ref, set0_ref, set1_ref, set2_ref, set3_ref,
    own_ref, cols_ref, sums_ref, positive_ref, near_ref, tile_scr,
):
    xh, c, xl, spot = position()
    cols_ref[...] = jnp.zeros_like(cols_ref)
    videos = video_ref[...]
    pieces = (set0_ref, set1_ref, set2_ref, set3_ref)
    tiles = [tile_of(xh, c, xl, spot, k) for k in range(4)]
    sums_ref[...], positive_ref[...] = score(
        videos, plane_rows(target_ref, xl), pieces, tiles, own_ref, tile_scr, cols_ref,
        jnp.zeros((PLANE_ROWS, 128), f32), jnp.zeros((1, TILE), f32), pl.multiple_of(spot * 8, 8),
    )
    near_ref[...] = near_exps(videos, pieces, tiles, 0)


def second_kernel(
    video_ref, target_ref, set4_ref, set5_ref, set6_ref, set7_ref, cols_ref, sums_ref, positive_ref,
    send_ref, own_ref, rowsum_ref, cols_out, total_ref, tile_scr,
):
    xh, c, xl, spot = position()
    target = plane_rows(target_ref, xl)
    videos = video_ref[...]
    pieces = (set4_ref, set5_ref, set6_ref, set7_ref)
    tiles = [tile_of(xh, c, xl, spot, k) for k in range(4, 8)]
    cols_out[...] = cols_ref[...]
    sums, positive = score(
        videos, target, pieces, tiles, own_ref, tile_scr, cols_out,
        sums_ref[...], positive_ref[...], pl.multiple_of(spot * 8, 8),
    )
    near = near_exps(videos, pieces, tiles, 1)
    rowsum = jnp.sum(sums, axis=1, keepdims=True)
    rowsum_ref[...] = rowsum
    total = jnp.sum(jnp.log(rowsum), axis=0, keepdims=True) - 2.0 * jnp.sum(
        positive, axis=1, keepdims=True
    )
    total_ref[...] = jnp.broadcast_to(total, (8, 128))
    near_sums(near, rowsum, target, videos, 1, cols_out[...], total_ref[...], send_ref)


def keep_kernel(video_ref, target_ref, near_ref, rowsum_ref, cols_ref, total_ref, keep_ref):
    target = plane_rows(target_ref, position()[2])
    near_sums(
        near_ref[...], rowsum_ref[...], target, video_ref[...], 0, cols_ref[...], total_ref[...],
        keep_ref,
    )


def keep_sums(*args):
    return pl.pallas_call(
        keep_kernel,
        in_specs=[VMEM] * 6,
        out_specs=VMEM,
        out_shape=jax.ShapeDtypeStruct((4, 8, SUMS), f32),
        compiler_params=pltpu.CompilerParams(vmem_limit_bytes=16 << 20),
        cost_estimate=pl.CostEstimate(
            flops=2 * PLANE_ROWS * 128 * E, bytes_accessed=1 << 20, transcendentals=0
        ),
    )(*args)


def first_logits(*args):
    return pl.pallas_call(
        first_kernel,
        in_specs=[VMEM] * 6,
        out_specs=[VMEM] * 5,
        out_shape=[
            jax.ShapeDtypeStruct((8, 2 * SET), f32),
            jax.ShapeDtypeStruct((8, TILE), f32),
            jax.ShapeDtypeStruct((PLANE_ROWS, 128), f32),
            jax.ShapeDtypeStruct((1, TILE), f32),
            jax.ShapeDtypeStruct((PLANE_ROWS, 32), f32),
        ],
        scratch_shapes=[pltpu.VMEM((PLANE_ROWS, TILE), f32)],
        compiler_params=pltpu.CompilerParams(vmem_limit_bytes=16 << 20),
        cost_estimate=pl.CostEstimate(
            flops=2 * PLANE_ROWS * 1024 * E, bytes_accessed=2 << 20, transcendentals=1 << 18
        ),
    )(*args)


def second_logits(*args):
    return pl.pallas_call(
        second_kernel,
        in_specs=[VMEM] * 9,
        out_specs=[VMEM] * 5,
        out_shape=[
            jax.ShapeDtypeStruct((4, 8, SUMS), f32),
            jax.ShapeDtypeStruct((8, 2 * SET), f32),
            jax.ShapeDtypeStruct((PLANE_ROWS, 1), f32),
            jax.ShapeDtypeStruct((8, TILE), f32),
            jax.ShapeDtypeStruct((8, 128), f32),
        ],
        scratch_shapes=[pltpu.VMEM((PLANE_ROWS, TILE), f32)],
        compiler_params=pltpu.CompilerParams(vmem_limit_bytes=16 << 20),
        cost_estimate=pl.CostEstimate(
            flops=2 * PLANE_ROWS * 1536 * E, bytes_accessed=4 << 20, transcendentals=1 << 18
        ),
    )(*args)


def add_kernel(keep_ref, got_ref, *out_refs):
    for k, out_ref in enumerate(out_refs):
        out_ref[...] = keep_ref[k] + got_ref[k]


def add_parts(keep, got):
    return pl.pallas_call(
        add_kernel,
        in_specs=[VMEM] * 2,
        out_specs=[VMEM] * 4,
        out_shape=[jax.ShapeDtypeStruct((8, SUMS), f32)] * 4,
        compiler_params=pltpu.CompilerParams(vmem_limit_bytes=16 << 20),
        cost_estimate=pl.CostEstimate(flops=1 << 16, bytes_accessed=1 << 19, transcendentals=0),
    )(keep, got)


def grad_kernel(
    part0_ref, part1_ref, part2_ref, part3_ref, own_ref, last_ref, target_ref,
    set0_ref, set1_ref, set2_ref, set3_ref, set4_ref, set5_ref, set6_ref, set7_ref,
    video_hat_ref, video_norm_ref, text_ref, loss_ref, video_grad_ref, text_grad_ref, col_scr,
):
    xh, c, xl, spot = position()
    got = (part0_ref[...] + part1_ref[...]) + (part2_ref[...] + part3_ref[...])
    cols = got[:, 2 * E : 2 * E + TILE]
    col_scr[...] = cols
    logs = jnp.sum(jnp.sum(jnp.log(cols), axis=0, keepdims=True), axis=1, keepdims=True)
    loss_ref[...] = (logs + got[0:1, 2 * E + TILE : 2 * E + TILE + 1]) / 4096.0

    def project(direction, hat, norm):
        return (direction - jnp.sum(direction * hat, axis=1, keepdims=True) * hat) / norm

    at = (xl * 32 + spot) * 4 + xh * 2
    lane = iota((4, TILE), 1) - at
    mine = jnp.where(c == 0, cols[0:4], cols[4:8])
    pair = [jnp.sum(jnp.where(lane == n, mine, 0.0), axis=1, keepdims=True) for n in range(2)]
    row = iota((8, 1), 0)
    mine = sum(
        jnp.where(row == n, pair[n % 2][n // 2 : n // 2 + 1], 0.0) for n in range(8)
    )
    text_dir = SCALE * (got[:, 0:E] + got[:, E : 2 * E] / mine)
    text_grad_ref[...] = project(text_dir, *unit_rows(text_ref[...].astype(f32)))

    rows = jnp.concatenate([own_ref[...], last_ref[...]], axis=1)
    rowsum = jnp.sum(rows, axis=1, keepdims=True)
    target = target_ref[pl.ds(pl.multiple_of((xl * 32 + spot) * 8, 8), 8), :]
    direction = jnp.zeros((8, E), f32)
    pieces = (set0_ref, set1_ref, set2_ref, set3_ref, set4_ref, set5_ref, set6_ref, set7_ref)
    for k, ref in enumerate(pieces):
        tile = tile_of(xh, c, xl, spot, k)
        ex = rows[:, k * TILE : (k + 1) * TILE]
        hot = jnp.where(target == texts_of(tile, iota((1, TILE), 1)), 2.0, 0.0)
        probe = ex / rowsum + ex / col_scr[pl.ds(tile, 1), :] - hot
        direction += dot(probe.astype(bf16), ref[...])
    video_grad_ref[...] = project(SCALE * direction, video_hat_ref[...], video_norm_ref[...])


def gradients(*args):
    return pl.pallas_call(
        grad_kernel,
        in_specs=[VMEM] * 18,
        out_specs=[VMEM] * 3,
        out_shape=[
            jax.ShapeDtypeStruct((1, 1), f32),
            jax.ShapeDtypeStruct((8, E), f32),
            jax.ShapeDtypeStruct((8, E), f32),
        ],
        scratch_shapes=[pltpu.VMEM((8, TILE), f32)],
        compiler_params=pltpu.CompilerParams(vmem_limit_bytes=12 << 20),
        cost_estimate=pl.CostEstimate(
            flops=2 * 8 * 2048 * E, bytes_accessed=5 << 20, transcendentals=2048
        ),
    )(*args)


def exchange(x, axes):
    return lax.all_to_all(x, axes, 0, 0, tiled=True)


def swap(x):
    return lax.ppermute(x, "c", [(0, 1), (1, 0)])


def along(x, step):
    return lax.ppermute(x, ("xh", "xl"), [(k, k ^ step) for k in range(4)])


def turn_y(x):
    return lax.ppermute(x, "y", [(k, k ^ 1) for k in range(4)])


def body(clip_tokens, clip_video, pool_vectors, out_proj, text_embed, pair_text):
    far_text = along(text_embed, 2)
    *sums, text_hat = clip_sums(
        clip_tokens, clip_video, pool_vectors, text_embed, pair_text
    )
    outgoing = pack(*sums, text_hat, far_text)
    arrived = exchange(outgoing.reshape(CLIPS, 8, SENT + PIECE), ROW)
    arrived = arrived.reshape(CLIPS * 8, SENT + PIECE)
    video_embed, video_hat, video_norm, send = embed(arrived, out_proj)
    texts, target, video_hat, video_norm = text_piece(arrived, video_hat, video_norm)
    moved = [turn_y(texts), along(texts, 3), along(texts, 1)]
    videos, moved[0] = lax.optimization_barrier((exchange(send, PLANE), moved[0]))
    videos = videos.reshape(PLANE_ROWS, E)
    mine = (texts, moved[2], moved[1], moved[0])
    theirs = tuple(swap(x) for x in mine)
    own, cols, sums, positive, near = first_logits(videos, target, *mine)
    send, last, rowsum, cols, total = second_logits(videos, target, *theirs, cols, sums, positive)
    keep = keep_sums(videos, target, near, rowsum, cols, total)
    parts = add_parts(keep, swap(send))
    parts = [parts[0]] + [along(parts[step], step) for step in (2, 3, 1)]
    loss, video_grad, text_grad = gradients(
        *parts, own, last, target, *mine, *theirs, video_hat, video_norm, text_embed
    )
    return video_embed, video_grad, text_grad, loss.reshape(())


def solution(mesh):
    split = Mesh(mesh.devices.reshape(2, 2, 2, 8, 4), ALL)
    return jax.shard_map(
        body,
        mesh=split,
        in_specs=(P(ALL, None, None), P(ALL), P(), P(), P(ALL, None), P(ALL)),
        out_specs=(P(ALL, None), P(ALL, None), P(ALL, None), P()),
        check_vma=False,
    )
```

```python
import jax
import jax.numpy as jnp
from jax import lax
from jax.experimental import pallas as pl
from jax.experimental.pallas import tpu as pltpu
from jax.sharding import Mesh, PartitionSpec as P

H = 25
HD = 128
D = 3200
E = 768
TOK = 16
CLIPS = 64
SOFT_CAP = 20.0
SCALE = 40.0
EPS = 1e-06
ALL = ("xh", "c", "xl", "z", "y")
ROW = ("xl", "z", "y")
PLANE = ("z", "y")
CHUNK = 32
TOKS = CHUNK * TOK
STEPS = CLIPS // CHUNK
PARTS = 4
WIDE = 7
SENT = WIDE * HD
TAIL = 4 * HD
TILE = 256
SET = CLIPS * 8
PLANE_ROWS = 256
SUMS = 2 * E + TILE + 128
PIECE = E // 2
VMEM = pl.BlockSpec(memory_space=pltpu.VMEM)
f32 = jnp.float32
bf16 = jnp.bfloat16
NT = (((1,), (1,)), ((), ()))
TN = (((0,), (0,)), ((), ()))


def dot(a, b, dims=(((1,), (0,)), ((), ()))):
    return lax.dot_general(a, b, dims, preferred_element_type=f32)


def iota(shape, dim):
    return lax.broadcasted_iota(jnp.int32, shape, dim)


def column_of(row):
    n = row.shape[1]
    eye = iota((n, n), 0) == iota((n, n), 1)
    return jnp.sum(jnp.where(eye, jnp.broadcast_to(row, (n, n)), 0.0), axis=1, keepdims=True)


def unit_rows(values):
    norms = jnp.sqrt(jnp.sum(values * values, axis=1, keepdims=True) + EPS)
    return values / norms, norms


def label_of(xh, xl, y):
    return (2 * xh + xl + 2 * y) % 4


def clip_kernel(
    video_hbm, token_hbm, pool_hbm, text_hbm, pair_hbm,
    num_ref, slot_ref, code_ref, hat_ref,
    video_ref, token_ref, pool_ref, text_ref, pair_ref, weight_scr, sems,
):
    small = ((pool_hbm, pool_ref), (video_hbm, video_ref), (text_hbm, text_ref), (pair_hbm, pair_ref))
    chunks = [pl.ds(i * TOKS, TOKS) for i in range(STEPS)]
    loads = [
        pltpu.make_async_copy(token_hbm.at[chunk], token_ref.at[chunk], sems.at[i])
        for i, chunk in enumerate(chunks)
    ]
    early = [
        pltpu.make_async_copy(src, dst, sems.at[STEPS + i]) for i, (src, dst) in enumerate(small)
    ]
    early[0].start()
    loads[0].start()
    for copy in early[1:] + loads[1:]:
        copy.start()
    weight_scr[...] = jnp.zeros_like(weight_scr)
    num_ref[...] = jnp.zeros_like(num_ref)
    mine = iota((CHUNK, TOKS), 1) // TOK == iota((CHUNK, TOKS), 0)
    ones = mine.astype(f32).astype(bf16)
    lane = iota((CHUNK, HD), 1)
    for copy in early[1:]:
        copy.wait()
    videos = video_ref[...].astype(f32)
    hat_ref[...], _ = unit_rows(text_ref[...].astype(f32))
    early[0].wait()
    pool = pool_ref[...]

    def put(step, j, value):
        at = j // WIDE * CLIPS + step * CHUNK
        num_ref[at : at + CHUNK, j % WIDE * HD : (j % WIDE + 1) * HD] = value.astype(bf16)

    def weigh(step):
        loads[step].wait()
        scores = dot(pool, token_ref[chunks[step], :], NT)
        weights = jnp.exp(SOFT_CAP * jnp.tanh(scores / SOFT_CAP))
        weight_scr[step, 0:H, :] = weights
        weight_scr[step, 32 : 32 + H, :] = weights

    def total(step):
        den = dot(ones, weight_scr[step].astype(bf16), NT)
        den_hi = den.astype(bf16).astype(f32)
        here = iota((CHUNK, CLIPS), 1) == iota((CHUNK, CLIPS), 0) + step * CHUNK
        video = jnp.where(here, jnp.broadcast_to(videos, (CHUNK, CLIPS)), 0.0)
        video = jnp.sum(video, axis=1, keepdims=True).astype(jnp.int32)
        local = jnp.where((lane < 96) & (lane % 8 == video % 8), 1.0, 0.0)
        tail = jnp.where(lane < 32, den_hi, jnp.where(lane < 64, den - den_hi, local))
        put(step, H, tail)
        for h in range(0, H, 2):
            pair = range(h, min(h + 2, H))
            lhs = jnp.concatenate(
                [
                    jnp.where(
                        mine, jnp.broadcast_to(weight_scr[step, k : k + 1, :], (CHUNK, TOKS)), 0.0
                    )
                    for k in pair
                ],
                axis=0,
            ).astype(bf16)
            part = dot(lhs, token_ref[chunks[step], h * HD : (h + len(pair)) * HD])
            for n, k in enumerate(pair):
                put(step, k, part[n * CHUNK : (n + 1) * CHUNK, n * HD : (n + 1) * HD])

    for step in range(STEPS):
        weigh(step)
        if step:
            total(step - 1)
    total(STEPS - 1)

    owner = (video_ref[...] // 8).astype(f32)
    before = (column_of(owner) == owner) & (iota((CLIPS, CLIPS), 0) < iota((CLIPS, CLIPS), 1))
    rank = jnp.sum(jnp.where(before, 1.0, 0.0), axis=0, keepdims=True)
    slot = owner * 2.0 + rank
    slot_ref[...] = jnp.concatenate([slot] * PARTS, axis=1)
    pair = pair_ref[...]
    code_ref[...] = jnp.concatenate(
        [
            jnp.zeros((1, 96), f32),
            (pair // 64).astype(f32),
            (pair % 64).astype(f32),
            jnp.zeros((1, 16), f32),
        ],
        axis=1,
    )


def pack_kernel(num_ref, slot_ref, code_ref, hat_ref, far_ref, out_ref):
    xh = lax.axis_index("xh")
    shape = (CLIPS * 8, PARTS * CLIPS)
    row, col = iota(shape, 0), iota(shape, 1)
    place = (row // PARTS == slot_ref[...].astype(jnp.int32)) & (row % PARTS == col // CLIPS)
    out = dot(jnp.where(place, 1.0, 0.0).astype(bf16), num_ref[...])
    last = iota((CLIPS * 8, HD), 0) % PARTS == PARTS - 1
    out_ref[:, 0:TAIL] = out[:, 0:TAIL].astype(bf16)
    out_ref[:, TAIL : TAIL + HD] = (
        out[:, TAIL : TAIL + HD] + jnp.where(last, code_ref[...], 0.0)
    ).astype(bf16)
    out_ref[:, TAIL + HD : SENT] = out[:, TAIL + HD : SENT].astype(bf16)
    near = hat_ref[...]
    far, _ = unit_rows(far_ref[...].astype(f32))
    low = xh == 0
    texts = jnp.concatenate([jnp.where(low, near, far), jnp.where(low, far, near)], axis=0)
    row, col = iota((CLIPS * 8, 16), 0), iota((CLIPS * 8, 16), 1)
    dest = row // 8
    label = label_of(xh, dest // 32, dest % 4)
    pick = row % 4 // 2 * 8 + 2 * label + row % 2 == col
    texts = dot(jnp.where(pick, 1.0, 0.0).astype(bf16), texts.astype(bf16))
    upper = iota((CLIPS * 8, PIECE), 0) % 8 < 4
    out_ref[:, SENT : SENT + PIECE] = jnp.where(
        upper, texts[:, 0:PIECE], texts[:, PIECE:E]
    ).astype(bf16)


def pack(*args):
    return pl.pallas_call(
        pack_kernel,
        in_specs=[VMEM] * 5,
        out_specs=VMEM,
        out_shape=jax.ShapeDtypeStruct((CLIPS * 8, SENT + PIECE), bf16),
        compiler_params=pltpu.CompilerParams(vmem_limit_bytes=16 << 20),
        cost_estimate=pl.CostEstimate(
            flops=2 * 512 * 256 * SENT, bytes_accessed=2 << 20, transcendentals=0
        ),
    )(*args)


def clip_sums(clip_tokens, clip_video, pool_vectors, text_embed, pair_text):
    args = (
        clip_video.reshape(1, CLIPS),
        clip_tokens.reshape(CLIPS * TOK, D),
        pool_vectors,
        text_embed,
        pair_text.reshape(1, 8),
    )
    return pl.pallas_call(
        clip_kernel,
        in_specs=[pl.BlockSpec(memory_space=pltpu.HBM)] * 5,
        out_specs=[VMEM] * 4,
        out_shape=[
            jax.ShapeDtypeStruct((PARTS * CLIPS, SENT), bf16),
            jax.ShapeDtypeStruct((1, PARTS * CLIPS), f32),
            jax.ShapeDtypeStruct((1, HD), f32),
            jax.ShapeDtypeStruct((8, E), f32),
        ],
        scratch_shapes=[pltpu.VMEM(x.shape, x.dtype) for x in args]
        + [
            pltpu.VMEM((STEPS, 128, TOKS), f32),
            pltpu.SemaphoreType.DMA((STEPS + 4,)),
        ],
        compiler_params=pltpu.CompilerParams(vmem_limit_bytes=16 << 20),
        cost_estimate=pl.CostEstimate(
            flops=2 * 1024 * D * 64, bytes_accessed=8 << 20, transcendentals=1 << 17
        ),
    )(*(pltpu.with_memory_space_constraint(x, pltpu.HBM) for x in args))


def embed_kernel(
    arrived_ref, proj_ref, emb_ref, hat_ref, norm_ref, send_ref
):
    rows = CLIPS * 8
    tails = arrived_ref[:, TAIL : TAIL + HD].astype(f32).reshape(CLIPS, 8, HD)
    upper = iota((CLIPS, 8, HD), 1) < 4
    hot = jnp.where(upper, tails[:, 3:4, :], tails[:, 7:8, :]).reshape(rows, HD)
    lane, row = iota((rows, HD), 1), iota((rows, HD), 0)
    hot = jnp.where(lane // 8 == 8 + row % PARTS, hot, 0.0)
    sums = dot(hot.astype(bf16), arrived_ref[:, 0:SENT], TN)

    def chunk(j):
        p, q = j // WIDE, j % WIDE
        return sums[64 + p * 8 : 72 + p * 8, q * HD : (q + 1) * HD]

    den = chunk(H)
    den = den[:, 0:32] + den[:, 32:64]
    pooled = jnp.concatenate([chunk(h) / den[:, h : h + 1] for h in range(H)], axis=1)
    hi = pooled.astype(bf16).astype(f32)
    mid = (pooled - hi).astype(bf16).astype(f32)
    low = pooled - hi - mid
    parts = dot(jnp.concatenate([hi, mid, low], axis=0).astype(bf16), proj_ref[...])
    emb = parts[0:8] + parts[8:16] + parts[16:24]
    emb_ref[...] = emb.astype(bf16)
    hat, norm = unit_rows(emb)
    hat_ref[...] = hat
    norm_ref[...] = norm
    hat_low = hat.astype(bf16)
    for k in range(32):
        send_ref[k] = hat_low


def embed(arrived, out_proj):
    return pl.pallas_call(
        embed_kernel,
        in_specs=[VMEM, VMEM],
        out_specs=[VMEM] * 4,
        out_shape=[
            jax.ShapeDtypeStruct((8, E), bf16),
            pltpu.HBM((8, E), f32),
            jax.ShapeDtypeStruct((8, 1), f32),
            jax.ShapeDtypeStruct((32, 8, E), bf16),
        ],
        compiler_params=pltpu.CompilerParams(vmem_limit_bytes=16 << 20),
        cost_estimate=pl.CostEstimate(
            flops=2 * 24 * D * E, bytes_accessed=6 << 20, transcendentals=0
        ),
    )(arrived, out_proj)


def text_kernel(arrived_ref, text_ref, target_ref):
    halves = arrived_ref[:, SENT : SENT + PIECE]
    row, col = iota((TILE, CLIPS * 8), 0), iota((TILE, CLIPS * 8), 1)
    for part in range(2):
        pick = row // 4 * 8 + part * 4 + row % 4 == col
        texts = dot(jnp.where(pick, 1.0, 0.0).astype(bf16), halves)
        text_ref[:, part * PIECE : (part + 1) * PIECE] = texts.astype(bf16)
    rows = CLIPS * 8
    code = arrived_ref[:, TAIL : TAIL + HD].astype(f32).reshape(CLIPS, 8, HD)[:, 3:4, :]
    code = jnp.broadcast_to(code, (CLIPS, 8, HD)).reshape(rows, HD)
    lane, own = iota((rows, HD), 1), iota((rows, HD), 0) % 8
    code = jnp.where(lane - 96 == own, 64.0 * code, jnp.where(lane - 104 == own, code, 0.0))
    target_ref[...] = jnp.sum(code, axis=1, keepdims=True)


def text_piece(*args):
    return pl.pallas_call(
        text_kernel,
        in_specs=[VMEM],
        out_specs=[VMEM] * 2,
        out_shape=[
            jax.ShapeDtypeStruct((TILE, E), bf16),
            jax.ShapeDtypeStruct((SET, 1), f32),
        ],
        compiler_params=pltpu.CompilerParams(vmem_limit_bytes=16 << 20),
        cost_estimate=pl.CostEstimate(
            flops=4 * 256 * 512 * PIECE, bytes_accessed=1 << 20, transcendentals=0
        ),
    )(*args)


def position():
    xh, c, xl, z, y = (lax.axis_index(a) for a in ALL)
    return xh, c, xl, z * 4 + y


def other(a, flip):
    return a + flip - 2 * flip * a


def row_of(xh, c, k):
    return other(xh, k // 2) * 2 + other(c, k % 2)


def tile_of(xh, c, xl, spot, k):
    y = spot % 4
    label = (
        label_of(xh, xl, y),
        label_of(xh, 1 - xl, y),
        label_of(1 - xh, 1 - xl, y),
        label_of(xh, xl, y + 1),
    )[k % 4]
    return other(c, k // 4) * 4 + label


def texts_of(tile, j):
    row = j % 4 // 2 * 2 + tile // 4
    return ((row * 64 + j // 4) * 8 + tile % 4 * 2 + j % 2).astype(f32)


def score(videos, target, pieces, tiles, own_ref, tile_scr, cols_ref, sums, positive, base):
    for n, (ref, tile) in enumerate(zip(pieces, tiles)):
        logits = SCALE * dot(videos, ref[...], NT)
        ex = jnp.exp(logits)
        tile_scr[...] = ex
        cols_ref[pl.ds(tile, 1), :] = jnp.sum(ex, axis=0, keepdims=True)
        sums += ex[:, 0:128] + ex[:, 128:TILE]
        hit = target == texts_of(tile, iota((1, TILE), 1))
        positive += jnp.sum(jnp.where(hit, logits, 0.0), axis=0, keepdims=True)
        own_ref[:, n * TILE : (n + 1) * TILE] = tile_scr[pl.ds(base, 8), :]
    return sums, positive


def plane_rows(target_ref, xl):
    return target_ref[pl.ds(pl.multiple_of(xl * PLANE_ROWS, PLANE_ROWS), PLANE_ROWS), :]


def near_texts(slot, flip):
    xh, c, _, spot = position()
    group = sum(
        jnp.where(slot // 8 == n, row_of(xh, c, n // 2 * 2 + flip) * 2 + n % 2, 0)
        for n in range(4)
    )
    return ((group * 32 + spot) * 8 + slot % 8).astype(f32)


def near_exps(videos, pieces, tiles, flip):
    spot = position()[3]
    blocks = [
        ref[pl.ds(pl.multiple_of(half * 128 + spot // 4 * 16, 16), 16), :]
        for ref in pieces
        for half in range(2)
    ]
    col = iota((1, 128), 1)
    tile = sum(jnp.where(col // 32 == k, tiles[k], 0) for k in range(4))
    held = texts_of(tile, col % 32 // 16 * 128 + spot // 4 * 16 + col % 16)
    pick = near_texts(iota((32, 1), 0), flip) == held
    near = dot(jnp.where(pick, 1.0, 0.0).astype(bf16), jnp.concatenate(blocks, axis=0))
    return jnp.exp(SCALE * dot(videos, near.astype(bf16), NT))


def near_sums(near, rowsum, target, videos, flip, cols, total, out_ref):
    first = near / rowsum - jnp.where(target == near_texts(iota((1, 32), 1), flip), 2.0, 0.0)
    first_hi = first.astype(bf16).astype(f32)
    near_hi = near.astype(bf16).astype(f32)
    terms = jnp.concatenate([first_hi, first - first_hi, near_hi, near - near_hi], axis=1)
    sums = dot(terms.astype(bf16), videos, TN)
    first, second = sums[0:32] + sums[32:64], sums[64:96] + sums[96:128]
    xl = position()[2]
    for n in range(4):
        step = n // 2 * 2 + other(xl, n % 2)
        out_ref[step, :, 0:E] = first[n * 8 : (n + 1) * 8]
        out_ref[step, :, E : 2 * E] = second[n * 8 : (n + 1) * 8]
        out_ref[step, :, 2 * E : 2 * E + TILE] = cols
        out_ref[step, :, 2 * E + TILE :] = total


def first_kernel(
    video_ref, target_ref, set0_ref, set1_ref, set2_ref, set3_ref,
    own_ref, cols_ref, sums_ref, positive_ref, near_ref, tile_scr,
):
    xh, c, xl, spot = position()
    cols_ref[...] = jnp.zeros_like(cols_ref)
    videos = video_ref[...]
    pieces = (set0_ref, set1_ref, set2_ref, set3_ref)
    tiles = [tile_of(xh, c, xl, spot, k) for k in range(4)]
    sums_ref[...], positive_ref[...] = score(
        videos, plane_rows(target_ref, xl), pieces, tiles, own_ref, tile_scr, cols_ref,
        jnp.zeros((PLANE_ROWS, 128), f32), jnp.zeros((1, TILE), f32), pl.multiple_of(spot * 8, 8),
    )
    near_ref[...] = near_exps(videos, pieces, tiles, 0)


def second_kernel(
    video_ref, target_ref, set4_ref, set5_ref, set6_ref, set7_ref, cols_ref, sums_ref, positive_ref,
    send_ref, own_ref, rowsum_ref, cols_out, total_ref, tile_scr,
):
    xh, c, xl, spot = position()
    target = plane_rows(target_ref, xl)
    videos = video_ref[...]
    pieces = (set4_ref, set5_ref, set6_ref, set7_ref)
    tiles = [tile_of(xh, c, xl, spot, k) for k in range(4, 8)]
    cols_out[...] = cols_ref[...]
    sums, positive = score(
        videos, target, pieces, tiles, own_ref, tile_scr, cols_out,
        sums_ref[...], positive_ref[...], pl.multiple_of(spot * 8, 8),
    )
    near = near_exps(videos, pieces, tiles, 1)
    rowsum = jnp.sum(sums, axis=1, keepdims=True)
    rowsum_ref[...] = rowsum
    total = jnp.sum(jnp.log(rowsum), axis=0, keepdims=True) - 2.0 * jnp.sum(
        positive, axis=1, keepdims=True
    )
    total_ref[...] = jnp.broadcast_to(total, (8, 128))
    near_sums(near, rowsum, target, videos, 1, cols_out[...], total_ref[...], send_ref)


def keep_kernel(video_ref, target_ref, near_ref, rowsum_ref, cols_ref, total_ref, keep_ref):
    target = plane_rows(target_ref, position()[2])
    near_sums(
        near_ref[...], rowsum_ref[...], target, video_ref[...], 0, cols_ref[...], total_ref[...],
        keep_ref,
    )


def keep_sums(*args):
    return pl.pallas_call(
        keep_kernel,
        in_specs=[VMEM] * 6,
        out_specs=VMEM,
        out_shape=jax.ShapeDtypeStruct((4, 8, SUMS), f32),
        compiler_params=pltpu.CompilerParams(vmem_limit_bytes=16 << 20),
        cost_estimate=pl.CostEstimate(
            flops=2 * PLANE_ROWS * 128 * E, bytes_accessed=1 << 20, transcendentals=0
        ),
    )(*args)


def first_logits(*args):
    return pl.pallas_call(
        first_kernel,
        in_specs=[VMEM] * 6,
        out_specs=[VMEM] * 5,
        out_shape=[
            jax.ShapeDtypeStruct((8, 2 * SET), f32),
            jax.ShapeDtypeStruct((8, TILE), f32),
            jax.ShapeDtypeStruct((PLANE_ROWS, 128), f32),
            jax.ShapeDtypeStruct((1, TILE), f32),
            jax.ShapeDtypeStruct((PLANE_ROWS, 32), f32),
        ],
        scratch_shapes=[pltpu.VMEM((PLANE_ROWS, TILE), f32)],
        compiler_params=pltpu.CompilerParams(vmem_limit_bytes=16 << 20),
        cost_estimate=pl.CostEstimate(
            flops=2 * PLANE_ROWS * 1024 * E, bytes_accessed=2 << 20, transcendentals=1 << 18
        ),
    )(*args)


def second_logits(*args):
    return pl.pallas_call(
        second_kernel,
        in_specs=[VMEM] * 9,
        out_specs=[VMEM] * 5,
        out_shape=[
            jax.ShapeDtypeStruct((4, 8, SUMS), f32),
            jax.ShapeDtypeStruct((8, 2 * SET), f32),
            jax.ShapeDtypeStruct((PLANE_ROWS, 1), f32),
            jax.ShapeDtypeStruct((8, TILE), f32),
            jax.ShapeDtypeStruct((8, 128), f32),
        ],
        scratch_shapes=[pltpu.VMEM((PLANE_ROWS, TILE), f32)],
        compiler_params=pltpu.CompilerParams(vmem_limit_bytes=16 << 20),
        cost_estimate=pl.CostEstimate(
            flops=2 * PLANE_ROWS * 1536 * E, bytes_accessed=4 << 20, transcendentals=1 << 18
        ),
    )(*args)


def add_kernel(keep_ref, got_ref, *out_refs):
    for k, out_ref in enumerate(out_refs):
        out_ref[...] = keep_ref[k] + got_ref[k]


def add_parts(keep, got):
    return pl.pallas_call(
        add_kernel,
        in_specs=[VMEM] * 2,
        out_specs=[VMEM] * 4,
        out_shape=[jax.ShapeDtypeStruct((8, SUMS), f32)] * 4,
        compiler_params=pltpu.CompilerParams(vmem_limit_bytes=16 << 20),
        cost_estimate=pl.CostEstimate(flops=1 << 16, bytes_accessed=1 << 19, transcendentals=0),
    )(keep, got)


def grad_kernel(
    part0_ref, part1_ref, part2_ref, part3_ref, own_ref, last_ref, target_ref,
    set0_ref, set1_ref, set2_ref, set3_ref, set4_ref, set5_ref, set6_ref, set7_ref,
    video_hat_ref, video_norm_ref, text_ref, loss_ref, video_grad_ref, text_grad_ref, col_scr,
):
    xh, c, xl, spot = position()
    got = (part0_ref[...] + part1_ref[...]) + (part2_ref[...] + part3_ref[...])
    cols = got[:, 2 * E : 2 * E + TILE]
    col_scr[...] = cols
    logs = jnp.sum(jnp.sum(jnp.log(cols), axis=0, keepdims=True), axis=1, keepdims=True)
    loss_ref[...] = (logs + got[0:1, 2 * E + TILE : 2 * E + TILE + 1]) / 4096.0

    def project(direction, hat, norm):
        return (direction - jnp.sum(direction * hat, axis=1, keepdims=True) * hat) / norm

    at = (xl * 32 + spot) * 4 + xh * 2
    lane = iota((4, TILE), 1) - at
    mine = jnp.where(c == 0, cols[0:4], cols[4:8])
    pair = [jnp.sum(jnp.where(lane == n, mine, 0.0), axis=1, keepdims=True) for n in range(2)]
    row = iota((8, 1), 0)
    mine = sum(
        jnp.where(row == n, pair[n % 2][n // 2 : n // 2 + 1], 0.0) for n in range(8)
    )
    text_dir = SCALE * (got[:, 0:E] + got[:, E : 2 * E] / mine)
    text_grad_ref[...] = project(text_dir, *unit_rows(text_ref[...].astype(f32)))

    rows = jnp.concatenate([own_ref[...], last_ref[...]], axis=1)
    rowsum = jnp.sum(rows, axis=1, keepdims=True)
    target = target_ref[pl.ds(pl.multiple_of((xl * 32 + spot) * 8, 8), 8), :]
    direction = jnp.zeros((8, E), f32)
    pieces = (set0_ref, set1_ref, set2_ref, set3_ref, set4_ref, set5_ref, set6_ref, set7_ref)
    for k, ref in enumerate(pieces):
        tile = tile_of(xh, c, xl, spot, k)
        ex = rows[:, k * TILE : (k + 1) * TILE]
        hot = jnp.where(target == texts_of(tile, iota((1, TILE), 1)), 2.0, 0.0)
        probe = ex / rowsum + ex / col_scr[pl.ds(tile, 1), :] - hot
        direction += dot(probe.astype(bf16), ref[...])
    video_grad_ref[...] = project(SCALE * direction, video_hat_ref[...], video_norm_ref[...])


def gradients(*args):
    return pl.pallas_call(
        grad_kernel,
        in_specs=[VMEM] * 18,
        out_specs=[VMEM] * 3,
        out_shape=[
            jax.ShapeDtypeStruct((1, 1), f32),
            jax.ShapeDtypeStruct((8, E), f32),
            jax.ShapeDtypeStruct((8, E), f32),
        ],
        scratch_shapes=[pltpu.VMEM((8, TILE), f32)],
        compiler_params=pltpu.CompilerParams(vmem_limit_bytes=12 << 20),
        cost_estimate=pl.CostEstimate(
            flops=2 * 8 * 2048 * E, bytes_accessed=5 << 20, transcendentals=2048
        ),
    )(*args)


def exchange(x, axes):
    return lax.all_to_all(x, axes, 0, 0, tiled=True)


def swap(x):
    return lax.ppermute(x, "c", [(0, 1), (1, 0)])


def along(x, step):
    return lax.ppermute(x, ("xh", "xl"), [(k, k ^ step) for k in range(4)])


def turn_y(x):
    return lax.ppermute(x, "y", [(k, k ^ 1) for k in range(4)])


def body(clip_tokens, clip_video, pool_vectors, out_proj, text_embed, pair_text):
    far_text = along(text_embed, 2)
    *sums, text_hat = clip_sums(
        clip_tokens, clip_video, pool_vectors, text_embed, pair_text
    )
    outgoing = pack(*sums, text_hat, far_text)
    arrived = exchange(outgoing.reshape(CLIPS, 8, SENT + PIECE), ROW)
    arrived = arrived.reshape(CLIPS * 8, SENT + PIECE)
    video_embed, video_hat, video_norm, send = embed(arrived, out_proj)
    texts, target = text_piece(arrived)
    moved = [turn_y(texts), along(texts, 3), along(texts, 1)]
    videos, moved[0] = lax.optimization_barrier((exchange(send, PLANE), moved[0]))
    videos = videos.reshape(PLANE_ROWS, E)
    mine = (texts, moved[2], moved[1], moved[0])
    theirs = tuple(swap(x) for x in mine)
    own, cols, sums, positive, near = first_logits(videos, target, *mine)
    send, last, rowsum, cols, total = second_logits(videos, target, *theirs, cols, sums, positive)
    keep = keep_sums(videos, target, near, rowsum, cols, total)
    parts = add_parts(keep, swap(send))
    parts = [parts[0]] + [along(parts[step], step) for step in (2, 3, 1)]
    loss, video_grad, text_grad = gradients(
        *parts, own, last, target, *mine, *theirs, video_hat, video_norm, text_embed
    )
    return video_embed, video_grad, text_grad, loss.reshape(())


def solution(mesh):
    split = Mesh(mesh.devices.reshape(2, 2, 2, 8, 4), ALL)
    return jax.shard_map(
        body,
        mesh=split,
        in_specs=(P(ALL, None, None), P(ALL), P(), P(), P(ALL, None), P(ALL)),
        out_specs=(P(ALL, None), P(ALL, None), P(ALL, None), P()),
        check_vma=False,
    )
```

```python
import jax
import jax.numpy as jnp
from jax import lax
from jax.experimental import pallas as pl
from jax.experimental.pallas import tpu as pltpu
from jax.sharding import Mesh, PartitionSpec as P

H = 25
HD = 128
D = 3200
E = 768
TOK = 16
CLIPS = 64
SOFT_CAP = 20.0
SCALE = 40.0
EPS = 1e-06
ALL = ("xh", "c", "xl", "z", "y")
ROW = ("xl", "z", "y")
PLANE = ("z", "y")
CHUNK = 32
TOKS = CHUNK * TOK
STEPS = CLIPS // CHUNK
PARTS = 4
WIDE = 7
SENT = WIDE * HD
TAIL = 4 * HD
TILE = 256
SET = CLIPS * 8
PLANE_ROWS = 256
SUMS = 2 * E + TILE + 128
PIECE = E // 2
VMEM = pl.BlockSpec(memory_space=pltpu.VMEM)
f32 = jnp.float32
bf16 = jnp.bfloat16
NT = (((1,), (1,)), ((), ()))
TN = (((0,), (0,)), ((), ()))


def dot(a, b, dims=(((1,), (0,)), ((), ()))):
    return lax.dot_general(a, b, dims, preferred_element_type=f32)


def iota(shape, dim):
    return lax.broadcasted_iota(jnp.int32, shape, dim)


def column_of(row):
    n = row.shape[1]
    eye = iota((n, n), 0) == iota((n, n), 1)
    return jnp.sum(jnp.where(eye, jnp.broadcast_to(row, (n, n)), 0.0), axis=1, keepdims=True)


def unit_rows(values):
    norms = jnp.sqrt(jnp.sum(values * values, axis=1, keepdims=True) + EPS)
    return values / norms, norms


def label_of(xh, xl, y):
    return (2 * xh + xl + 2 * y) % 4


def clip_kernel(
    video_hbm, token_hbm, pool_hbm, text_hbm, pair_hbm,
    num_ref, slot_ref, code_ref, hat_ref,
    video_ref, token_ref, pool_ref, text_ref, pair_ref, weight_scr, sems,
):
    small = ((pool_hbm, pool_ref), (video_hbm, video_ref), (text_hbm, text_ref), (pair_hbm, pair_ref))
    chunks = [pl.ds(i * TOKS, TOKS) for i in range(STEPS)]
    loads = [
        pltpu.make_async_copy(token_hbm.at[chunk], token_ref.at[chunk], sems.at[i])
        for i, chunk in enumerate(chunks)
    ]
    early = [
        pltpu.make_async_copy(src, dst, sems.at[STEPS + i]) for i, (src, dst) in enumerate(small)
    ]
    early[0].start()
    loads[0].start()
    for copy in early[1:] + loads[1:]:
        copy.start()
    weight_scr[...] = jnp.zeros_like(weight_scr)
    num_ref[...] = jnp.zeros_like(num_ref)
    mine = iota((CHUNK, TOKS), 1) // TOK == iota((CHUNK, TOKS), 0)
    ones = mine.astype(f32).astype(bf16)
    lane = iota((CHUNK, HD), 1)
    for copy in early[1:]:
        copy.wait()
    videos = video_ref[...].astype(f32)
    hat_ref[...], _ = unit_rows(text_ref[...].astype(f32))
    early[0].wait()
    pool = pool_ref[...]

    def put(step, j, value):
        at = j // WIDE * CLIPS + step * CHUNK
        num_ref[at : at + CHUNK, j % WIDE * HD : (j % WIDE + 1) * HD] = value.astype(bf16)

    def weigh(step):
        loads[step].wait()
        scores = dot(pool, token_ref[chunks[step], :], NT)
        weights = jnp.exp(SOFT_CAP * jnp.tanh(scores / SOFT_CAP))
        weight_scr[step, 0:H, :] = weights
        weight_scr[step, 32 : 32 + H, :] = weights

    def total(step):
        den = dot(ones, weight_scr[step].astype(bf16), NT)
        den_hi = den.astype(bf16).astype(f32)
        here = iota((CHUNK, CLIPS), 1) == iota((CHUNK, CLIPS), 0) + step * CHUNK
        video = jnp.where(here, jnp.broadcast_to(videos, (CHUNK, CLIPS)), 0.0)
        video = jnp.sum(video, axis=1, keepdims=True).astype(jnp.int32)
        local = jnp.where((lane < 96) & (lane % 8 == video % 8), 1.0, 0.0)
        tail = jnp.where(lane < 32, den_hi, jnp.where(lane < 64, den - den_hi, local))
        put(step, H, tail)
        for h in range(0, H, 2):
            pair = range(h, min(h + 2, H))
            lhs = jnp.concatenate(
                [
                    jnp.where(
                        mine, jnp.broadcast_to(weight_scr[step, k : k + 1, :], (CHUNK, TOKS)), 0.0
                    )
                    for k in pair
                ],
                axis=0,
            ).astype(bf16)
            part = dot(lhs, token_ref[chunks[step], h * HD : (h + len(pair)) * HD])
            for n, k in enumerate(pair):
                put(step, k, part[n * CHUNK : (n + 1) * CHUNK, n * HD : (n + 1) * HD])

    for step in range(STEPS):
        weigh(step)
        if step:
            total(step - 1)
    total(STEPS - 1)

    owner = (video_ref[...] // 8).astype(f32)
    before = (column_of(owner) == owner) & (iota((CLIPS, CLIPS), 0) < iota((CLIPS, CLIPS), 1))
    rank = jnp.sum(jnp.where(before, 1.0, 0.0), axis=0, keepdims=True)
    slot = owner * 2.0 + rank
    slot_ref[...] = jnp.concatenate([slot] * PARTS, axis=1)
    pair = pair_ref[...]
    code_ref[...] = jnp.concatenate(
        [
            jnp.zeros((1, 96), f32),
            (pair // 64).astype(f32),
            (pair % 64).astype(f32),
            jnp.zeros((1, 16), f32),
        ],
        axis=1,
    )


def pack_kernel(num_ref, slot_ref, code_ref, hat_ref, far_ref, out_ref):
    xh = lax.axis_index("xh")
    shape = (CLIPS * 8, PARTS * CLIPS)
    row, col = iota(shape, 0), iota(shape, 1)
    place = (row // PARTS == slot_ref[...].astype(jnp.int32)) & (row % PARTS == col // CLIPS)
    out = dot(jnp.where(place, 1.0, 0.0).astype(bf16), num_ref[...])
    last = iota((CLIPS * 8, HD), 0) % PARTS == PARTS - 1
    out_ref[:, 0:TAIL] = out[:, 0:TAIL].astype(bf16)
    out_ref[:, TAIL : TAIL + HD] = (
        out[:, TAIL : TAIL + HD] + jnp.where(last, code_ref[...], 0.0)
    ).astype(bf16)
    out_ref[:, TAIL + HD : SENT] = out[:, TAIL + HD : SENT].astype(bf16)
    near = hat_ref[...]
    far, _ = unit_rows(far_ref[...].astype(f32))
    low = xh == 0
    texts = jnp.concatenate([jnp.where(low, near, far), jnp.where(low, far, near)], axis=0)
    row, col = iota((CLIPS * 8, 16), 0), iota((CLIPS * 8, 16), 1)
    dest = row // 8
    label = label_of(xh, dest // 32, dest % 4)
    pick = row % 4 // 2 * 8 + 2 * label + row % 2 == col
    texts = dot(jnp.where(pick, 1.0, 0.0).astype(bf16), texts.astype(bf16))
    upper = iota((CLIPS * 8, PIECE), 0) % 8 < 4
    out_ref[:, SENT : SENT + PIECE] = jnp.where(
        upper, texts[:, 0:PIECE], texts[:, PIECE:E]
    ).astype(bf16)


def pack(*args):
    return pl.pallas_call(
        pack_kernel,
        in_specs=[VMEM] * 5,
        out_specs=VMEM,
        out_shape=jax.ShapeDtypeStruct((CLIPS * 8, SENT + PIECE), bf16),
        compiler_params=pltpu.CompilerParams(vmem_limit_bytes=16 << 20),
        cost_estimate=pl.CostEstimate(
            flops=2 * 512 * 256 * SENT, bytes_accessed=2 << 20, transcendentals=0
        ),
    )(*args)


def clip_sums(clip_tokens, clip_video, pool_vectors, text_embed, pair_text):
    args = (
        clip_video.reshape(1, CLIPS),
        clip_tokens.reshape(CLIPS * TOK, D),
        pool_vectors,
        text_embed,
        pair_text.reshape(1, 8),
    )
    return pl.pallas_call(
        clip_kernel,
        in_specs=[pl.BlockSpec(memory_space=pltpu.HBM)] * 5,
        out_specs=[VMEM] * 4,
        out_shape=[
            jax.ShapeDtypeStruct((PARTS * CLIPS, SENT), bf16),
            jax.ShapeDtypeStruct((1, PARTS * CLIPS), f32),
            jax.ShapeDtypeStruct((1, HD), f32),
            jax.ShapeDtypeStruct((8, E), f32),
        ],
        scratch_shapes=[pltpu.VMEM(x.shape, x.dtype) for x in args]
        + [
            pltpu.VMEM((STEPS, 128, TOKS), f32),
            pltpu.SemaphoreType.DMA((STEPS + 4,)),
        ],
        compiler_params=pltpu.CompilerParams(vmem_limit_bytes=16 << 20),
        cost_estimate=pl.CostEstimate(
            flops=2 * 1024 * D * 64, bytes_accessed=8 << 20, transcendentals=1 << 17
        ),
    )(*(pltpu.with_memory_space_constraint(x, pltpu.HBM) for x in args))


def embed_kernel(
    arrived_ref, proj_ref, emb_ref, hat_ref, norm_ref, send_ref
):
    rows = CLIPS * 8
    tails = arrived_ref[:, TAIL : TAIL + HD].astype(f32).reshape(CLIPS, 8, HD)
    upper = iota((CLIPS, 8, HD), 1) < 4
    hot = jnp.where(upper, tails[:, 3:4, :], tails[:, 7:8, :]).reshape(rows, HD)
    lane, row = iota((rows, HD), 1), iota((rows, HD), 0)
    hot = jnp.where(lane // 8 == 8 + row % PARTS, hot, 0.0)
    sums = dot(hot.astype(bf16), arrived_ref[:, 0:SENT], TN)

    def chunk(j):
        p, q = j // WIDE, j % WIDE
        return sums[64 + p * 8 : 72 + p * 8, q * HD : (q + 1) * HD]

    den = chunk(H)
    den = den[:, 0:32] + den[:, 32:64]
    pooled = jnp.concatenate([chunk(h) / den[:, h : h + 1] for h in range(H)], axis=1)
    hi = pooled.astype(bf16).astype(f32)
    mid = (pooled - hi).astype(bf16).astype(f32)
    low = pooled - hi - mid
    parts = dot(jnp.concatenate([hi, mid, low], axis=0).astype(bf16), proj_ref[...])
    emb = parts[0:8] + parts[8:16] + parts[16:24]
    emb_ref[...] = emb.astype(bf16)
    hat, norm = unit_rows(emb)
    hat_ref[...] = hat
    norm_ref[...] = norm
    hat_low = hat.astype(bf16)
    for k in range(32):
        send_ref[k] = hat_low


def embed(arrived, out_proj):
    return pl.pallas_call(
        embed_kernel,
        in_specs=[VMEM, VMEM],
        out_specs=[VMEM] * 4,
        out_shape=[
            jax.ShapeDtypeStruct((8, E), bf16),
            pltpu.HBM((8, E), f32),
            jax.ShapeDtypeStruct((8, 1), f32),
            jax.ShapeDtypeStruct((32, 8, E), bf16),
        ],
        compiler_params=pltpu.CompilerParams(vmem_limit_bytes=16 << 20),
        cost_estimate=pl.CostEstimate(
            flops=2 * 24 * D * E, bytes_accessed=6 << 20, transcendentals=0
        ),
    )(arrived, out_proj)


def text_kernel(arrived_ref, text_ref):
    halves = arrived_ref[:, SENT : SENT + PIECE]
    row, col = iota((TILE, CLIPS * 8), 0), iota((TILE, CLIPS * 8), 1)
    for part in range(2):
        pick = row // 4 * 8 + part * 4 + row % 4 == col
        texts = dot(jnp.where(pick, 1.0, 0.0).astype(bf16), halves)
        text_ref[:, part * PIECE : (part + 1) * PIECE] = texts.astype(bf16)


def target_kernel(arrived_ref, target_ref):
    rows = CLIPS * 8
    code = arrived_ref[:, TAIL : TAIL + HD].astype(f32).reshape(CLIPS, 8, HD)[:, 3:4, :]
    code = jnp.broadcast_to(code, (CLIPS, 8, HD)).reshape(rows, HD)
    lane, own = iota((rows, HD), 1), iota((rows, HD), 0) % 8
    code = jnp.where(lane - 96 == own, 64.0 * code, jnp.where(lane - 104 == own, code, 0.0))
    target_ref[...] = jnp.sum(code, axis=1, keepdims=True)


def text_piece(arrived):
    return pl.pallas_call(
        text_kernel,
        in_specs=[VMEM],
        out_specs=VMEM,
        out_shape=jax.ShapeDtypeStruct((TILE, E), bf16),
        compiler_params=pltpu.CompilerParams(vmem_limit_bytes=16 << 20),
        cost_estimate=pl.CostEstimate(
            flops=4 * 256 * 512 * PIECE, bytes_accessed=1 << 20, transcendentals=0
        ),
    )(arrived)


def targets(arrived):
    return pl.pallas_call(
        target_kernel,
        in_specs=[VMEM],
        out_specs=VMEM,
        out_shape=jax.ShapeDtypeStruct((SET, 1), f32),
        compiler_params=pltpu.CompilerParams(vmem_limit_bytes=16 << 20),
        cost_estimate=pl.CostEstimate(flops=1 << 18, bytes_accessed=1 << 19, transcendentals=0),
    )(arrived)


def position():
    xh, c, xl, z, y = (lax.axis_index(a) for a in ALL)
    return xh, c, xl, z * 4 + y


def other(a, flip):
    return a + flip - 2 * flip * a


def row_of(xh, c, k):
    return other(xh, k // 2) * 2 + other(c, k % 2)


def tile_of(xh, c, xl, spot, k):
    y = spot % 4
    label = (
        label_of(xh, xl, y),
        label_of(xh, 1 - xl, y),
        label_of(1 - xh, 1 - xl, y),
        label_of(xh, xl, y + 1),
    )[k % 4]
    return other(c, k // 4) * 4 + label


def texts_of(tile, j):
    row = j % 4 // 2 * 2 + tile // 4
    return ((row * 64 + j // 4) * 8 + tile % 4 * 2 + j % 2).astype(f32)


def score(videos, target, pieces, tiles, own_ref, tile_scr, cols_ref, sums, positive, base):
    for n, (ref, tile) in enumerate(zip(pieces, tiles)):
        logits = SCALE * dot(videos, ref[...], NT)
        ex = jnp.exp(logits)
        tile_scr[...] = ex
        cols_ref[pl.ds(tile, 1), :] = jnp.sum(ex, axis=0, keepdims=True)
        sums += ex[:, 0:128] + ex[:, 128:TILE]
        hit = target == texts_of(tile, iota((1, TILE), 1))
        positive += jnp.sum(jnp.where(hit, logits, 0.0), axis=0, keepdims=True)
        own_ref[:, n * TILE : (n + 1) * TILE] = tile_scr[pl.ds(base, 8), :]
    return sums, positive


def plane_rows(target_ref, xl):
    return target_ref[pl.ds(pl.multiple_of(xl * PLANE_ROWS, PLANE_ROWS), PLANE_ROWS), :]


def near_texts(slot, flip):
    xh, c, _, spot = position()
    group = sum(
        jnp.where(slot // 8 == n, row_of(xh, c, n // 2 * 2 + flip) * 2 + n % 2, 0)
        for n in range(4)
    )
    return ((group * 32 + spot) * 8 + slot % 8).astype(f32)


def near_exps(videos, pieces, tiles, flip):
    spot = position()[3]
    blocks = [
        ref[pl.ds(pl.multiple_of(half * 128 + spot // 4 * 16, 16), 16), :]
        for ref in pieces
        for half in range(2)
    ]
    col = iota((1, 128), 1)
    tile = sum(jnp.where(col // 32 == k, tiles[k], 0) for k in range(4))
    held = texts_of(tile, col % 32 // 16 * 128 + spot // 4 * 16 + col % 16)
    pick = near_texts(iota((32, 1), 0), flip) == held
    near = dot(jnp.where(pick, 1.0, 0.0).astype(bf16), jnp.concatenate(blocks, axis=0))
    return jnp.exp(SCALE * dot(videos, near.astype(bf16), NT))


def near_sums(near, rowsum, target, videos, flip, cols, total, out_ref):
    first = near / rowsum - jnp.where(target == near_texts(iota((1, 32), 1), flip), 2.0, 0.0)
    first_hi = first.astype(bf16).astype(f32)
    near_hi = near.astype(bf16).astype(f32)
    terms = jnp.concatenate([first_hi, first - first_hi, near_hi, near - near_hi], axis=1)
    sums = dot(terms.astype(bf16), videos, TN)
    first, second = sums[0:32] + sums[32:64], sums[64:96] + sums[96:128]
    xl = position()[2]
    for n in range(4):
        step = n // 2 * 2 + other(xl, n % 2)
        out_ref[step, :, 0:E] = first[n * 8 : (n + 1) * 8]
        out_ref[step, :, E : 2 * E] = second[n * 8 : (n + 1) * 8]
        out_ref[step, :, 2 * E : 2 * E + TILE] = cols
        out_ref[step, :, 2 * E + TILE :] = total


def first_kernel(
    video_ref, target_ref, set0_ref, set1_ref, set2_ref, set3_ref,
    own_ref, cols_ref, sums_ref, positive_ref, near_ref, tile_scr,
):
    xh, c, xl, spot = position()
    cols_ref[...] = jnp.zeros_like(cols_ref)
    videos = video_ref[...]
    pieces = (set0_ref, set1_ref, set2_ref, set3_ref)
    tiles = [tile_of(xh, c, xl, spot, k) for k in range(4)]
    sums_ref[...], positive_ref[...] = score(
        videos, plane_rows(target_ref, xl), pieces, tiles, own_ref, tile_scr, cols_ref,
        jnp.zeros((PLANE_ROWS, 128), f32), jnp.zeros((1, TILE), f32), pl.multiple_of(spot * 8, 8),
    )
    near_ref[...] = near_exps(videos, pieces, tiles, 0)


def second_kernel(
    video_ref, target_ref, set4_ref, set5_ref, set6_ref, set7_ref, cols_ref, sums_ref, positive_ref,
    send_ref, own_ref, rowsum_ref, cols_out, total_ref, tile_scr,
):
    xh, c, xl, spot = position()
    target = plane_rows(target_ref, xl)
    videos = video_ref[...]
    pieces = (set4_ref, set5_ref, set6_ref, set7_ref)
    tiles = [tile_of(xh, c, xl, spot, k) for k in range(4, 8)]
    cols_out[...] = cols_ref[...]
    sums, positive = score(
        videos, target, pieces, tiles, own_ref, tile_scr, cols_out,
        sums_ref[...], positive_ref[...], pl.multiple_of(spot * 8, 8),
    )
    near = near_exps(videos, pieces, tiles, 1)
    rowsum = jnp.sum(sums, axis=1, keepdims=True)
    rowsum_ref[...] = rowsum
    total = jnp.sum(jnp.log(rowsum), axis=0, keepdims=True) - 2.0 * jnp.sum(
        positive, axis=1, keepdims=True
    )
    total_ref[...] = jnp.broadcast_to(total, (8, 128))
    near_sums(near, rowsum, target, videos, 1, cols_out[...], total_ref[...], send_ref)


def keep_kernel(video_ref, target_ref, near_ref, rowsum_ref, cols_ref, total_ref, keep_ref):
    target = plane_rows(target_ref, position()[2])
    near_sums(
        near_ref[...], rowsum_ref[...], target, video_ref[...], 0, cols_ref[...], total_ref[...],
        keep_ref,
    )


def keep_sums(*args):
    return pl.pallas_call(
        keep_kernel,
        in_specs=[VMEM] * 6,
        out_specs=VMEM,
        out_shape=jax.ShapeDtypeStruct((4, 8, SUMS), f32),
        compiler_params=pltpu.CompilerParams(vmem_limit_bytes=16 << 20),
        cost_estimate=pl.CostEstimate(
            flops=2 * PLANE_ROWS * 128 * E, bytes_accessed=1 << 20, transcendentals=0
        ),
    )(*args)


def first_logits(*args):
    return pl.pallas_call(
        first_kernel,
        in_specs=[VMEM] * 6,
        out_specs=[VMEM] * 5,
        out_shape=[
            jax.ShapeDtypeStruct((8, 2 * SET), f32),
            jax.ShapeDtypeStruct((8, TILE), f32),
            jax.ShapeDtypeStruct((PLANE_ROWS, 128), f32),
            jax.ShapeDtypeStruct((1, TILE), f32),
            jax.ShapeDtypeStruct((PLANE_ROWS, 32), f32),
        ],
        scratch_shapes=[pltpu.VMEM((PLANE_ROWS, TILE), f32)],
        compiler_params=pltpu.CompilerParams(vmem_limit_bytes=16 << 20),
        cost_estimate=pl.CostEstimate(
            flops=2 * PLANE_ROWS * 1024 * E, bytes_accessed=2 << 20, transcendentals=1 << 18
        ),
    )(*args)


def second_logits(*args):
    return pl.pallas_call(
        second_kernel,
        in_specs=[VMEM] * 9,
        out_specs=[VMEM] * 5,
        out_shape=[
            jax.ShapeDtypeStruct((4, 8, SUMS), f32),
            jax.ShapeDtypeStruct((8, 2 * SET), f32),
            jax.ShapeDtypeStruct((PLANE_ROWS, 1), f32),
            jax.ShapeDtypeStruct((8, TILE), f32),
            jax.ShapeDtypeStruct((8, 128), f32),
        ],
        scratch_shapes=[pltpu.VMEM((PLANE_ROWS, TILE), f32)],
        compiler_params=pltpu.CompilerParams(vmem_limit_bytes=16 << 20),
        cost_estimate=pl.CostEstimate(
            flops=2 * PLANE_ROWS * 1536 * E, bytes_accessed=4 << 20, transcendentals=1 << 18
        ),
    )(*args)


def add_kernel(keep_ref, got_ref, *out_refs):
    for k, out_ref in enumerate(out_refs):
        out_ref[...] = keep_ref[k] + got_ref[k]


def add_parts(keep, got):
    return pl.pallas_call(
        add_kernel,
        in_specs=[VMEM] * 2,
        out_specs=[VMEM] * 4,
        out_shape=[jax.ShapeDtypeStruct((8, SUMS), f32)] * 4,
        compiler_params=pltpu.CompilerParams(vmem_limit_bytes=16 << 20),
        cost_estimate=pl.CostEstimate(flops=1 << 16, bytes_accessed=1 << 19, transcendentals=0),
    )(keep, got)


def grad_kernel(
    part0_ref, part1_ref, part2_ref, part3_ref, own_ref, last_ref, target_ref,
    set0_ref, set1_ref, set2_ref, set3_ref, set4_ref, set5_ref, set6_ref, set7_ref,
    video_hat_ref, video_norm_ref, text_ref, loss_ref, video_grad_ref, text_grad_ref, col_scr,
):
    xh, c, xl, spot = position()
    got = (part0_ref[...] + part1_ref[...]) + (part2_ref[...] + part3_ref[...])
    cols = got[:, 2 * E : 2 * E + TILE]
    col_scr[...] = cols
    logs = jnp.sum(jnp.sum(jnp.log(cols), axis=0, keepdims=True), axis=1, keepdims=True)
    loss_ref[...] = (logs + got[0:1, 2 * E + TILE : 2 * E + TILE + 1]) / 4096.0

    def project(direction, hat, norm):
        return (direction - jnp.sum(direction * hat, axis=1, keepdims=True) * hat) / norm

    at = (xl * 32 + spot) * 4 + xh * 2
    lane = iota((4, TILE), 1) - at
    mine = jnp.where(c == 0, cols[0:4], cols[4:8])
    pair = [jnp.sum(jnp.where(lane == n, mine, 0.0), axis=1, keepdims=True) for n in range(2)]
    row = iota((8, 1), 0)
    mine = sum(
        jnp.where(row == n, pair[n % 2][n // 2 : n // 2 + 1], 0.0) for n in range(8)
    )
    text_dir = SCALE * (got[:, 0:E] + got[:, E : 2 * E] / mine)
    text_grad_ref[...] = project(text_dir, *unit_rows(text_ref[...].astype(f32)))

    rows = jnp.concatenate([own_ref[...], last_ref[...]], axis=1)
    rowsum = jnp.sum(rows, axis=1, keepdims=True)
    target = target_ref[pl.ds(pl.multiple_of((xl * 32 + spot) * 8, 8), 8), :]
    direction = jnp.zeros((8, E), f32)
    pieces = (set0_ref, set1_ref, set2_ref, set3_ref, set4_ref, set5_ref, set6_ref, set7_ref)
    for k, ref in enumerate(pieces):
        tile = tile_of(xh, c, xl, spot, k)
        ex = rows[:, k * TILE : (k + 1) * TILE]
        hot = jnp.where(target == texts_of(tile, iota((1, TILE), 1)), 2.0, 0.0)
        probe = ex / rowsum + ex / col_scr[pl.ds(tile, 1), :] - hot
        direction += dot(probe.astype(bf16), ref[...])
    video_grad_ref[...] = project(SCALE * direction, video_hat_ref[...], video_norm_ref[...])


def gradients(*args):
    return pl.pallas_call(
        grad_kernel,
        in_specs=[VMEM] * 18,
        out_specs=[VMEM] * 3,
        out_shape=[
            jax.ShapeDtypeStruct((1, 1), f32),
            jax.ShapeDtypeStruct((8, E), f32),
            jax.ShapeDtypeStruct((8, E), f32),
        ],
        scratch_shapes=[pltpu.VMEM((8, TILE), f32)],
        compiler_params=pltpu.CompilerParams(vmem_limit_bytes=12 << 20),
        cost_estimate=pl.CostEstimate(
            flops=2 * 8 * 2048 * E, bytes_accessed=5 << 20, transcendentals=2048
        ),
    )(*args)


def exchange(x, axes):
    return lax.all_to_all(x, axes, 0, 0, tiled=True)


def swap(x):
    return lax.ppermute(x, "c", [(0, 1), (1, 0)])


def along(x, step):
    return lax.ppermute(x, ("xh", "xl"), [(k, k ^ step) for k in range(4)])


def turn_y(x):
    return lax.ppermute(x, "y", [(k, k ^ 1) for k in range(4)])


def body(clip_tokens, clip_video, pool_vectors, out_proj, text_embed, pair_text):
    far_text = along(text_embed, 2)
    *sums, text_hat = clip_sums(
        clip_tokens, clip_video, pool_vectors, text_embed, pair_text
    )
    outgoing = pack(*sums, text_hat, far_text)
    arrived = exchange(outgoing.reshape(CLIPS, 8, SENT + PIECE), ROW)
    arrived = arrived.reshape(CLIPS * 8, SENT + PIECE)
    video_embed, video_hat, video_norm, send = embed(arrived, out_proj)
    texts, target = text_piece(arrived), targets(arrived)
    moved = [turn_y(texts), along(texts, 3), along(texts, 1)]
    videos, moved[0] = lax.optimization_barrier((exchange(send, PLANE), moved[0]))
    videos = videos.reshape(PLANE_ROWS, E)
    mine = (texts, moved[2], moved[1], moved[0])
    theirs = tuple(swap(x) for x in mine)
    own, cols, sums, positive, near = first_logits(videos, target, *mine)
    send, last, rowsum, cols, total = second_logits(videos, target, *theirs, cols, sums, positive)
    keep = keep_sums(videos, target, near, rowsum, cols, total)
    parts = add_parts(keep, swap(send))
    parts = [parts[0]] + [along(parts[step], step) for step in (2, 3, 1)]
    loss, video_grad, text_grad = gradients(
        *parts, own, last, target, *mine, *theirs, video_hat, video_norm, text_embed
    )
    return video_embed, video_grad, text_grad, loss.reshape(())


def solution(mesh):
    split = Mesh(mesh.devices.reshape(2, 2, 2, 8, 4), ALL)
    return jax.shard_map(
        body,
        mesh=split,
        in_specs=(P(ALL, None, None), P(ALL), P(), P(), P(ALL, None), P(ALL)),
        out_specs=(P(ALL, None), P(ALL, None), P(ALL, None), P()),
        check_vma=False,
    )
```
